32 devices in a mesh: cells: 8 (over z, x), spots: 4 (over y, core).
Axes of the slice: x: 2, y: 2, z: 4, core: 2. Of those that a mesh axis runs over, the one named last changes fastest.
Arguments:
- logits: float32 [12288, 9216], P('cells', 'spots'), may hold values from -8 to 8
- expression: bfloat16 [12288, 2048], P('cells'), may hold values from 0.049804688 to 4
- target: bfloat16 [2048, 9216], P(None, 'spots'), may hold values from 0.049804688 to 4
- density: float32 [9216], P('spots'), may hold values from 0.2 to 5
- assignment: int32 [9216], P('spots'), may hold values from 0 to 1, as said below
- labels: int32 [12288], P('cells'), may hold values from 0 to 127
- counts: int32 [8], P('cells'), may hold values from 512 to 1536, as said below
Outputs:
- predicted: bfloat16 [2048, 9216], P('cells', 'spots')
- grad_logits: float32 [12288, 9216], P('cells', 'spots')
- grad_expression: float32 [12288, 2048], P('cells', 'spots')
- losses: float32 [2, 3], replicated
- type_share: float32 [128, 9216], P(None, 'spots')
The draws below stay inside these ranges and needn't reach their ends.
Inputs may be any that keep to these rules, and one draw needn't show every extreme that they name: assignment[s] is 1 for a spot of the Visium slide and 0 for a bin of the second slide; both slides have spots. counts[g] is the number of live rows of group g, which are its first ones; some group has all 1536 rows live.
All inputs are finite; a program needn't handle non-finite values.
Results may differ from the reference program's by a relative error of at most 0.0049.
Values may be sent and summed in bfloat16 or wider, within the bound.
No kernel may reach another device: no remote copies, remote signals or barrier semaphores. Data moves between devices by JAX's collectives and lax.ppermute only.
A program may use at most 192 MiB of HBM per device.

```python
import math
import jax
import jax.numpy as jnp
from jax import lax

CAP = 1536
GENES = 2048
NTYPE = 128
GROUPS = 8
CELLS = 12288
SPOTS = 9216


def draw_assignment(key, part):
    key = jax.random.fold_in(key, 11)
    key_mask, key_one, key_zero = jax.random.split(key, 3)
    quarter = jax.random.randint(key_mask, (SPOTS,), 0, 4)
    marked = jnp.where(quarter == 0, 1, 0).astype(jnp.int32)
    visium_at = jax.random.randint(key_one, (), 0, SPOTS)
    second_at = (visium_at + 1 + jax.random.randint(key_zero, (), 0, SPOTS - 1)) % SPOTS
    return marked.at[visium_at].set(1).at[second_at].set(0)


def draw_counts(key, part):
    key = jax.random.fold_in(key, 23)
    key_rows, key_full = jax.random.split(key)
    counted = jax.random.randint(key_rows, (GROUPS,), CAP // 3, CAP + 1)
    full_at = jax.random.randint(key_full, (), 0, GROUPS)
    return counted.at[full_at].set(CAP).astype(jnp.int32)


def plant(drawn, stream_key, smallest, top_value):
    extent = drawn.shape
    place = [jax.random.randint(jax.random.fold_in(stream_key, axis), (), 0, extent[axis]) for axis in range(len(extent))]
    drawn = drawn.at[tuple(place)].set(smallest)
    longest = extent.index(max(extent))
    place[longest] = (place[longest] + 1) % extent[longest]
    return drawn.at[tuple(place)].set(top_value)


def steps_of(key, shape, pieces, low, high):
    level, own = 1.0, jax.random.fold_in(key, 6)
    for axis_at, parts in pieces:
        steps = jnp.exp(jax.random.uniform(jax.random.fold_in(own, axis_at), (parts,), jnp.float32, low / len(pieces), high / len(pieces)))
        level = level * jnp.repeat(steps, shape[axis_at] // parts).reshape([-1 if axis == axis_at else 1 for axis in range(len(shape))])
    return level


def scatter_about(stream_key, extent, scale, bound, shards=(), kind=jnp.bfloat16):
    loudness = steps_of(stream_key, extent, shards, -0.22, 0.18) if shards else 1.0
    array = jax.random.normal(stream_key, extent, jnp.float32) * scale * loudness
    return jnp.minimum(jnp.maximum(array, -bound), bound).astype(kind)


def setup_inputs(seed: int = 0) -> dict:
    keys = jax.random.split(jax.random.key(seed), 8)
    logits = scatter_about(keys[0], (CELLS, SPOTS), 2.0, 8.0, ((0, 8), (1, 4)), jnp.float32)
    expression = jnp.clip(jnp.exp(math.log(4.0) - 4.3859405 * jax.random.uniform(keys[1], (CELLS, GENES), jnp.float32) ** steps_of(keys[1], (CELLS, GENES), ((0, 8),), -0.2, 0.2)), 0.049804688, 4.0).astype(jnp.bfloat16)
    target = jnp.clip(jnp.exp(math.log(4.0) - 4.3859405 * jax.random.uniform(keys[2], (GENES, SPOTS), jnp.float32) ** steps_of(keys[2], (GENES, SPOTS), ((1, 4),), -0.2, 0.2)), 0.049804688, 4.0).astype(jnp.bfloat16)
    density = jnp.clip(jnp.exp(math.log(5.0) - 3.218876 * jax.random.uniform(keys[3], (SPOTS,), jnp.float32) ** steps_of(keys[3], (SPOTS,), ((0, 4),), -0.2, 0.2)), 0.2, 5.0)
    assignment = draw_assignment(jax.random.fold_in(keys[7], 71), 0)
    labels = plant(jax.random.randint(keys[5], (CELLS,), 0, NTYPE), jax.random.fold_in(keys[5], 1), 0, NTYPE - 1).astype(jnp.int32)
    counts = draw_counts(jax.random.fold_in(keys[7], 71), 0)
    return {"logits": logits, "expression": expression, "target": target, "density": density, "assignment": assignment, "labels": labels, "counts": counts}


@jax.custom_vjp
def low(v):
    return lax.optimization_barrier(v.astype(jnp.bfloat16)).astype(jnp.float32)

@jax.custom_vjp
def low_back(v):
    return v

def low_keep(v):
    return (low(v), None)

def low_pass(kept, grad):
    return (grad,)

def back_keep(v):
    return (v, None)

def back_low(kept, grad):
    return (low(grad),)
low.defvjp(low_keep, low_pass)
low_back.defvjp(back_keep, back_low)

def score(predicted, dens_pred, target, assignment, density):
    highest = lax.Precision.HIGHEST
    sides = jnp.stack([assignment == 0, assignment == 1]).astype(jnp.float32)
    gene_dot = jnp.dot(predicted * target, sides.T, precision=highest)
    gene_pred = jnp.dot(predicted * predicted, sides.T, precision=highest)
    gene_target = jnp.dot(target * target, sides.T, precision=highest)
    gene_cosine = gene_dot * lax.rsqrt(gene_pred) * lax.rsqrt(gene_target)
    spot_dot = lax.optimization_barrier(jnp.sum(predicted * target, axis=0))
    spot_pred = lax.optimization_barrier(jnp.sum(predicted * predicted, axis=0))
    spot_target = lax.optimization_barrier(jnp.sum(target * target, axis=0))
    spot_cosine = spot_dot * lax.rsqrt(spot_pred) * lax.rsqrt(spot_target)
    columns = jnp.stack([jnp.ones_like(density), density, density * jnp.log(density), density * jnp.log(dens_pred), dens_pred, spot_cosine])
    slide_sums = jnp.dot(sides, columns.T, precision=highest)
    spot_count = slide_sums[:, 0]
    dens_mass = slide_sums[:, 1]
    dens_log = slide_sums[:, 2]
    cross_log = slide_sums[:, 3]
    pred_mass = slide_sums[:, 4]
    cosine_sum = slide_sums[:, 5]
    gene_mean = lax.optimization_barrier(jnp.sum(gene_cosine, axis=0)) / GENES
    spot_mean = cosine_sum / spot_count
    divergence = (dens_log - cross_log) / dens_mass - jnp.log(dens_mass) + jnp.log(pred_mass)
    table = jnp.stack([gene_mean, spot_mean, divergence], axis=1)
    total = jnp.sum(divergence - gene_mean - spot_mean) * float(CELLS * SPOTS)
    return (table, total)

def objective(logits, expression, target, assignment, density, live, one_hot):
    row_peak = lax.optimization_barrier(jnp.max(logits, axis=1, keepdims=True))
    raised = jnp.exp(logits - row_peak)
    probs = jnp.where(live, raised / lax.optimization_barrier(jnp.sum(raised, axis=1, keepdims=True)), 0.0)
    probs_low = low(probs)
    predicted = low_back(jnp.dot(expression.T, probs_low, precision=lax.Precision.HIGHEST))
    type_share = jnp.dot(one_hot.T, probs_low, precision=lax.Precision.HIGHEST) * NTYPE
    dens_pred = lax.optimization_barrier(jnp.sum(probs, axis=0)) / float(CELLS)
    table, total = score(predicted, dens_pred, target, assignment, density)
    return (total, (predicted, type_share, table))

def reference(logits, expression, target, density, assignment, labels, counts):
    row_index = jnp.arange(CELLS, dtype=jnp.int32)
    group_index = (row_index // CAP).astype(jnp.int32)
    live = (row_index % CAP < counts[group_index])[:, None]
    target_full = target.astype(jnp.float32)
    one_hot = (labels[:, None] == jnp.arange(NTYPE, dtype=jnp.int32)[None, :]).astype(jnp.float32)

    def wrapped(logit_values, expression_values):
        return objective(logit_values, expression_values, target_full, assignment, density, live, one_hot)
    total, pullback, extras = jax.vjp(wrapped, logits, expression.astype(jnp.float32), has_aux=True)
    grad_logits, grad_expression = pullback(jnp.ones((), jnp.float32))
    predicted, type_share, table = extras
    return (predicted.astype(jnp.bfloat16), grad_logits, grad_expression, table, type_share)
```

```python
import functools
import math

import jax
import jax.numpy as jnp
import numpy as np
from jax import lax
from jax.experimental import pallas as pl
from jax.experimental.pallas import tpu as pltpu
from jax.sharding import PartitionSpec as P

GENES = 2048
NTYPE = 128
LANES = 128
BF = jnp.bfloat16
F32 = jnp.float32
highest = lax.Precision.HIGHEST


def over_rows(left_side, right_side):
    return lax.dot_general(
        left_side, right_side, (((0,), (0,)), ((), ())), preferred_element_type=F32
    )


def over_columns(left_side, right_side):
    return lax.dot_general(
        left_side, right_side, (((1,), (1,)), ((), ())), preferred_element_type=F32
    )


def general(logits, expression, target, density, assignment, labels, counts):
    row_count = logits.shape[0]
    spot_width = logits.shape[1]
    cell_devices = lax.axis_size("cells")
    slot_total = float(row_count * cell_devices)
    scale = float(row_count * cell_devices * spot_width * lax.axis_size("spots"))
    live = (jnp.arange(row_count, dtype=jnp.int32) < counts[0])[:, None]
    raised = jnp.exp(logits)
    row_mass = lax.psum(jnp.sum(raised, axis=1), "spots")
    probs = jnp.where(live, raised / row_mass[:, None], 0.0)
    probs_low = probs.astype(BF)
    one_hot = (labels[:, None] == jnp.arange(NTYPE, dtype=jnp.int32)[None, :]).astype(BF)
    type_total, dens_total = lax.psum((over_rows(one_hot, probs_low), jnp.sum(probs, axis=0)), "cells")
    gene_rows = GENES // cell_devices
    predicted = lax.psum_scatter(
        over_rows(expression, probs_low), "cells", scatter_dimension=0, tiled=True
    )
    target_full = lax.dynamic_slice_in_dim(
        target, lax.axis_index("cells") * gene_rows, gene_rows, 0
    ).astype(F32)
    spot_dot, spot_pred, spot_target = lax.psum(
        (
            jnp.sum(predicted * target_full, axis=0),
            jnp.sum(predicted * predicted, axis=0),
            jnp.sum(target_full * target_full, axis=0),
        ),
        "cells",
    )
    dens_pred = dens_total / slot_total
    sides = jnp.stack([assignment == 0, assignment == 1]).astype(F32)
    inv_spot_pred = lax.rsqrt(spot_pred)
    inv_spot_target = lax.rsqrt(spot_target)
    spot_cosine = spot_dot * inv_spot_pred * inv_spot_target
    columns = jnp.stack(
        [
            jnp.ones_like(density),
            density,
            density * jnp.log(density),
            density * jnp.log(dens_pred),
            dens_pred,
            spot_cosine,
        ]
    )
    slide_part = jnp.dot(sides, columns.T, precision=highest)
    gene_part = jnp.stack(
        [
            jnp.dot(predicted * target_full, sides.T, precision=highest),
            jnp.dot(predicted * predicted, sides.T, precision=highest),
            jnp.dot(target_full * target_full, sides.T, precision=highest),
        ]
    )
    slide_sums, gene_sums = lax.psum((slide_part, gene_part), "spots")
    spot_count, dens_mass, dens_log, cross_log, pred_mass, cosine_sum = [
        slide_sums[:, at] for at in range(6)
    ]
    inv_gene_pred = lax.rsqrt(gene_sums[1])
    inv_gene_target = lax.rsqrt(gene_sums[2])
    gene_cosine = gene_sums[0] * inv_gene_pred * inv_gene_target
    gene_along_target = jnp.dot(inv_gene_pred * inv_gene_target, sides, precision=highest)
    gene_along_pred = jnp.dot(gene_cosine * inv_gene_pred * inv_gene_pred, sides, precision=highest)
    spot_weight = 1.0 / jnp.dot(spot_count, sides, precision=highest)
    spot_along_target = inv_spot_pred * inv_spot_target * spot_weight
    spot_along_pred = spot_cosine * inv_spot_pred * inv_spot_pred * spot_weight
    grad_dens = scale * (
        jnp.dot(1.0 / pred_mass, sides, precision=highest)
        - density / (jnp.dot(dens_mass, sides, precision=highest) * dens_pred)
    )
    grad_pred = scale * (
        -(target_full * gene_along_target - predicted * gene_along_pred) / GENES
        - (target_full * spot_along_target[None, :] - predicted * spot_along_pred[None, :])
    )
    grad_low = lax.all_gather(grad_pred.astype(BF), "cells", axis=0, tiled=True)
    grad_probs = jnp.dot(expression, grad_low, preferred_element_type=F32)
    grad_expr_part = over_columns(probs_low, grad_low)
    gene_loss = lax.psum(jnp.sum(gene_cosine, axis=0), "cells")
    grad_probs = grad_probs + (grad_dens / slot_total)[None, :]
    row_total = lax.psum(jnp.sum(probs * grad_probs, axis=1), "spots")
    grad_logits = probs * (grad_probs - row_total[:, None])
    grad_expression = lax.psum_scatter(grad_expr_part, "spots", scatter_dimension=1, tiled=True)
    divergence = (dens_log - cross_log) / dens_mass - jnp.log(dens_mass) + jnp.log(pred_mass)
    table = jnp.stack([gene_loss / GENES, cosine_sum / spot_count, divergence], axis=1)
    return (predicted.astype(BF), grad_logits, grad_expression, table, type_total * NTYPE)


VMEM = pltpu.MemorySpace.VMEM
HBM = pltpu.MemorySpace.HBM
IN_VMEM = pl.BlockSpec(memory_space=VMEM)
IN_SMEM = pl.BlockSpec(memory_space=pltpu.MemorySpace.SMEM)
IN_PLACE = pl.BlockSpec(memory_space=pl.ANY)
CHUNK = 2 * LANES
MIB = 1024 * 1024
GROUP = GENES // 8
KINDS = NTYPE // 8

FRONT = 144
ROWS = GROUP + KINDS
BACK = ROWS - FRONT


def line_at(numbers_ref):
    return numbers_ref[0] // 2


def order_of(line, turn):
    return (line, 1 + line % 2, (line + 2) % 4, 3 - 3 * (line % 2))[turn]


def block_at(numbers_ref, place):
    turn, other = place
    rung = numbers_ref[0] % 2
    return 2 * order_of(line_at(numbers_ref), turn) + (1 - rung if other else rung)


def call(kernel, name, inputs, outputs, scratch=(), aliases=None, limit=8):
    return pl.pallas_call(
        kernel,
        in_specs=[spec for _, spec in inputs],
        out_specs=[spec for _, spec in outputs],
        out_shape=[shape for shape, _ in outputs],
        scratch_shapes=list(scratch),
        input_output_aliases=aliases or {},
        compiler_params=pltpu.CompilerParams(vmem_limit_bytes=limit * MIB),
        cost_estimate=pl.CostEstimate(flops=1024, bytes_accessed=1024, transcendentals=0),
        name=name,
    )(*[array for array, _ in inputs])


def plain(*shape, dtype=F32):
    return jax.ShapeDtypeStruct(shape, dtype)


def pinned(array, space):
    return pltpu.with_memory_space_constraint(array, space)


def to_row(column):
    return jnp.broadcast_to(column, (LANES, LANES)).T[:1]


def to_column(row):
    return jnp.broadcast_to(row, (LANES, LANES)).T[:, :1]


def line_of(at):
    return pl.ds(at * LANES, LANES)


def columns_of(at):
    return pl.ds(pl.multiple_of(at * GROUP, GROUP), GROUP)


def packed_row(values):
    lane = lax.broadcasted_iota(jnp.int32, (1, LANES), 1)
    row = jnp.zeros((1, LANES), F32)
    for at, value in enumerate(values):
        row = jnp.where(lane == at, value, row)
    return row


def row_sum(row):
    return jnp.sum(row, axis=1, keepdims=True)


def mass_kernel(logits_ref, raised_ref, mass_ref, sems):
    lines = mass_ref.shape[0]
    copies = [
        pltpu.make_async_copy(logits_ref.at[line_of(at)], raised_ref.at[line_of(at)], sems.at[at])
        for at in range(lines)
    ]
    for copy in copies:
        copy.start()
    for at, copy in enumerate(copies):
        copy.wait()
        raised = jnp.exp(raised_ref[line_of(at), :])
        raised_ref[line_of(at), :] = raised
        mass_ref[pl.ds(at, 1), :] = to_row(jnp.sum(raised, axis=1, keepdims=True))


def mass_of(logits):
    rows, width = logits.shape
    lines = rows // LANES
    return call(
        mass_kernel,
        "mass",
        [(pinned(logits, HBM), IN_PLACE)],
        [(VMEM((rows, width), F32), IN_VMEM), (plain(lines, LANES), IN_VMEM)],
        [pltpu.SemaphoreType.DMA((lines,))],
    )


def left_kernel(places, numbers_ref, expr_ref, labels_ref, left_ref, held, sems):
    _, _, cells = left_ref.shape

    def copy(n):
        return pltpu.make_async_copy(
            expr_ref.at[:, columns_of(block_at(numbers_ref, places[n]))], held.at[n % 2], sems.at[n % 2]
        )

    copy(0).start()
    for n, place in enumerate(places):
        if n + 1 < len(places):
            copy(n + 1).start()
        kind = lax.broadcasted_iota(jnp.int32, (KINDS, cells), 0) + block_at(numbers_ref, place) * KINDS
        left_ref[n, GROUP:, :] = jnp.where(kind == labels_ref[...], 1.0, 0.0).astype(BF)
        copy(n).wait()
        left_ref[n, :GROUP, :] = held[n % 2].T


def left_of(numbers, places, expression, labels):
    cells = expression.shape[0]
    count = len(places)
    return call(
        functools.partial(left_kernel, places),
        "left",
        [(numbers, IN_SMEM), (pinned(expression, HBM), IN_PLACE), (labels, IN_VMEM)],
        [(VMEM((count, GROUP + KINDS, cells), BF), IN_VMEM)],
        [pltpu.VMEM((2, cells, GROUP), BF), pltpu.SemaphoreType.DMA((2,))],
    )[0]


def first_kernel(counts_ref, raised_ref, near_ref, far_ref, left_ref, low_ref, dens_ref, factor_ref, front_ref, back_ref, total):
    cells = raised_ref.shape[0]
    lines = cells // LANES
    row = lax.broadcasted_iota(jnp.int32, (lines, LANES), 0) * LANES + lax.broadcasted_iota(
        jnp.int32, (lines, LANES), 1
    )
    factor_ref[...] = jnp.where(row < counts_ref[0], 1.0 / (near_ref[...] + far_ref[...]), 0.0)
    mass = 0.0
    for at in range(lines):
        probs = raised_ref[line_of(at), :] * to_column(factor_ref[pl.ds(at, 1), :])
        low_ref[line_of(at), :] = probs.astype(BF)
        mass = mass + jnp.sum(probs, axis=0, keepdims=True)
        if at % 2:
            part = pl.ds((at // 2) * CHUNK, CHUNK)
            more = jnp.dot(left_ref[0, :, part], low_ref[part, :], preferred_element_type=F32)
            if at == 1:
                total[...] = more
            elif at + 1 < lines:
                total[...] += more
            else:
                whole = (total[...] + more).astype(BF)
                front_ref[...] = whole[:FRONT]
                back_ref[...] = whole[FRONT:]
    dens_ref[...] = mass


def first_of(counts, raised, near, far, left):
    cells, width = raised.shape
    rows = left.shape[1]
    return call(
        first_kernel,
        "first",
        [(counts, IN_SMEM)] + [(a, IN_VMEM) for a in (raised, near, far, left)],
        [(VMEM((cells, width), BF), IN_VMEM), (plain(1, width), IN_VMEM)]
        + [(plain(*near.shape), IN_VMEM), (plain(FRONT, width, dtype=BF), IN_VMEM), (plain(BACK, width, dtype=BF), IN_VMEM)],
        [pltpu.VMEM((rows, width), F32)],
    )


def blocks_kernel(which, left_ref, low_ref, *out_refs):
    width = low_ref.shape[1]
    tile = width // 3
    for n, out_ref in zip(which, out_refs):

        def step(at, _, n=n, out_ref=out_ref):
            columns = pl.ds(pl.multiple_of(at * tile, LANES), tile)
            out_ref[:, columns] = jnp.dot(
                left_ref[n], low_ref[:, columns], preferred_element_type=F32
            ).astype(out_ref.dtype)
            return 0

        lax.fori_loop(0, 3, step, 0)


def blocks_of(left, low, which, dtype):
    cells, width = low.shape
    rows = left.shape[1]
    return call(
        functools.partial(blocks_kernel, which),
        "blocks",
        [(left, IN_VMEM), (low, IN_VMEM)],
        [(plain(rows, width, dtype=dtype), IN_VMEM)] * len(which),
        limit=6,
    )


def early_kernel(numbers_ref, target_ref, density_ref, side_ref, spot_ref, own_ref, sums_ref, held, sems):
    genes = target_ref.shape[0]
    count = genes // GROUP

    def copy(n):
        rows = pl.ds(n * GROUP, GROUP)
        return pltpu.make_async_copy(target_ref.at[rows], held.at[n % 2], sems.at[n % 2])

    mine = pltpu.make_async_copy(target_ref.at[columns_of(numbers_ref[0])], own_ref, sems.at[2])
    mine.start()
    copy(0).start()
    spot_ref[...] = jnp.zeros_like(spot_ref)
    for n in range(count):
        if n + 1 < count:
            copy(n + 1).start()
        copy(n).wait()
        target = held[n % 2].astype(F32)
        spot_ref[...] += jnp.sum(target * target, axis=0, keepdims=True)
    mine.wait()
    side = side_ref[...]
    other = 1.0 - side
    density = density_ref[...]
    target = own_ref[...].astype(F32)
    square = target * target
    lane = lax.broadcasted_iota(jnp.int32, (GROUP, LANES), 1)
    columns = jnp.where(
        lane == 0,
        jnp.sum(square * other, axis=1, keepdims=True),
        jnp.where(lane == 1, jnp.sum(square * side, axis=1, keepdims=True), 0.0),
    )
    sums_ref[0:2, :] = columns.T[:2]
    logged = density * jnp.log(density)
    known = packed_row([row_sum(value * part) for value in (1.0, density, logged) for part in (other, side)])
    sums_ref[2:3, :] = jnp.concatenate([known, jnp.zeros_like(known)], axis=1)


def early_of(numbers, target, density, side):
    width = target.shape[1]
    return call(
        early_kernel,
        "early",
        [(numbers, IN_SMEM), (pinned(target, HBM), IN_PLACE), (density, IN_VMEM), (side, IN_VMEM)],
        [(plain(1, width), IN_VMEM), (VMEM((GROUP, width), BF), IN_VMEM), (plain(3, GROUP), IN_VMEM)],
        [pltpu.VMEM((2, GROUP, width), BF), pltpu.SemaphoreType.DMA((3,))],
        limit=16,
    )


def half_kernel(kept_ref, front_ref, half_ref, low_ref):
    half_ref[...] = kept_ref[...]
    half_ref[:FRONT] += front_ref[...].astype(F32)
    low_ref[...] = half_ref[...].astype(BF)


def half_of(kept, front):
    return call(
        half_kernel,
        "half",
        [(kept, IN_VMEM), (front, IN_VMEM)],
        [(plain(*kept.shape), IN_VMEM), (plain(*kept.shape, dtype=BF), IN_VMEM)],
        limit=10,
    )


def join_kernel(lines, numbers_ref, part_ref, back_ref, out_ref):
    out_ref[:FRONT] = part_ref[:FRONT].astype(BF)
    line = line_at(numbers_ref)
    here = jnp.logical_or(line == lines[0], line == lines[1])

    @pl.when(here)
    def _():
        out_ref[FRONT:] = (part_ref[FRONT:] + back_ref[...].astype(F32)).astype(BF)

    @pl.when(jnp.logical_not(here))
    def _():
        out_ref[FRONT:] = part_ref[FRONT:].astype(BF)


def join_of(numbers, part, back, lines):
    return call(
        functools.partial(join_kernel, lines),
        "join",
        [(numbers, IN_SMEM), (part, IN_VMEM), (back, IN_VMEM)],
        [(plain(*part.shape, dtype=BF), IN_VMEM)],
        limit=8,
    )[0]


def step_kernel(kept_ref, cross_ref, up_ref, down_ref, up_out, down_out):
    half = kept_ref[...] + cross_ref[...].astype(F32)
    up_out[...] = (half + up_ref[...].astype(F32)).astype(BF)
    down_out[...] = (half + down_ref[...].astype(F32)).astype(BF)


def step_of(kept, cross, up, down):
    return call(
        step_kernel,
        "step",
        [(a, IN_VMEM) for a in (kept, cross, up, down)],
        [(plain(*up.shape, dtype=BF), IN_VMEM)] * 2,
        limit=12,
    )


def turn_kernel(numbers_ref, kept_ref, cross_ref, early_ref, up_ref, down_ref, up_out, down_out):
    half = kept_ref[...] + cross_ref[...].astype(F32)
    for place, more_ref, out_ref in ((2, up_ref, up_out), (1, down_ref, down_out)):
        here = line_at(numbers_ref) == place

        @pl.when(here)
        def _(more_ref=more_ref, out_ref=out_ref):
            out_ref[...] = (early_ref[...] + more_ref[...].astype(F32)).astype(BF)

        @pl.when(jnp.logical_not(here))
        def _(more_ref=more_ref, out_ref=out_ref):
            out_ref[...] = (half + more_ref[...].astype(F32)).astype(BF)


def turn_of(numbers, kept, cross, early, up, down):
    return call(
        turn_kernel,
        "turn",
        [(numbers, IN_SMEM)] + [(a, IN_VMEM) for a in (kept, cross, early, up, down)],
        [(plain(*up.shape, dtype=BF), IN_VMEM)] * 2,
        limit=15,
    )


def sums_kernel(
    kept_ref, cross_ref, up_ref, down_ref, target_ref, side_ref, dens_ref,
    total_ref, low_ref, gene_ref, spot_ref,
):
    total = (
        kept_ref[...] + cross_ref[...].astype(F32) + up_ref[...].astype(F32) + down_ref[...].astype(F32)
    )
    total_ref[...] = total
    pred = total[:GROUP]
    low_ref[...] = pred.astype(BF)
    dot = pred * target_ref[...].astype(F32)
    square = pred * pred
    side = side_ref[...]
    spot_ref[0:1, :] = jnp.sum(dot, axis=0, keepdims=True)
    spot_ref[1:2, :] = jnp.sum(square, axis=0, keepdims=True)
    spot_ref[2:3, :] = dens_ref[...]
    sums = [
        jnp.sum(dot * (1.0 - side), axis=1, keepdims=True),
        jnp.sum(dot * side, axis=1, keepdims=True),
        jnp.sum(square * (1.0 - side), axis=1, keepdims=True),
        jnp.sum(square * side, axis=1, keepdims=True),
    ]
    lane = lax.broadcasted_iota(jnp.int32, (GROUP, LANES), 1)
    packed = jnp.zeros((GROUP, LANES), F32)
    for place, column in enumerate(sums):
        packed = jnp.where(lane == place, column, packed)
    gene_ref[...] = packed.T[:4]


def sums_of(kept, *inputs):
    rows, width = kept.shape
    return call(
        sums_kernel,
        "sums",
        [(a, IN_VMEM) for a in (kept, *inputs)],
        [(VMEM((rows, width), F32), IN_VMEM), (plain(GROUP, width, dtype=BF), IN_VMEM)]
        + [(plain(4, GROUP), IN_VMEM), (plain(3, width), IN_VMEM)],
        limit=16,
    )


def grads_kernel(
    scale, slots, total_ref, target_ref, side_ref, density_ref, gene_ref, gene_more_ref, early_ref, spot_ref, spot_target_ref,
    more0_ref, more1_ref, more2_ref, out_ref, dens_ref, cross_ref, loss_ref
):
    side = side_ref[...]
    other = 1.0 - side
    spot = spot_ref[...] + more0_ref[...] + more1_ref[...] + more2_ref[...]
    inv_spot_pred = lax.rsqrt(spot[1:2])
    inv_spot_target = lax.rsqrt(spot_target_ref[...])
    cosine = spot[0:1] * inv_spot_pred * inv_spot_target
    known = early_ref[2:3, :]
    weight = scale / (other * known[:, 0:1] + side * known[:, 1:2])
    spot_along_target = inv_spot_pred * inv_spot_target * weight
    spot_along_pred = cosine * inv_spot_pred * inv_spot_pred * weight
    gene = gene_ref[...] + gene_more_ref[...]
    inv_gene_pred = lax.rsqrt(gene[2:4])
    inv_gene_target = lax.rsqrt(early_ref[0:2, :])
    gene_cosine = gene[0:2] * inv_gene_pred * inv_gene_target
    along = jnp.concatenate(
        [
            (scale / GENES) * inv_gene_pred * inv_gene_target,
            (scale / GENES) * gene_cosine * inv_gene_pred * inv_gene_pred,
            jnp.zeros((LANES - 4, GROUP), F32),
        ],
        axis=0,
    ).T
    along_target = along[:, 0:1] * other + along[:, 1:2] * side + spot_along_target
    along_pred = along[:, 2:3] * other + along[:, 3:4] * side + spot_along_pred
    out_ref[:GROUP] = (total_ref[:GROUP] * along_pred - target_ref[...].astype(F32) * along_target).astype(BF)
    out_ref[GROUP:] = total_ref[GROUP:].astype(BF)
    dens_pred = spot[2:3] / slots
    dens_ref[...] = dens_pred
    cross = density_ref[...] * jnp.log(dens_pred)
    cross_ref[...] = packed_row([row_sum(value * part) for value in (cross, dens_pred, cosine) for part in (other, side)])
    loss_ref[...] = packed_row([row_sum(gene_cosine[0:1]), row_sum(gene_cosine[1:2])])


def grads_of(scale, slots, total, *inputs):
    rows, width = total.shape
    return call(
        functools.partial(grads_kernel, scale, slots),
        "grads",
        [(a, IN_VMEM) for a in (total, *inputs)],
        [(plain(rows, width, dtype=BF), IN_VMEM), (plain(1, width), IN_VMEM)]
        + [(plain(1, LANES), IN_VMEM)] * 2,
        limit=14,
    )


def density_kernel(scale, slots, early_ref, cross_ref, cross_more_ref, side_ref, density_ref, dens_ref, out_ref, cross_out):
    side = side_ref[...]
    other = 1.0 - side
    known = early_ref[2:3, :]
    cross = cross_ref[...] + cross_more_ref[...]
    cross_out[...] = cross
    inverse = other / cross[:, 2:3] + side / cross[:, 3:4]
    dens_mass = other * known[:, 2:3] + side * known[:, 3:4]
    out_ref[...] = (scale / slots) * (inverse - density_ref[...] / (dens_mass * dens_ref[...]))


def density_of(scale, slots, early, cross, cross_more, side, density, dens):
    return call(
        functools.partial(density_kernel, scale, slots),
        "density",
        [(a, IN_VMEM) for a in (early, cross, cross_more, side, density, dens)],
        [(plain(*side.shape), IN_VMEM), (plain(1, LANES), IN_VMEM)],
    )


def table_kernel(early_ref, cross_ref, loss_ref, more0_ref, more1_ref, more2_ref, out_ref):
    known = early_ref[2:3, :LANES]
    cross = cross_ref[...]
    loss = loss_ref[...] + more0_ref[...] + more1_ref[...] + more2_ref[...]
    for k in range(2):
        one = lambda row, at: row[:, 2 * at + k : 2 * at + k + 1]
        count, dens_mass, dens_log = one(known, 0), one(known, 1), one(known, 2)
        cross_log, pred_mass, cosine_sum = one(cross, 0), one(cross, 1), one(cross, 2)
        divergence = (dens_log - cross_log) / dens_mass - jnp.log(dens_mass) + jnp.log(pred_mass)
        row = packed_row([loss[:, k : k + 1] / GENES, cosine_sum / count, divergence])
        out_ref[k : k + 1, :] = row[:, :3]


def table_of(early, cross, loss, mores):
    return call(
        table_kernel,
        "table",
        [(a, IN_VMEM) for a in (early, cross, loss, *mores)],
        [(plain(2, 3), IN_VMEM)],
    )[0]


def choose_kernel(plan, numbers_ref, *refs):
    count = max(max(choices) for choices, _, _, _, _ in plan) + 1
    sources, out_refs, sems = refs[:count], refs[count:-1], refs[-1]
    line = line_at(numbers_ref)
    for place in range(4):

        @pl.when(line == place)
        def _(place=place):
            copies = [
                pltpu.make_async_copy(
                    sources[choices[place]].at[pl.ds(start, rows)], out_refs[out].at[pl.ds(to, rows)], sems.at[n]
                )
                for n, (choices, start, rows, out, to) in enumerate(plan)
            ]
            for copy in copies:
                copy.start()
            for copy in copies:
                copy.wait()


def choose_of(numbers, arrays, outputs, plan):
    width = arrays[0].shape[1]
    return call(
        functools.partial(choose_kernel, plan),
        "choose",
        [(numbers, IN_SMEM)] + [(a, IN_PLACE) for a in arrays],
        [(plain(rows, width, dtype=BF), IN_PLACE) for rows in outputs],
        [pltpu.SemaphoreType.DMA((len(plan),))],
    )


def mine_at(numbers_ref, turn):
    return order_of(line_at(numbers_ref), turn) % 2 == numbers_ref[1] % 2


def keep(numbers_ref, turn, grads, mine_ref, theirs_ref):
    mine = mine_at(numbers_ref, turn)

    @pl.when(mine)
    def _():
        mine_ref[...] = grads[...]

    @pl.when(jnp.logical_not(mine))
    def _():
        theirs_ref[...] = grads[...].astype(BF)


def update_kernel(start, place, numbers_ref, expr_ref, low_ref, acc_ref, mass_ref, types_ref, block_ref, *refs):
    acc_out, mass_out, types_out, mine_ref, theirs_ref, held, turned, grads, sem = refs[-9:]
    cells = low_ref.shape[0]
    copy = pltpu.make_async_copy(expr_ref.at[:, columns_of(block_at(numbers_ref, place))], held, sem)
    copy.start()
    kinds = pl.ds(pl.multiple_of(block_at(numbers_ref, place) * KINDS, KINDS), KINDS)
    types_out[kinds, :] = block_ref[GROUP:, :].astype(F32) * NTYPE
    turned[...] = block_ref[:GROUP, :].T
    copy.wait()
    for at in range(cells // CHUNK):
        part = pl.ds(at * CHUNK, CHUNK)
        expr = held[part, :]
        low = low_ref[part, :]
        more = jnp.dot(expr, block_ref[:GROUP, :], preferred_element_type=F32)
        grad = jnp.dot(low, turned[...], preferred_element_type=F32)
        grads[part, :] = grad
        mass = jnp.sum(expr.astype(F32) * grad, axis=1, keepdims=True)
        if start:
            dens = acc_ref[...]
            acc_out[part, :] = more + dens
            mass = mass + jnp.sum(low.astype(F32) * dens, axis=1, keepdims=True)
        else:
            acc_out[part, :] += more
        for half in range(CHUNK // LANES):
            line = pl.ds(at * (CHUNK // LANES) + half, 1)
            row = to_row(mass[half * LANES : (half + 1) * LANES])
            mass_out[line, :] = row if start else row + mass_ref[line, :]
    keep(numbers_ref, place[0], grads, mine_ref, theirs_ref)


def update_of(numbers, place, block, expression, low, acc, mass, types, start=False, kept=()):
    cells, width = low.shape
    inputs = [(numbers, IN_SMEM), (pinned(expression, HBM), IN_PLACE)]
    inputs += [(a, IN_VMEM) for a in (low, acc, mass, types, block, *kept)]
    aliases = {5: 2} if start else {3: 0, 5: 2}
    if kept:
        aliases |= {7: 3, 8: 4}
    acc, mass, types, *kept = call(
        functools.partial(update_kernel, start, place),
        "update",
        inputs,
        [(VMEM((cells, width), F32), IN_VMEM), (plain(*mass.shape), IN_VMEM), (VMEM((NTYPE, width), F32), IN_VMEM)]
        + [(VMEM((cells, GROUP), F32), IN_VMEM), (VMEM((cells, GROUP), BF), IN_VMEM)],
        [
            pltpu.VMEM((cells, GROUP), BF),
            pltpu.VMEM((width, GROUP), BF),
            pltpu.VMEM((cells, GROUP), F32),
            pltpu.SemaphoreType.DMA,
        ],
        aliases=aliases,
        limit=9,
    )
    return acc, mass, types, kept


def part_kernel(place, numbers_ref, expr_ref, low_ref, mass_ref, types_ref, front_ref, back_ref, *refs):
    mass_out, types_out, mine_ref, theirs_ref, held, turned, grads, sem = refs
    cells = low_ref.shape[0]
    copy = pltpu.make_async_copy(expr_ref.at[:, columns_of(block_at(numbers_ref, place))], held, sem)
    copy.start()
    kinds = pl.ds(pl.multiple_of(block_at(numbers_ref, place) * KINDS, KINDS), KINDS)
    types_out[kinds, :] = back_ref[GROUP - FRONT :, :].astype(F32) * NTYPE
    turned[...] = jnp.concatenate([front_ref[...], back_ref[: GROUP - FRONT, :]], axis=0).T
    copy.wait()
    for at in range(cells // CHUNK):
        part = pl.ds(at * CHUNK, CHUNK)
        grad = jnp.dot(low_ref[part, :], turned[...], preferred_element_type=F32)
        grads[part, :] = grad
        mass = jnp.sum(held[part, :].astype(F32) * grad, axis=1, keepdims=True)
        for half in range(CHUNK // LANES):
            line = pl.ds(at * (CHUNK // LANES) + half, 1)
            mass_out[line, :] = mass_ref[line, :] + to_row(mass[half * LANES : (half + 1) * LANES])
    keep(numbers_ref, place[0], grads, mine_ref, theirs_ref)


def part_of(numbers, place, front, back, expression, low, mass, types):
    cells, width = low.shape
    return call(
        functools.partial(part_kernel, place),
        "part",
        [(numbers, IN_SMEM), (pinned(expression, HBM), IN_PLACE)]
        + [(a, IN_VMEM) for a in (low, mass, types, front, back)],
        [(plain(*mass.shape), IN_VMEM), (VMEM((NTYPE, width), F32), IN_VMEM)]
        + [(VMEM((cells, GROUP), F32), IN_VMEM), (VMEM((cells, GROUP), BF), IN_VMEM)],
        [
            pltpu.VMEM((cells, GROUP), BF),
            pltpu.VMEM((width, GROUP), BF),
            pltpu.VMEM((cells, GROUP), F32),
            pltpu.SemaphoreType.DMA,
        ],
        aliases={4: 1},
        limit=14,
    )


def pair_kernel(mine_ref, near_ref, out_ref):
    out_ref[...] = (mine_ref[...] + near_ref[...].astype(F32)).astype(BF)


def pair_of(mine, near):
    return call(
        pair_kernel,
        "pair",
        [(mine, IN_VMEM), (near, IN_VMEM)],
        [(plain(*mine.shape, dtype=BF), IN_VMEM)],
    )[0]


def owned_kernel(places, numbers_ref, result_ref, mine_ref, near_ref, far_ref, out_ref):
    rung = numbers_ref[0] % 2
    for turn, other in places:

        @pl.when(order_of(line_at(numbers_ref), turn) == numbers_ref[1])
        def _(other=other):
            total = mine_ref[...] + near_ref[...].astype(F32) + far_ref[...].astype(F32)
            out_ref[:, columns_of(1 - rung if other else rung)] = total


def owned_of(numbers, places, result, mine, near, far):
    return call(
        functools.partial(owned_kernel, places),
        "owned",
        [(numbers, IN_SMEM)] + [(a, IN_VMEM) for a in (result, mine, near, far)],
        [(VMEM(result.shape, F32), IN_VMEM)],
        aliases={1: 0},
        limit=8,
    )[0]


def finish_kernel(
    place, numbers_ref, expr_ref, front_ref, back_ref, logits_ref, factor_ref, acc_ref, mass_ref, more_ref, out_ref,
    expr, block, held, sem, sems
):
    lines = mass_ref.shape[0]
    depth = held.shape[0]
    copy = pltpu.make_async_copy(expr_ref.at[:, columns_of(block_at(numbers_ref, place))], expr, sem)
    copy.start()
    block[:FRONT] = front_ref[...]
    block[FRONT:] = back_ref[: GROUP - FRONT, :]
    copy.wait()
    copies = []
    for at in range(lines):
        if at >= depth:
            copies[at - depth].wait()
        one = pl.ds(at, 1)
        rows = line_of(at)
        grad = acc_ref[rows, :] + jnp.dot(expr[rows, :], block[...], preferred_element_type=F32)
        probs = jnp.exp(logits_ref[rows, :]) * to_column(factor_ref[one, :])
        held[at % depth] = probs * (grad - to_column(mass_ref[one, :] + more_ref[one, :]))
        copies.append(pltpu.make_async_copy(held.at[at % depth], out_ref.at[rows], sems.at[at % depth]))
        copies[-1].start()
    for copy in copies[-depth:]:
        copy.wait()


def finish_of(numbers, place, expression, front, back, logits, factor, acc, mass, more):
    rows, width = logits.shape
    depth = 4
    inputs = (front, back, pinned(logits, VMEM), factor, acc, mass, more)
    return call(
        functools.partial(finish_kernel, place),
        "finish",
        [(numbers, IN_SMEM), (pinned(expression, HBM), IN_PLACE)] + [(a, IN_VMEM) for a in inputs],
        [(HBM((rows, width), F32), IN_PLACE)],
        [
            pltpu.VMEM((rows, GROUP), BF),
            pltpu.VMEM((GROUP, width), BF),
            pltpu.VMEM((depth, LANES, width), F32),
            pltpu.SemaphoreType.DMA,
            pltpu.SemaphoreType.DMA((depth,)),
        ],
        limit=12,
    )[0]


def blank_kernel(*refs):
    for ref in refs:
        ref[...] = jnp.zeros_like(ref)


def blank(*shapes):
    return call(blank_kernel, "blank", [], [(VMEM(shape, F32), IN_VMEM) for shape in shapes])


tied = lax.optimization_barrier


def across(array):
    return lax.ppermute(array, "cells", [(at, at ^ 1) for at in range(8)])


def along(array, way, allowed):
    pairs = [(at, at + 2 * way) for at in range(8) if 0 <= at + 2 * way < 8 and allowed(at // 2)]
    return lax.ppermute(array, "cells", pairs)


def on_line(array, step):
    return lax.ppermute(array, "cells", [(at, at ^ (2 * step)) for at in range(8)])


def swapped(array, step):
    return lax.ppermute(array, "spots", [(at, at ^ step) for at in range(4)])


def near_of(theirs, turns):
    pairs = [
        (at * 4 + place, at * 4 + (place ^ 1))
        for at in range(8)
        for place in range(4)
        if any(order_of(at // 2, turn) % 2 != place % 2 for turn in turns)
    ]
    return lax.ppermute(theirs, ("cells", "spots"), pairs)


def far_of(mine, near, turns):
    pairs = []
    for at in range(8):
        for owner in (order_of(at // 2, turn) for turn in turns):
            pairs.append((at * 4 + (owner ^ 2), at * 4 + owner))
    return lax.ppermute(pair_of(mine, near), ("cells", "spots"), pairs)


def ladder(logits, expression, target, density, assignment, labels, counts):
    cells, width = logits.shape
    slots = float(cells * lax.axis_size("cells"))
    scale = float(cells * lax.axis_size("cells") * width * lax.axis_size("spots"))
    numbers = jnp.stack([lax.axis_index("cells"), lax.axis_index("spots")]).astype(jnp.int32)
    logits, numbers = tied((logits, numbers))
    side = (assignment == 1).astype(F32)[None, :]
    density = density[None, :]
    labels = labels[None, :]

    raised, mass = mass_of(logits)
    left_a = left_of(numbers, ((3, 1), (3, 0)), expression, labels)
    mass_near = mass + swapped(mass, 1)
    mass_near, left_a = tied((mass_near, left_a))
    mass_far = swapped(mass_near, 2)
    left_b = left_of(numbers, ((2, 1), (2, 0)), expression, labels)
    mass_far, left_b = tied((mass_far, left_b))
    low, dens_part, factor, front, back = first_of(counts, raised, mass_near, mass_far, left_a)

    front = across(front)
    back = on_line(back, 1)
    (kept3,) = blocks_of(left_a, low, (1,), F32)
    (send2,) = blocks_of(left_b, low, (0,), F32)
    left_c = left_of(numbers, ((1, 1), (1, 0), (0, 1), (0, 0)), expression, labels)
    front, back, kept3, send2, left_c = tied((front, back, kept3, send2, left_c))
    send2 = join_of(numbers, send2, back, (1, 2))
    cross2 = across(send2)
    front, send2 = tied((front, send2))
    half3, half3_low = half_of(kept3, front)
    up = along(half3_low, 1, lambda at: at <= 0)
    down = along(half3_low, -1, lambda at: at >= 3)
    (kept2,) = blocks_of(left_b, low, (1,), F32)
    (send1,) = blocks_of(left_c, low, (0,), BF)
    (kept1,) = blocks_of(left_c, low, (1,), F32)
    (send0,) = blocks_of(left_c, low, (2,), F32)
    send0 = join_of(numbers, send0, back, (0, 3))
    cross1 = across(send1)
    up, down, cross2, kept2, kept1, send0 = tied((up, down, cross2, kept2, kept1, send0))
    up, down = step_of(kept2, cross2, up, down)
    up = along(up, 1, lambda at: at <= 1)
    down = along(down, -1, lambda at: at >= 2)
    (kept0,) = blocks_of(left_c, low, (3,), F32)
    spot_target, own_target, early = early_of(numbers, target, density, side)
    early = early + swapped(early, 1)
    early = early + swapped(early, 2)
    cross0 = across(send0)
    up, down, cross1, early, kept0 = tied((up, down, cross1, early, kept0))
    up, down = turn_of(numbers, kept1, cross1, half3, up, down)
    up = along(up, 1, lambda at: True)
    down = along(down, -1, lambda at: True)
    up, down, cross0 = tied((up, down, cross0))

    total, predicted, gene, spots = sums_of(kept0, cross0, up, down, own_target, side, dens_part)
    spots_more = across(spots)
    gene_more = swapped(gene, 1)
    spots_more, gene_more = tied((spots_more, gene_more))
    gene = gene + gene_more
    gene_more = swapped(gene, 2)
    spots = spots + spots_more
    mores = [on_line(spots, step) for step in (3, 2, 1)]
    own, dens, cross, loss = grads_of(
        scale, slots, total, own_target, side, density, gene, gene_more, early, spots, spot_target, *mores
    )

    def update(place, block, acc, mass, types, **options):
        return update_of(numbers, place, block, expression, low, acc, mass, types, **options)

    up0 = along(own, 1, lambda at: True)
    down0 = along(own, -1, lambda at: True)
    cross0 = across(own)
    cross = cross + swapped(cross, 1)
    dens_row, cross = density_of(scale, slots, early, cross, swapped(cross, 2), side, density, dens)
    types, result = blank((NTYPE, width), (cells, 2 * GROUP))
    acc, mass, types, (mine0, theirs0) = update((0, 0), own, dens_row, mass, types, start=True)
    near0 = near_of(theirs0, (0,))
    up0, down0, cross0, mass, near0 = tied((up0, down0, cross0, mass, near0))

    whole = [((1, 1, 0, 0), 0, ROWS, 0, 0)]
    (block1,) = choose_of(numbers, (up0, down0), (ROWS,), whole)
    up1 = along(up0, 1, lambda at: at >= 1)
    down1 = along(down0, -1, lambda at: at <= 2)
    cross1 = across(block1)
    far0 = far_of(mine0, near0, (0,))
    acc, mass, types, kept = update((0, 1), cross0, acc, mass, types)
    acc, mass, types, (mine1, theirs1) = update((1, 0), block1, acc, mass, types, kept=kept)
    near1 = near_of(theirs1, (0, 1))
    up1, down1, cross1, mass, near1, far0 = tied((up1, down1, cross1, mass, near1, far0))

    (block2,) = choose_of(numbers, (up1, down1), (ROWS,), whole)
    up2 = along(up1, 1, lambda at: at >= 2)
    down2 = along(down1, -1, lambda at: at <= 1)
    cross2 = across(block2)
    far1 = far_of(mine1, near1, (0, 1))
    acc, mass, types, kept = update((2, 0), block2, acc, mass, types)
    acc, mass, types, (mine2, theirs2) = update((1, 1), cross1, acc, mass, types, kept=kept)
    near2 = near_of(theirs2, (1, 2))
    up2, down2, cross2, mass, near2, far1 = tied((up2, down2, cross2, mass, near2, far1))

    block3, front, back = choose_of(
        numbers,
        (up0, down0, up2, down2, cross0, cross2),
        (ROWS, FRONT, BACK),
        [
            ((3, 0, 1, 2), 0, ROWS, 0, 0),
            ((3, 0, 1, 2), 0, FRONT, 1, 0),
            ((4, 5, 5, 4), FRONT, BACK, 2, 0),
        ],
    )
    front = across(front)
    back = on_line(back, 1)
    far2 = far_of(mine2, near2, (1, 2))
    acc, mass, types, kept = update((2, 1), cross2, acc, mass, types)
    acc, mass, types, (mine3, theirs3) = update((3, 0), block3, acc, mass, types, kept=kept)
    near3 = near_of(theirs3, (2, 3))
    front, back, acc, mass = tied((front, back, acc, mass))

    mass, types, mine4, theirs4 = part_of(numbers, (3, 1), front, back, expression, low, mass, types)
    mass_far = swapped(mass, 2)
    near4 = near_of(theirs4, (3,))
    loss_more = across(loss)
    mass_far, near3, far2, loss_more = tied((mass_far, near3, far2, loss_more))
    loss = loss + loss_more
    mass = mass + mass_far
    mass_near = swapped(mass, 1)
    far3 = far_of(mine3, near3, (2, 3))
    far4 = far_of(mine4, near4, (3,))
    result = owned_of(numbers, ((0, 0),), result, mine0, near0, far0)
    result = owned_of(numbers, ((0, 1), (1, 0)), result, mine1, near1, far1)
    result = owned_of(numbers, ((1, 1), (2, 0)), result, mine2, near2, far2)
    mores = [on_line(loss, step) for step in (1, 2, 3)]
    mass_near, result = tied((mass_near, result))
    grad_logits = finish_of(numbers, (3, 1), expression, front, back, logits, factor, acc, mass, mass_near)
    mores, grad_logits = tied((mores, grad_logits))
    table = table_of(early, cross, loss, mores)
    result = owned_of(numbers, ((2, 1), (3, 0)), result, mine3, near3, far3)
    result = owned_of(numbers, ((3, 1),), result, mine4, near4, far4)
    return (predicted, grad_logits, result, table, types)


def solution(mesh):
    in_specs = (
        P("cells", "spots"),
        P("cells", None),
        P(None, "spots"),
        P("spots"),
        P("spots"),
        P("cells"),
        P("cells"),
    )
    out_specs = (
        P("cells", "spots"),
        P("cells", "spots"),
        P("cells", "spots"),
        P(),
        P(None, "spots"),
    )
    fits = mesh.shape["cells"] == 8 and mesh.shape["spots"] == 4
    return jax.shard_map(
        ladder if fits else general, mesh=mesh, in_specs=in_specs, out_specs=out_specs, check_vma=False
    )
```

```python
import functools
import math

import jax
import jax.numpy as jnp
import numpy as np
from jax import lax
from jax.experimental import pallas as pl
from jax.experimental.pallas import tpu as pltpu
from jax.sharding import PartitionSpec as P

GENES = 2048
NTYPE = 128
LANES = 128
BF = jnp.bfloat16
F32 = jnp.float32
highest = lax.Precision.HIGHEST


def over_rows(left_side, right_side):
    return lax.dot_general(
        left_side, right_side, (((0,), (0,)), ((), ())), preferred_element_type=F32
    )


def over_columns(left_side, right_side):
    return lax.dot_general(
        left_side, right_side, (((1,), (1,)), ((), ())), preferred_element_type=F32
    )


def general(logits, expression, target, density, assignment, labels, counts):
    row_count = logits.shape[0]
    spot_width = logits.shape[1]
    cell_devices = lax.axis_size("cells")
    slot_total = float(row_count * cell_devices)
    scale = float(row_count * cell_devices * spot_width * lax.axis_size("spots"))
    live = (jnp.arange(row_count, dtype=jnp.int32) < counts[0])[:, None]
    raised = jnp.exp(logits)
    row_mass = lax.psum(jnp.sum(raised, axis=1), "spots")
    probs = jnp.where(live, raised / row_mass[:, None], 0.0)
    probs_low = probs.astype(BF)
    one_hot = (labels[:, None] == jnp.arange(NTYPE, dtype=jnp.int32)[None, :]).astype(BF)
    type_total, dens_total = lax.psum((over_rows(one_hot, probs_low), jnp.sum(probs, axis=0)), "cells")
    gene_rows = GENES // cell_devices
    predicted = lax.psum_scatter(
        over_rows(expression, probs_low), "cells", scatter_dimension=0, tiled=True
    )
    target_full = lax.dynamic_slice_in_dim(
        target, lax.axis_index("cells") * gene_rows, gene_rows, 0
    ).astype(F32)
    spot_dot, spot_pred, spot_target = lax.psum(
        (
            jnp.sum(predicted * target_full, axis=0),
            jnp.sum(predicted * predicted, axis=0),
            jnp.sum(target_full * target_full, axis=0),
        ),
        "cells",
    )
    dens_pred = dens_total / slot_total
    sides = jnp.stack([assignment == 0, assignment == 1]).astype(F32)
    inv_spot_pred = lax.rsqrt(spot_pred)
    inv_spot_target = lax.rsqrt(spot_target)
    spot_cosine = spot_dot * inv_spot_pred * inv_spot_target
    columns = jnp.stack(
        [
            jnp.ones_like(density),
            density,
            density * jnp.log(density),
            density * jnp.log(dens_pred),
            dens_pred,
            spot_cosine,
        ]
    )
    slide_part = jnp.dot(sides, columns.T, precision=highest)
    gene_part = jnp.stack(
        [
            jnp.dot(predicted * target_full, sides.T, precision=highest),
            jnp.dot(predicted * predicted, sides.T, precision=highest),
            jnp.dot(target_full * target_full, sides.T, precision=highest),
        ]
    )
    slide_sums, gene_sums = lax.psum((slide_part, gene_part), "spots")
    spot_count, dens_mass, dens_log, cross_log, pred_mass, cosine_sum = [
        slide_sums[:, at] for at in range(6)
    ]
    inv_gene_pred = lax.rsqrt(gene_sums[1])
    inv_gene_target = lax.rsqrt(gene_sums[2])
    gene_cosine = gene_sums[0] * inv_gene_pred * inv_gene_target
    gene_along_target = jnp.dot(inv_gene_pred * inv_gene_target, sides, precision=highest)
    gene_along_pred = jnp.dot(gene_cosine * inv_gene_pred * inv_gene_pred, sides, precision=highest)
    spot_weight = 1.0 / jnp.dot(spot_count, sides, precision=highest)
    spot_along_target = inv_spot_pred * inv_spot_target * spot_weight
    spot_along_pred = spot_cosine * inv_spot_pred * inv_spot_pred * spot_weight
    grad_dens = scale * (
        jnp.dot(1.0 / pred_mass, sides, precision=highest)
        - density / (jnp.dot(dens_mass, sides, precision=highest) * dens_pred)
    )
    grad_pred = scale * (
        -(target_full * gene_along_target - predicted * gene_along_pred) / GENES
        - (target_full * spot_along_target[None, :] - predicted * spot_along_pred[None, :])
    )
    grad_low = lax.all_gather(grad_pred.astype(BF), "cells", axis=0, tiled=True)
    grad_probs = jnp.dot(expression, grad_low, preferred_element_type=F32)
    grad_expr_part = over_columns(probs_low, grad_low)
    gene_loss = lax.psum(jnp.sum(gene_cosine, axis=0), "cells")
    grad_probs = grad_probs + (grad_dens / slot_total)[None, :]
    row_total = lax.psum(jnp.sum(probs * grad_probs, axis=1), "spots")
    grad_logits = probs * (grad_probs - row_total[:, None])
    grad_expression = lax.psum_scatter(grad_expr_part, "spots", scatter_dimension=1, tiled=True)
    divergence = (dens_log - cross_log) / dens_mass - jnp.log(dens_mass) + jnp.log(pred_mass)
    table = jnp.stack([gene_loss / GENES, cosine_sum / spot_count, divergence], axis=1)
    return (predicted.astype(BF), grad_logits, grad_expression, table, type_total * NTYPE)


VMEM = pltpu.MemorySpace.VMEM
HBM = pltpu.MemorySpace.HBM
IN_VMEM = pl.BlockSpec(memory_space=VMEM)
IN_SMEM = pl.BlockSpec(memory_space=pltpu.MemorySpace.SMEM)
IN_PLACE = pl.BlockSpec(memory_space=pl.ANY)
CHUNK = 2 * LANES
MIB = 1024 * 1024
GROUP = GENES // 8
KINDS = NTYPE // 8
PIECES = 4
PAD = 16

FRONT = 144
ROWS = GROUP + KINDS
BACK = ROWS - FRONT
UPPER = GROUP // 2


def line_at(numbers_ref):
    return numbers_ref[0] // 2


def order_of(line, turn):
    return (line, 1 + line % 2, (line + 2) % 4, 3 - 3 * (line % 2))[turn]


def block_at(numbers_ref, place):
    turn, other = place
    rung = numbers_ref[0] % 2
    return 2 * order_of(line_at(numbers_ref), turn) + (1 - rung if other else rung)


def call(kernel, name, inputs, outputs, scratch=(), aliases=None, limit=8, flops=1024):
    return pl.pallas_call(
        kernel,
        in_specs=[spec for _, spec in inputs],
        out_specs=[spec for _, spec in outputs],
        out_shape=[shape for shape, _ in outputs],
        scratch_shapes=list(scratch),
        input_output_aliases=aliases or {},
        compiler_params=pltpu.CompilerParams(vmem_limit_bytes=limit * MIB),
        cost_estimate=pl.CostEstimate(flops=flops, bytes_accessed=1024, transcendentals=0),
        name=name,
    )(*[array for array, _ in inputs])


def plain(*shape, dtype=F32):
    return jax.ShapeDtypeStruct(shape, dtype)


def pinned(array, space):
    return pltpu.with_memory_space_constraint(array, space)


def to_row(column):
    return jnp.broadcast_to(column, (LANES, LANES)).T[:1]


def to_column(row):
    return jnp.broadcast_to(row, (LANES, LANES)).T[:, :1]


def line_of(at):
    return pl.ds(at * LANES, LANES)


def columns_of(at):
    return pl.ds(pl.multiple_of(at * GROUP, GROUP), GROUP)


def packed_row(values):
    lane = lax.broadcasted_iota(jnp.int32, (1, LANES), 1)
    row = jnp.zeros((1, LANES), F32)
    for at, value in enumerate(values):
        row = jnp.where(lane == at, value, row)
    return row


def row_sum(row):
    return jnp.sum(row, axis=1, keepdims=True)


def mass_kernel(logits_ref, raised_ref, mass_ref, sems):
    lines = mass_ref.shape[0]
    copies = [
        pltpu.make_async_copy(logits_ref.at[line_of(at)], raised_ref.at[line_of(at)], sems.at[at])
        for at in range(lines)
    ]
    for copy in copies:
        copy.start()
    for at, copy in enumerate(copies):
        copy.wait()
        raised = jnp.exp(raised_ref[line_of(at), :])
        raised_ref[line_of(at), :] = raised
        mass_ref[pl.ds(at, 1), :] = to_row(jnp.sum(raised, axis=1, keepdims=True))


def mass_of(logits):
    rows, width = logits.shape
    lines = rows // LANES
    return call(
        mass_kernel,
        "mass",
        [(pinned(logits, HBM), IN_PLACE)],
        [(VMEM((rows, width), F32), IN_VMEM), (plain(lines, LANES), IN_VMEM)],
        [pltpu.SemaphoreType.DMA((lines,))],
    )


def left_kernel(places, numbers_ref, expr_ref, labels_ref, left_ref, held, sems):
    _, _, cells = left_ref.shape

    def copy(n):
        return pltpu.make_async_copy(
            expr_ref.at[:, columns_of(block_at(numbers_ref, places[n]))], held.at[n % 2], sems.at[n % 2]
        )

    copy(0).start()
    for n, place in enumerate(places):
        if n + 1 < len(places):
            copy(n + 1).start()
        kind = lax.broadcasted_iota(jnp.int32, (KINDS, cells), 0) + block_at(numbers_ref, place) * KINDS
        left_ref[n, GROUP:, :] = jnp.where(kind == labels_ref[...], 1.0, 0.0).astype(BF)
        copy(n).wait()
        left_ref[n, :GROUP, :] = held[n % 2].T


def left_of(numbers, places, expression, labels):
    cells = expression.shape[0]
    count = len(places)
    return call(
        functools.partial(left_kernel, places),
        "left",
        [(numbers, IN_SMEM), (pinned(expression, HBM), IN_PLACE), (labels, IN_VMEM)],
        [(VMEM((count, GROUP + KINDS, cells), BF), IN_VMEM)],
        [pltpu.VMEM((2, cells, GROUP), BF), pltpu.SemaphoreType.DMA((2,))],
    )[0]


def first_kernel(counts_ref, raised_ref, near_ref, far_ref, left_ref, low_ref, dens_ref, factor_ref, front_ref, back_ref, total):
    cells = raised_ref.shape[0]
    lines = cells // LANES
    row = lax.broadcasted_iota(jnp.int32, (lines, LANES), 0) * LANES + lax.broadcasted_iota(
        jnp.int32, (lines, LANES), 1
    )
    factor_ref[...] = jnp.where(row < counts_ref[0], 1.0 / (near_ref[...] + far_ref[...]), 0.0)
    mass = 0.0
    for at in range(lines):
        probs = raised_ref[line_of(at), :] * to_column(factor_ref[pl.ds(at, 1), :])
        low_ref[line_of(at), :] = probs.astype(BF)
        mass = mass + jnp.sum(probs, axis=0, keepdims=True)
        if at % 2:
            part = pl.ds((at // 2) * CHUNK, CHUNK)
            more = jnp.dot(left_ref[0, :, part], low_ref[part, :], preferred_element_type=F32)
            if at == 1:
                total[...] = more
            elif at + 1 < lines:
                total[...] += more
            else:
                whole = (total[...] + more).astype(BF)
                front_ref[...] = whole[:FRONT]
                back_ref[...] = whole[FRONT:]
    dens_ref[...] = mass


def first_of(counts, raised, near, far, left):
    cells, width = raised.shape
    rows = left.shape[1]
    return call(
        first_kernel,
        "first",
        [(counts, IN_SMEM)] + [(a, IN_VMEM) for a in (raised, near, far, left)],
        [(VMEM((cells, width), BF), IN_VMEM), (plain(1, width), IN_VMEM)]
        + [(plain(*near.shape), IN_VMEM), (plain(FRONT, width, dtype=BF), IN_VMEM), (plain(BACK, width, dtype=BF), IN_VMEM)],
        [pltpu.VMEM((rows, width), F32)],
    )


def blocks_kernel(which, left_ref, low_ref, *out_refs):
    width = low_ref.shape[1]
    tile = width // 3
    for n, out_ref in zip(which, out_refs):

        def step(at, _, n=n, out_ref=out_ref):
            columns = pl.ds(pl.multiple_of(at * tile, LANES), tile)
            out_ref[:, columns] = jnp.dot(
                left_ref[n], low_ref[:, columns], preferred_element_type=F32
            ).astype(out_ref.dtype)
            return 0

        lax.fori_loop(0, 3, step, 0)


def blocks_of(left, low, which, dtype):
    cells, width = low.shape
    rows = left.shape[1]
    return call(
        functools.partial(blocks_kernel, which),
        "blocks",
        [(left, IN_VMEM), (low, IN_VMEM)],
        [(plain(rows, width, dtype=dtype), IN_VMEM)] * len(which),
        limit=6,
    )


def early_kernel(numbers_ref, target_ref, density_ref, side_ref, spot_ref, own_ref, sums_ref, held, sems):
    genes = target_ref.shape[0]
    count = genes // GROUP

    def copy(n):
        rows = pl.ds(n * GROUP, GROUP)
        return pltpu.make_async_copy(target_ref.at[rows], held.at[n % 2], sems.at[n % 2])

    mine = pltpu.make_async_copy(target_ref.at[columns_of(numbers_ref[0])], own_ref, sems.at[2])
    mine.start()
    copy(0).start()
    spot_ref[...] = jnp.zeros_like(spot_ref)
    for n in range(count):
        if n + 1 < count:
            copy(n + 1).start()
        copy(n).wait()
        target = held[n % 2].astype(F32)
        spot_ref[...] += jnp.sum(target * target, axis=0, keepdims=True)
    mine.wait()
    side = side_ref[...]
    other = 1.0 - side
    density = density_ref[...]
    target = own_ref[...].astype(F32)
    square = target * target
    lane = lax.broadcasted_iota(jnp.int32, (GROUP, LANES), 1)
    columns = jnp.where(
        lane == 0,
        jnp.sum(square * other, axis=1, keepdims=True),
        jnp.where(lane == 1, jnp.sum(square * side, axis=1, keepdims=True), 0.0),
    )
    sums_ref[0:2, :] = columns.T[:2]
    logged = density * jnp.log(density)
    known = packed_row([row_sum(value * part) for value in (1.0, density, logged) for part in (other, side)])
    sums_ref[2:3, :] = jnp.concatenate([known, jnp.zeros_like(known)], axis=1)


def early_of(numbers, target, density, side):
    width = target.shape[1]
    return call(
        early_kernel,
        "early",
        [(numbers, IN_SMEM), (pinned(target, HBM), IN_PLACE), (density, IN_VMEM), (side, IN_VMEM)],
        [(plain(1, width), IN_VMEM), (VMEM((GROUP, width), BF), IN_VMEM), (plain(3, GROUP), IN_VMEM)],
        [pltpu.VMEM((2, GROUP, width), BF), pltpu.SemaphoreType.DMA((3,))],
        limit=16,
    )


def half_kernel(kept_ref, front_ref, half_ref, front_out, back_out):
    half_ref[...] = kept_ref[...]
    half_ref[:FRONT] += front_ref[...].astype(F32)
    front_out[...] = half_ref[:FRONT].astype(BF)
    back_out[...] = half_ref[FRONT:].astype(BF)


def half_of(kept, front):
    width = kept.shape[1]
    return call(
        half_kernel,
        "half",
        [(kept, IN_VMEM), (front, IN_VMEM)],
        [(plain(*kept.shape), IN_VMEM)] + [(plain(rows, width, dtype=BF), IN_VMEM) for rows in (FRONT, BACK)],
        limit=10,
    )


def join_kernel(lines, numbers_ref, part_ref, back_ref, out_ref):
    out_ref[:FRONT] = part_ref[:FRONT].astype(BF)
    line = line_at(numbers_ref)
    here = jnp.logical_or(line == lines[0], line == lines[1])

    @pl.when(here)
    def _():
        out_ref[FRONT:] = (part_ref[FRONT:] + back_ref[...].astype(F32)).astype(BF)

    @pl.when(jnp.logical_not(here))
    def _():
        out_ref[FRONT:] = part_ref[FRONT:].astype(BF)


def join_of(numbers, part, back, lines):
    return call(
        functools.partial(join_kernel, lines),
        "join",
        [(numbers, IN_SMEM), (part, IN_VMEM), (back, IN_VMEM)],
        [(plain(*part.shape, dtype=BF), IN_VMEM)],
        limit=8,
    )[0]


def step_kernel(kept_ref, cross_ref, front_ref, back_ref, out_ref):
    for start, more_ref in ((0, front_ref), (FRONT, back_ref)):
        rows = pl.ds(start, more_ref.shape[0])
        out_ref[rows, :] = (
            kept_ref[rows, :] + cross_ref[rows, :].astype(F32) + more_ref[...].astype(F32)
        ).astype(BF)


def step_of(kept, cross, front, back):
    return call(
        step_kernel,
        "step",
        [(a, IN_VMEM) for a in (kept, cross, front, back)],
        [(plain(*kept.shape, dtype=BF), IN_VMEM)],
        limit=12,
    )[0]


def in_middle(numbers_ref):
    line = line_at(numbers_ref)
    return jnp.logical_or(line == 1, line == 2)


def turn_kernel(numbers_ref, kept_ref, cross_ref, early_ref, inner_ref, middle_ref, near_out, middle_out):
    middle = in_middle(numbers_ref)

    @pl.when(middle)
    def _():
        near_out[...] = (early_ref[...] + middle_ref[...].astype(F32)).astype(BF)
        middle_out[...] = (kept_ref[...] + cross_ref[...].astype(F32) + inner_ref[...].astype(F32)).astype(BF)

    @pl.when(jnp.logical_not(middle))
    def _():
        near_out[...] = (kept_ref[...] + cross_ref[...].astype(F32)).astype(BF)
        middle_out[...] = near_out[...]


def turn_of(numbers, kept, cross, early, inner, middle):
    return call(
        turn_kernel,
        "turn",
        [(numbers, IN_SMEM)] + [(a, IN_VMEM) for a in (kept, cross, early, inner, middle)],
        [(plain(*inner.shape, dtype=BF), IN_VMEM)] * 2,
        limit=15,
    )


def sums_kernel(
    kept_ref, cross_ref, up_ref, down_ref, target_ref, side_ref, dens_ref,
    total_ref, low_ref, kinds_ref, gene_ref, spot_ref,
):
    total = (
        kept_ref[...] + cross_ref[...].astype(F32) + up_ref[...].astype(F32) + down_ref[...].astype(F32)
    )
    pred = total[:GROUP]
    total_ref[...] = pred
    kinds_ref[...] = total[GROUP:].astype(BF)
    low_ref[...] = pred.astype(BF)
    dot = pred * target_ref[...].astype(F32)
    square = pred * pred
    side = side_ref[...]
    spot_ref[0:1, :] = jnp.sum(dot, axis=0, keepdims=True)
    spot_ref[1:2, :] = jnp.sum(square, axis=0, keepdims=True)
    spot_ref[2:3, :] = dens_ref[...]
    sums = [
        jnp.sum(dot * (1.0 - side), axis=1, keepdims=True),
        jnp.sum(dot * side, axis=1, keepdims=True),
        jnp.sum(square * (1.0 - side), axis=1, keepdims=True),
        jnp.sum(square * side, axis=1, keepdims=True),
    ]
    lane = lax.broadcasted_iota(jnp.int32, (GROUP, LANES), 1)
    packed = jnp.zeros((GROUP, LANES), F32)
    for place, column in enumerate(sums):
        packed = jnp.where(lane == place, column, packed)
    gene_ref[...] = packed.T[:4]


def sums_of(kept, *inputs):
    rows, width = kept.shape
    return call(
        sums_kernel,
        "sums",
        [(a, IN_VMEM) for a in (kept, *inputs)],
        [(VMEM((GROUP, width), F32), IN_VMEM), (plain(GROUP, width, dtype=BF), IN_VMEM)]
        + [(plain(KINDS, width, dtype=BF), IN_VMEM)]
        + [(plain(4, GROUP), IN_VMEM), (plain(3, width), IN_VMEM)],
        limit=16,
    )


def grads_kernel(
    scale, slots, total_ref, target_ref, side_ref, density_ref, gene_ref, gene_more_ref, early_ref, spot_ref, spot_target_ref,
    more0_ref, more1_ref, more2_ref, out_ref, dens_ref, cross_ref, loss_ref
):
    side = side_ref[...]
    other = 1.0 - side
    spot = spot_ref[...] + more0_ref[...] + more1_ref[...] + more2_ref[...]
    inv_spot_pred = lax.rsqrt(spot[1:2])
    inv_spot_target = lax.rsqrt(spot_target_ref[...])
    cosine = spot[0:1] * inv_spot_pred * inv_spot_target
    known = early_ref[2:3, :]
    weight = scale / (other * known[:, 0:1] + side * known[:, 1:2])
    spot_along_target = inv_spot_pred * inv_spot_target * weight
    spot_along_pred = cosine * inv_spot_pred * inv_spot_pred * weight
    gene = gene_ref[...] + gene_more_ref[...]
    inv_gene_pred = lax.rsqrt(gene[2:4])
    inv_gene_target = lax.rsqrt(early_ref[0:2, :])
    gene_cosine = gene[0:2] * inv_gene_pred * inv_gene_target
    along = jnp.concatenate(
        [
            (scale / GENES) * inv_gene_pred * inv_gene_target,
            (scale / GENES) * gene_cosine * inv_gene_pred * inv_gene_pred,
            jnp.zeros((LANES - 4, GROUP), F32),
        ],
        axis=0,
    ).T
    along_target = along[:, 0:1] * other + along[:, 1:2] * side + spot_along_target
    along_pred = along[:, 2:3] * other + along[:, 3:4] * side + spot_along_pred
    out_ref[...] = (total_ref[...] * along_pred - target_ref[...].astype(F32) * along_target).astype(BF)
    dens_pred = spot[2:3] / slots
    dens_ref[...] = dens_pred
    cross = density_ref[...] * jnp.log(dens_pred)
    cross_ref[...] = packed_row([row_sum(value * part) for value in (cross, dens_pred, cosine) for part in (other, side)])
    loss_ref[...] = packed_row([row_sum(gene_cosine[0:1]), row_sum(gene_cosine[1:2])])


def grads_of(scale, slots, total, *inputs):
    rows, width = total.shape
    return call(
        functools.partial(grads_kernel, scale, slots),
        "grads",
        [(a, IN_VMEM) for a in (total, *inputs)],
        [(plain(rows, width, dtype=BF), IN_VMEM), (plain(1, width), IN_VMEM)]
        + [(plain(1, LANES), IN_VMEM)] * 2,
        limit=14,
    )


def density_kernel(scale, slots, early_ref, cross_ref, cross_more_ref, side_ref, density_ref, dens_ref, out_ref, cross_out):
    side = side_ref[...]
    other = 1.0 - side
    known = early_ref[2:3, :]
    cross = cross_ref[...] + cross_more_ref[...]
    cross_out[...] = cross
    inverse = other / cross[:, 2:3] + side / cross[:, 3:4]
    dens_mass = other * known[:, 2:3] + side * known[:, 3:4]
    out_ref[...] = (scale / slots) * (inverse - density_ref[...] / (dens_mass * dens_ref[...]))


def density_of(scale, slots, early, cross, cross_more, side, density, dens):
    return call(
        functools.partial(density_kernel, scale, slots),
        "density",
        [(a, IN_VMEM) for a in (early, cross, cross_more, side, density, dens)],
        [(plain(*side.shape), IN_VMEM), (plain(1, LANES), IN_VMEM)],
    )


def table_kernel(early_ref, cross_ref, loss_ref, loss_more_ref, out_ref):
    known = early_ref[2:3, :LANES]
    cross = cross_ref[...]
    loss = loss_ref[...] + loss_more_ref[...]
    for k in range(2):
        one = lambda row, at: row[:, 2 * at + k : 2 * at + k + 1]
        count, dens_mass, dens_log = one(known, 0), one(known, 1), one(known, 2)
        cross_log, pred_mass, cosine_sum = one(cross, 0), one(cross, 1), one(cross, 2)
        divergence = (dens_log - cross_log) / dens_mass - jnp.log(dens_mass) + jnp.log(pred_mass)
        row = packed_row([loss[:, k : k + 1] / GENES, cosine_sum / count, divergence])
        out_ref[k : k + 1, :] = row[:, :3]


def table_of(early, cross, loss, loss_more):
    return call(
        table_kernel,
        "table",
        [(a, IN_VMEM) for a in (early, cross, loss, loss_more)],
        [(plain(2, 3), IN_VMEM)],
        limit=1,
    )[0]


def choose_kernel(plan, numbers_ref, *refs):
    count = max(max(choices) for choices, _, _, _, _ in plan) + 1
    sources, out_refs, sems = refs[:count], refs[count:-1], refs[-1]
    line = line_at(numbers_ref)
    for place in range(4):

        @pl.when(line == place)
        def _(place=place):
            copies = [
                pltpu.make_async_copy(
                    sources[choices[place]].at[pl.ds(start, rows)], out_refs[out].at[pl.ds(to, rows)], sems.at[n]
                )
                for n, (choices, start, rows, out, to) in enumerate(plan)
            ]
            for copy in copies:
                copy.start()
            for copy in copies:
                copy.wait()


def choose_of(numbers, arrays, outputs, plan):
    width = arrays[0].shape[1]
    return call(
        functools.partial(choose_kernel, plan),
        "choose",
        [(numbers, IN_SMEM)] + [(a, IN_PLACE) for a in arrays],
        [(plain(rows, width, dtype=BF), IN_PLACE) for rows in outputs],
        [pltpu.SemaphoreType.DMA((len(plan),))],
    )


def mine_at(numbers_ref, turn):
    return order_of(line_at(numbers_ref), turn) % 2 == numbers_ref[1] % 2


def keep(numbers_ref, turn, grads, mine_ref, *theirs_refs):
    mine = mine_at(numbers_ref, turn)

    @pl.when(mine)
    def _():
        mine_ref[...] = grads[...]

    @pl.when(jnp.logical_not(mine))
    def _():
        depth = theirs_refs[0].shape[0]
        for n, theirs_ref in enumerate(theirs_refs):
            theirs_ref[...] = grads[pl.ds(n * depth, depth), :].astype(BF)


def update_kernel(start, place, numbers_ref, expr_ref, low_ref, acc_ref, mass_ref, block_ref, *refs):
    acc_out, mass_out, mine_ref, theirs_ref, held, turned, grads, sem = refs[-8:]
    cells = low_ref.shape[0]
    copy = pltpu.make_async_copy(expr_ref.at[:, columns_of(block_at(numbers_ref, place))], held, sem)
    copy.start()
    turned[...] = block_ref[...].T
    copy.wait()
    for at in range(cells // CHUNK):
        part = pl.ds(at * CHUNK, CHUNK)
        expr = held[part, :]
        low = low_ref[part, :]
        more = jnp.dot(expr, block_ref[...], preferred_element_type=F32)
        grad = jnp.dot(low, turned[...], preferred_element_type=F32)
        grads[part, :] = grad
        mass = jnp.sum(expr.astype(F32) * grad, axis=1, keepdims=True)
        if start:
            dens = acc_ref[...]
            acc_out[part, :] = more + dens
            mass = mass + jnp.sum(low.astype(F32) * dens, axis=1, keepdims=True)
        else:
            acc_out[part, :] += more
        for half in range(CHUNK // LANES):
            line = pl.ds(at * (CHUNK // LANES) + half, 1)
            row = to_row(mass[half * LANES : (half + 1) * LANES])
            mass_out[line, :] = row if start else row + mass_ref[line, :]
    keep(numbers_ref, place[0], grads, mine_ref, theirs_ref)


def update_of(numbers, place, block, expression, low, acc, mass, start=False, kept=()):
    cells, width = low.shape
    inputs = [(numbers, IN_SMEM), (pinned(expression, HBM), IN_PLACE)]
    inputs += [(a, IN_VMEM) for a in (low, acc, mass, block, *kept)]
    aliases = {} if start else {3: 0}
    if kept:
        aliases |= {6: 2, 7: 3}
    acc, mass, *kept = call(
        functools.partial(update_kernel, start, place),
        "update",
        inputs,
        [(VMEM((cells, width), F32), IN_VMEM), (plain(*mass.shape), IN_VMEM)]
        + [(VMEM((cells, GROUP), F32), IN_VMEM), (VMEM((cells, GROUP), BF), IN_VMEM)],
        [
            pltpu.VMEM((cells, GROUP), BF),
            pltpu.VMEM((width, GROUP), BF),
            pltpu.VMEM((cells, GROUP), F32),
            pltpu.SemaphoreType.DMA,
        ],
        aliases=aliases,
        limit=6,
    )
    return acc, mass, kept


def both_kernel(places, numbers_ref, expr_ref, low_ref, mass_ref, first_ref, second_ref, *refs):
    mass_out, mine_ref, front_ref, back_ref, held, turned, grads, sems = refs
    cells = low_ref.shape[0]
    copies = [
        pltpu.make_async_copy(
            expr_ref.at[:, columns_of(block_at(numbers_ref, place))], held.at[n], sems.at[n]
        )
        for n, place in enumerate(places)
    ]
    for copy in copies:
        copy.start()
    for n, block_ref in enumerate((first_ref, second_ref)):
        turned[:, n * GROUP : (n + 1) * GROUP] = block_ref[...].T
    for copy in copies:
        copy.wait()
    for at in range(cells // CHUNK):
        part = pl.ds(at * CHUNK, CHUNK)
        grad = jnp.dot(low_ref[part, :], turned[...], preferred_element_type=F32)
        mass = 0.0
        for n in range(2):
            one = grad[:, n * GROUP : (n + 1) * GROUP]
            grads[n, part, :] = one
            mass = mass + jnp.sum(held[n, part, :].astype(F32) * one, axis=1, keepdims=True)
        for half in range(CHUNK // LANES):
            line = pl.ds(at * (CHUNK // LANES) + half, 1)
            mass_out[line, :] = mass_ref[line, :] + to_row(mass[half * LANES : (half + 1) * LANES])
    for n, (turn, _) in enumerate(places):
        keep(numbers_ref, turn, grads.at[n], mine_ref, front_ref, back_ref)


def both_of(numbers, places, blocks, expression, low, mass):
    cells, width = low.shape
    mass, mine, front, back, columns = call(
        functools.partial(both_kernel, places),
        "both",
        [(numbers, IN_SMEM), (pinned(expression, HBM), IN_PLACE)] + [(a, IN_VMEM) for a in (low, mass, *blocks)],
        [(plain(*mass.shape), IN_VMEM), (VMEM((cells, GROUP), F32), IN_VMEM)]
        + [(plain(cells // 2, GROUP, dtype=BF), IN_VMEM)] * 2
        + [(VMEM((2, cells, GROUP), BF), IN_VMEM)],
        [
            pltpu.VMEM((width, 2 * GROUP), BF),
            pltpu.VMEM((2, cells, GROUP), F32),
            pltpu.SemaphoreType.DMA((2,)),
        ],
        limit=10,
    )
    return mass, mine, (front, back), columns


def gather_kernel(columns_ref, acc_ref, first_ref, second_ref, logits_ref, *refs):
    acc_out, *fetched, sems = refs
    cells = acc_ref.shape[0]
    depth = fetched[0].shape[0]
    copies = [
        pltpu.make_async_copy(logits_ref.at[pl.ds(n * depth, depth)], piece, sems.at[n])
        for n, piece in enumerate(fetched)
    ]
    for copy in copies:
        copy.start()
    blocks = (first_ref, second_ref)
    for at in range(cells // CHUNK):
        part = pl.ds(at * CHUNK, CHUNK)
        total = acc_out[part, :]
        for n, block_ref in enumerate(blocks):
            total = total + jnp.dot(columns_ref[n, part, :], block_ref[...], preferred_element_type=F32)
        acc_out[part, :] = total
    for copy in copies:
        copy.wait()


def gather_of(columns, acc, blocks, logits):
    cells, width = acc.shape
    acc, *pieces = call(
        gather_kernel,
        "gather",
        [(a, IN_VMEM) for a in (columns, acc, *blocks)] + [(pinned(logits, HBM), IN_PLACE)],
        [(VMEM((cells, width), F32), IN_VMEM)]
        + [(VMEM((cells // PIECES, width), F32), IN_VMEM)] * PIECES,
        [pltpu.SemaphoreType.DMA((PIECES,))],
        aliases={1: 0},
        limit=5,
    )
    return acc, pieces


def part_kernel(
    place, numbers_ref, expr_ref, low_ref, mass_ref, front_ref, back_ref, *refs
):
    mass_out, mine_ref, theirs_ref, held, block, turned, grads, sem = refs
    cells = low_ref.shape[0]
    copy = pltpu.make_async_copy(expr_ref.at[:, columns_of(block_at(numbers_ref, place))], held, sem)
    copy.start()
    block[:UPPER] = front_ref[...]
    block[UPPER:] = back_ref[...]
    turned[...] = block[...].T
    copy.wait()
    for at in range(cells // CHUNK):
        part = pl.ds(at * CHUNK, CHUNK)
        grad = jnp.dot(low_ref[part, :], turned[...], preferred_element_type=F32)
        grads[part, :] = grad
        mass = jnp.sum(held[part, :].astype(F32) * grad, axis=1, keepdims=True)
        for half in range(CHUNK // LANES):
            line = pl.ds(at * (CHUNK // LANES) + half, 1)
            mass_out[line, :] = mass_ref[line, :] + to_row(mass[half * LANES : (half + 1) * LANES])
    keep(numbers_ref, place[0], grads, mine_ref, theirs_ref)


def part_of(numbers, place, front, back, expression, low, mass):
    cells, width = low.shape
    return call(
        functools.partial(part_kernel, place),
        "part",
        [(numbers, IN_SMEM), (pinned(expression, HBM), IN_PLACE)]
        + [(a, IN_VMEM) for a in (low, mass, front, back)],
        [(plain(*mass.shape), IN_VMEM)]
        + [(VMEM((cells, GROUP), F32), IN_VMEM), (VMEM((cells, GROUP), BF), IN_VMEM)]
        + [(VMEM((cells, GROUP), BF), IN_VMEM), (VMEM((GROUP, width), BF), IN_VMEM)],
        [
            pltpu.VMEM((width, GROUP), BF),
            pltpu.VMEM((cells, GROUP), F32),
            pltpu.SemaphoreType.DMA,
        ],
        limit=7,
    )


def pair_kernel(mine_ref, *refs):
    *near_refs, out_ref = refs
    depth = near_refs[0].shape[0]
    for n, near_ref in enumerate(near_refs):
        rows = pl.ds(n * depth, depth)
        out_ref[rows, :] = (mine_ref[rows, :] + near_ref[...].astype(F32)).astype(BF)
    rows = mine_ref.shape[0]
    out_ref[rows:] = jnp.zeros((PAD, out_ref.shape[1]), BF)


def pair_of(mine, nears):
    return call(
        pair_kernel,
        "pair",
        [(mine, IN_VMEM)] + [(near, IN_VMEM) for near in nears],
        [(plain(mine.shape[0] + PAD, mine.shape[1], dtype=BF), IN_VMEM)],
        limit=5,
    )[0]


def collect_kernel(plan, counts, numbers_ref, *refs):
    out_ref, total, near, far, sems = refs[-5:]
    triples, at = [], 0
    for count in counts:
        triples.append((refs[at], refs[at + 1], refs[at + 2 : at + 2 + count]))
        at += 2 + count
    rows = total.shape[1]
    rung = numbers_ref[0] % 2

    def loads(slot, pair):
        mine_ref, far_ref, near_refs = triples[pair]
        copies = [
            pltpu.make_async_copy(mine_ref, total.at[slot], sems.at[slot, 0]),
            pltpu.make_async_copy(far_ref.at[pl.ds(0, rows)], far.at[slot], sems.at[slot, 1]),
        ]
        depth = rows // len(near_refs)
        for n, near_ref in enumerate(near_refs):
            part = pl.ds(n * depth, depth)
            copies.append(pltpu.make_async_copy(near_ref, near.at[slot, part], sems.at[slot, 3 + n]))
        return copies

    for turn in sorted({turn for (turn, _), _ in plan}):
        entries = [(other, pair) for (at, other), pair in plan if at == turn]

        @pl.when(order_of(line_at(numbers_ref), turn) == numbers_ref[1])
        def _(entries=entries):
            for slot, (_, pair) in enumerate(entries):
                for copy in loads(slot, pair):
                    copy.start()
            stores = []
            for slot, (other, pair) in enumerate(entries):
                for copy in loads(slot, pair):
                    copy.wait()
                total[slot] += near[slot].astype(F32) + far[slot].astype(F32)
                columns = columns_of(1 - rung if other else rung)
                stores.append(pltpu.make_async_copy(total.at[slot], out_ref.at[:, columns], sems.at[slot, 2]))
                stores[-1].start()
            for store in stores:
                store.wait()


def collect_of(numbers, plan, triples, result=None):
    cells = triples[0][0].shape[0]
    depth = max(sum(1 for (at, _), _ in plan if at == turn) for (turn, _), _ in plan)
    inputs = [(numbers, IN_SMEM)]
    inputs += [(a, IN_PLACE) for mine, nears, far in triples for a in (mine, far, *nears)]
    aliases = {}
    if result is not None:
        aliases = {len(inputs): 0}
        inputs.append((result, IN_PLACE))
    return call(
        functools.partial(collect_kernel, plan, [len(nears) for _, nears, _ in triples]),
        "collect",
        inputs,
        [(HBM((cells, 2 * GROUP), F32), IN_PLACE)],
        [
            pltpu.VMEM((depth, cells, GROUP), F32),
            pltpu.VMEM((depth, cells, GROUP), BF),
            pltpu.VMEM((depth, cells, GROUP), BF),
            pltpu.SemaphoreType.DMA((depth, 5)),
        ],
        aliases=aliases,
        limit=1 + 4 * depth,
    )[0]


def plus_kernel(first_ref, second_ref, out_ref):
    out_ref[...] = first_ref[...] + second_ref[...]


def plus(first, second):
    return call(
        plus_kernel,
        "plus",
        [(first, IN_VMEM), (second, IN_VMEM)],
        [(plain(*first.shape), IN_VMEM)],
        limit=1,
    )[0]


def finish_kernel(columns_ref, block_ref, factor_ref, acc_ref, mass_ref, more_ref, *refs):
    *pieces, out_ref, held, sems = refs
    lines = mass_ref.shape[0]
    share = lines // len(pieces)
    depth = held.shape[0]
    copies = []
    for at in range(lines):
        if at >= depth:
            copies[at - depth].wait()
        one = pl.ds(at, 1)
        rows = line_of(at)
        grad = acc_ref[rows, :] + jnp.dot(columns_ref[rows, :], block_ref[...], preferred_element_type=F32)
        logits = pieces[at // share][line_of(at % share), :]
        probs = jnp.exp(logits) * to_column(factor_ref[one, :])
        held[at % depth] = probs * (grad - to_column(mass_ref[one, :] + more_ref[one, :]))
        copies.append(pltpu.make_async_copy(held.at[at % depth], out_ref.at[rows], sems.at[at % depth]))
        copies[-1].start()
    for copy in copies[-depth:]:
        copy.wait()


def finish_of(columns, block, pieces, factor, acc, mass, more):
    rows, width = acc.shape
    depth = 4
    inputs = (columns, block, factor, acc, mass, more, *pieces)
    return call(
        finish_kernel,
        "finish",
        [(a, IN_VMEM) for a in inputs],
        [(HBM((rows, width), F32), IN_PLACE)],
        [pltpu.VMEM((depth, LANES, width), F32), pltpu.SemaphoreType.DMA((depth,))],
        limit=6,
        flops=1024,
    )[0]


def merge_kernel(bit, numbers_ref, mine_ref, theirs_ref, out_ref):
    rows = mine_ref.shape[0]
    own = (numbers_ref[0] // 2**bit) % 2
    for value in range(2):

        @pl.when(own == value)
        def _(value=value):
            out_ref[value * rows : (value + 1) * rows, :] = mine_ref[...]
            out_ref[(1 - value) * rows : (2 - value) * rows, :] = theirs_ref[...]


def merge_of(numbers, bit, mine, theirs):
    rows, width = mine.shape
    return call(
        functools.partial(merge_kernel, bit),
        "merge",
        [(numbers, IN_SMEM), (mine, IN_VMEM), (theirs, IN_VMEM)],
        [(plain(2 * rows, width, dtype=BF), IN_VMEM)],
        limit=2,
    )[0]


def kinds_kernel(numbers_ref, mine_ref, theirs_ref, out_ref, held, sem):
    own = numbers_ref[0] % 2
    for low_bit in range(2):
        for middle in range(2):
            for high in range(2):
                source = (2 * middle + high) * KINDS
                block = (4 * high + 2 * middle + low_bit) * KINDS

                @pl.when(own == low_bit)
                def _(source=source, block=block):
                    held[block : block + KINDS, :] = mine_ref[source : source + KINDS, :].astype(F32) * NTYPE

                @pl.when(own != low_bit)
                def _(source=source, block=block):
                    held[block : block + KINDS, :] = theirs_ref[source : source + KINDS, :].astype(F32) * NTYPE

    copy = pltpu.make_async_copy(held, out_ref, sem)
    copy.start()
    copy.wait()


def kinds_of(numbers, mine, theirs):
    width = mine.shape[1]
    return call(
        kinds_kernel,
        "kinds",
        [(numbers, IN_SMEM), (mine, IN_VMEM), (theirs, IN_VMEM)],
        [(HBM((NTYPE, width), F32), IN_PLACE)],
        [pltpu.VMEM((NTYPE, width), F32), pltpu.SemaphoreType.DMA],
        limit=3,
    )[0]


tied = lax.optimization_barrier


def across(array):
    return lax.ppermute(array, "cells", [(at, at ^ 1) for at in range(8)])


def inward(array):
    return lax.ppermute(array, "cells", [(at, at ^ 2) for at in (0, 1, 6, 7)])


def between(array):
    return lax.ppermute(array, "cells", [(at, at ^ 6) for at in range(2, 6)])


def outward(array):
    return lax.ppermute(array, "cells", [(at ^ 2, at) for at in (0, 1, 6, 7)])


def on_line(array, step):
    return lax.ppermute(array, "cells", [(at, at ^ (2 * step)) for at in range(8)])


def swapped(array, step):
    return lax.ppermute(array, "spots", [(at, at ^ step) for at in range(4)])


def near_of(theirs, turns):
    pairs = [
        (at * 4 + place, at * 4 + (place ^ 1))
        for at in range(8)
        for place in range(4)
        if any(order_of(at // 2, turn) % 2 != place % 2 for turn in turns)
    ]
    return [lax.ppermute(piece, ("cells", "spots"), pairs) for piece in theirs]


def far_of(pair, turns):
    pairs = []
    for at in range(8):
        for owner in (order_of(at // 2, turn) for turn in turns):
            pairs.append((at * 4 + (owner ^ 2), at * 4 + owner))
    return lax.ppermute(pair, ("cells", "spots"), pairs)


def ladder(logits, expression, target, density, assignment, labels, counts):
    cells, width = logits.shape
    slots = float(cells * lax.axis_size("cells"))
    scale = float(cells * lax.axis_size("cells") * width * lax.axis_size("spots"))
    numbers = jnp.stack([lax.axis_index("cells"), lax.axis_index("spots")]).astype(jnp.int32)
    logits, numbers = tied((logits, numbers))
    side = (assignment == 1).astype(F32)[None, :]
    density = density[None, :]
    labels = labels[None, :]

    raised, mass = mass_of(logits)
    left_a = left_of(numbers, ((3, 1), (3, 0)), expression, labels)
    mass_near = mass + swapped(mass, 1)
    mass_near, left_a = tied((mass_near, left_a))
    mass_far = swapped(mass_near, 2)
    left_b = left_of(numbers, ((2, 1), (2, 0)), expression, labels)
    mass_far, left_b = tied((mass_far, left_b))
    low, dens_part, factor, front, back = first_of(counts, raised, mass_near, mass_far, left_a)

    front = across(front)
    back = on_line(back, 1)
    (kept3,) = blocks_of(left_a, low, (1,), F32)
    (send2,) = blocks_of(left_b, low, (0,), F32)
    left_c = left_of(numbers, ((1, 1), (1, 0), (0, 1), (0, 0)), expression, labels)
    front, back, kept3, send2, left_c = tied((front, back, kept3, send2, left_c))
    send2 = join_of(numbers, send2, back, (1, 2))
    cross2 = across(send2)
    front, send2 = tied((front, send2))
    half3, half3_f, half3_b = half_of(kept3, front)
    more_f = inward(half3_f)
    more_b = inward(half3_b)
    (kept2,) = blocks_of(left_b, low, (1,), F32)
    (send1,) = blocks_of(left_c, low, (0,), BF)
    cross1 = across(send1)
    (kept1,) = blocks_of(left_c, low, (1,), F32)
    (send0,) = blocks_of(left_c, low, (2,), F32)
    send0 = join_of(numbers, send0, back, (0, 3))
    more_f, more_b, cross2, kept2, kept1, send0 = tied((more_f, more_b, cross2, kept2, kept1, send0))
    more = step_of(kept2, cross2, more_f, more_b)
    inner = inward(more)
    mid = between(more)
    cross0 = across(send0)
    (kept0,) = blocks_of(left_c, low, (3,), F32)
    spot_target, own_target, early = early_of(numbers, target, density, side)
    early = early + swapped(early, 1)
    early = early + swapped(early, 2)
    inner, mid, cross1, early, kept0 = tied((inner, mid, cross1, early, kept0))
    close, mid = turn_of(numbers, kept1, cross1, half3, inner, mid)
    close = on_line(close, 1)
    mid = between(mid)
    close, mid, cross0 = tied((close, mid, cross0))

    total, predicted, kinds, gene, spots = sums_of(kept0, cross0, close, mid, own_target, side, dens_part)
    spots_more = across(spots)
    gene_more = swapped(gene, 1)
    spots_more, gene_more = tied((spots_more, gene_more))
    gene = gene + gene_more
    gene_more = swapped(gene, 2)
    spots = spots + spots_more
    mores = [on_line(spots, step) for step in (3, 2, 1)]
    own, dens, cross, loss = grads_of(
        scale, slots, total, own_target, side, density, gene, gene_more, early, spots, spot_target, *mores
    )

    def update(place, block, acc, mass, **options):
        return update_of(numbers, place, block, expression, low, acc, mass, **options)

    cross0 = across(own)
    close0 = on_line(own, 1)
    mid0 = between(own)
    cross = cross + swapped(cross, 1)
    dens_row, cross = density_of(scale, slots, early, cross, swapped(cross, 2), side, density, dens)
    acc, mass, (mine0, theirs0) = update((0, 0), own, dens_row, mass, start=True)
    near0 = near_of([theirs0], (0,))
    close0, mid0, cross0, mass, near0 = tied((close0, mid0, cross0, mass, near0))

    whole = [((0, 1, 1, 0), 0, GROUP, 0, 0)]
    (block1,) = choose_of(numbers, (close0, mid0), (GROUP,), whole)
    cross1 = across(block1)
    mid1 = between(close0)
    outer1 = outward(mid0)
    far0 = far_of(pair_of(mine0, near0), (0,))
    acc, mass, kept = update((0, 1), cross0, acc, mass)
    acc, mass, (mine1, theirs1) = update((1, 0), block1, acc, mass, kept=kept)
    near1 = near_of([theirs1], (0, 1))
    outer1, mid1, cross1, mass, near1, far0 = tied((outer1, mid1, cross1, mass, near1, far0))

    (block2,) = choose_of(numbers, (outer1, mid1), (GROUP,), whole)
    last = outward(mid1)
    cross2 = across(block2)
    far1 = far_of(pair_of(mine1, near1), (0, 1))
    acc, mass, kept = update((2, 0), block2, acc, mass)
    acc, mass, (mine2, theirs2) = update((1, 1), cross1, acc, mass, kept=kept)
    near2 = near_of([theirs2], (1, 2))
    kinds_more = on_line(kinds, 2)
    last, cross2, mass, near2, far1, kinds_more = tied((last, cross2, mass, near2, far1, kinds_more))

    block3, front, back = choose_of(
        numbers,
        (close0, last, cross0, cross2),
        (GROUP, UPPER, UPPER),
        [
            ((1, 0, 0, 1), 0, GROUP, 0, 0),
            ((1, 0, 0, 1), 0, UPPER, 1, 0),
            ((2, 3, 3, 2), UPPER, UPPER, 2, 0),
        ],
    )
    front = across(front)
    back = on_line(back, 1)
    far2 = far_of(pair_of(mine2, near2), (1, 2))
    mass, mine3, theirs3, columns3 = both_of(numbers, ((2, 1), (3, 0)), (cross2, block3), expression, low, mass)
    near3 = near_of(theirs3, (2, 3))
    pair3 = pair_of(mine3, near3)
    front, back, mass, pair3, far2 = tied((front, back, mass, pair3, far2))

    mass, mine4, theirs4, columns, block = part_of(numbers, (3, 1), front, back, expression, low, mass)
    mass_far = swapped(mass, 2)
    near4 = near_of([theirs4], (3,))
    loss_more = across(loss)
    kinds = merge_of(numbers, 2, kinds, kinds_more)
    kinds_more = on_line(kinds, 1)
    mass_far, loss_more, pair3, columns3, kinds_more = tied((mass_far, loss_more, pair3, columns3, kinds_more))
    far3 = far_of(pair3, (2, 3))
    acc, fetched = gather_of(columns3, acc, (cross2, block3), logits)
    loss = plus(loss, loss_more)
    mass = plus(mass, mass_far)
    mass_near = swapped(mass, 1)
    far4 = far_of(pair_of(mine4, near4), (3,))
    loss_more = on_line(loss, 1)
    kinds = merge_of(numbers, 1, kinds, kinds_more)
    kinds_more = across(kinds)
    mass_near, near4, loss_more, acc = tied((mass_near, near4, loss_more, acc))
    loss = plus(loss, loss_more)
    grad_logits = finish_of(columns, block, fetched, factor, acc, mass, mass_near)
    loss_more = on_line(loss, 2)
    kinds_more, grad_logits, loss_more = tied((kinds_more, grad_logits, loss_more))
    grad_logits, far3 = tied((grad_logits, far3))
    triples = [(mine0, near0, far0), (mine1, near1, far1), (mine2, near2, far2), (mine3, near3, far3)]
    plan = [((turn, 0), turn) for turn in range(4)] + [((turn, 1), turn + 1) for turn in range(3)]
    result = collect_of(numbers, plan, triples)
    table = table_of(early, cross, loss, loss_more)
    result = collect_of(numbers, [((3, 1), 0)], [(mine4, near4, far4)], result)
    types = kinds_of(numbers, kinds, kinds_more)
    return (predicted, grad_logits, result, table, types)


def solution(mesh):
    in_specs = (
        P("cells", "spots"),
        P("cells", None),
        P(None, "spots"),
        P("spots"),
        P("spots"),
        P("cells"),
        P("cells"),
    )
    out_specs = (
        P("cells", "spots"),
        P("cells", "spots"),
        P("cells", "spots"),
        P(),
        P(None, "spots"),
    )
    fits = mesh.shape["cells"] == 8 and mesh.shape["spots"] == 4
    return jax.shard_map(
        ladder if fits else general, mesh=mesh, in_specs=in_specs, out_specs=out_specs, check_vma=False
    )
```

```python
import functools
import math

import jax
import jax.numpy as jnp
import numpy as np
from jax import lax
from jax.experimental import pallas as pl
from jax.experimental.pallas import tpu as pltpu
from jax.sharding import PartitionSpec as P

GENES = 2048
NTYPE = 128
LANES = 128
BF = jnp.bfloat16
F32 = jnp.float32
highest = lax.Precision.HIGHEST


def over_rows(left_side, right_side):
    return lax.dot_general(
        left_side, right_side, (((0,), (0,)), ((), ())), preferred_element_type=F32
    )


def over_columns(left_side, right_side):
    return lax.dot_general(
        left_side, right_side, (((1,), (1,)), ((), ())), preferred_element_type=F32
    )


def general(logits, expression, target, density, assignment, labels, counts):
    row_count = logits.shape[0]
    spot_width = logits.shape[1]
    cell_devices = lax.axis_size("cells")
    slot_total = float(row_count * cell_devices)
    scale = float(row_count * cell_devices * spot_width * lax.axis_size("spots"))
    live = (jnp.arange(row_count, dtype=jnp.int32) < counts[0])[:, None]
    raised = jnp.exp(logits)
    row_mass = lax.psum(jnp.sum(raised, axis=1), "spots")
    probs = jnp.where(live, raised / row_mass[:, None], 0.0)
    probs_low = probs.astype(BF)
    one_hot = (labels[:, None] == jnp.arange(NTYPE, dtype=jnp.int32)[None, :]).astype(BF)
    type_total, dens_total = lax.psum((over_rows(one_hot, probs_low), jnp.sum(probs, axis=0)), "cells")
    gene_rows = GENES // cell_devices
    predicted = lax.psum_scatter(
        over_rows(expression, probs_low), "cells", scatter_dimension=0, tiled=True
    )
    target_full = lax.dynamic_slice_in_dim(
        target, lax.axis_index("cells") * gene_rows, gene_rows, 0
    ).astype(F32)
    spot_dot, spot_pred, spot_target = lax.psum(
        (
            jnp.sum(predicted * target_full, axis=0),
            jnp.sum(predicted * predicted, axis=0),
            jnp.sum(target_full * target_full, axis=0),
        ),
        "cells",
    )
    dens_pred = dens_total / slot_total
    sides = jnp.stack([assignment == 0, assignment == 1]).astype(F32)
    inv_spot_pred = lax.rsqrt(spot_pred)
    inv_spot_target = lax.rsqrt(spot_target)
    spot_cosine = spot_dot * inv_spot_pred * inv_spot_target
    columns = jnp.stack(
        [
            jnp.ones_like(density),
            density,
            density * jnp.log(density),
            density * jnp.log(dens_pred),
            dens_pred,
            spot_cosine,
        ]
    )
    slide_part = jnp.dot(sides, columns.T, precision=highest)
    gene_part = jnp.stack(
        [
            jnp.dot(predicted * target_full, sides.T, precision=highest),
            jnp.dot(predicted * predicted, sides.T, precision=highest),
            jnp.dot(target_full * target_full, sides.T, precision=highest),
        ]
    )
    slide_sums, gene_sums = lax.psum((slide_part, gene_part), "spots")
    spot_count, dens_mass, dens_log, cross_log, pred_mass, cosine_sum = [
        slide_sums[:, at] for at in range(6)
    ]
    inv_gene_pred = lax.rsqrt(gene_sums[1])
    inv_gene_target = lax.rsqrt(gene_sums[2])
    gene_cosine = gene_sums[0] * inv_gene_pred * inv_gene_target
    gene_along_target = jnp.dot(inv_gene_pred * inv_gene_target, sides, precision=highest)
    gene_along_pred = jnp.dot(gene_cosine * inv_gene_pred * inv_gene_pred, sides, precision=highest)
    spot_weight = 1.0 / jnp.dot(spot_count, sides, precision=highest)
    spot_along_target = inv_spot_pred * inv_spot_target * spot_weight
    spot_along_pred = spot_cosine * inv_spot_pred * inv_spot_pred * spot_weight
    grad_dens = scale * (
        jnp.dot(1.0 / pred_mass, sides, precision=highest)
        - density / (jnp.dot(dens_mass, sides, precision=highest) * dens_pred)
    )
    grad_pred = scale * (
        -(target_full * gene_along_target - predicted * gene_along_pred) / GENES
        - (target_full * spot_along_target[None, :] - predicted * spot_along_pred[None, :])
    )
    grad_low = lax.all_gather(grad_pred.astype(BF), "cells", axis=0, tiled=True)
    grad_probs = jnp.dot(expression, grad_low, preferred_element_type=F32)
    grad_expr_part = over_columns(probs_low, grad_low)
    gene_loss = lax.psum(jnp.sum(gene_cosine, axis=0), "cells")
    grad_probs = grad_probs + (grad_dens / slot_total)[None, :]
    row_total = lax.psum(jnp.sum(probs * grad_probs, axis=1), "spots")
    grad_logits = probs * (grad_probs - row_total[:, None])
    grad_expression = lax.psum_scatter(grad_expr_part, "spots", scatter_dimension=1, tiled=True)
    divergence = (dens_log - cross_log) / dens_mass - jnp.log(dens_mass) + jnp.log(pred_mass)
    table = jnp.stack([gene_loss / GENES, cosine_sum / spot_count, divergence], axis=1)
    return (predicted.astype(BF), grad_logits, grad_expression, table, type_total * NTYPE)


VMEM = pltpu.MemorySpace.VMEM
HBM = pltpu.MemorySpace.HBM
IN_VMEM = pl.BlockSpec(memory_space=VMEM)
IN_SMEM = pl.BlockSpec(memory_space=pltpu.MemorySpace.SMEM)
IN_PLACE = pl.BlockSpec(memory_space=pl.ANY)
CHUNK = 2 * LANES
MIB = 1024 * 1024
GROUP = GENES // 8
KINDS = NTYPE // 8
PIECES = 4
PAD = 16

FRONT = 144
ROWS = GROUP + KINDS
BACK = ROWS - FRONT
UPPER = GROUP // 2


def line_at(numbers_ref):
    return numbers_ref[0] // 2


def order_of(line, turn):
    return (line, 1 + line % 2, (line + 2) % 4, 3 - 3 * (line % 2))[turn]


def block_at(numbers_ref, place):
    turn, other = place
    rung = numbers_ref[0] % 2
    return 2 * order_of(line_at(numbers_ref), turn) + (1 - rung if other else rung)


def call(kernel, name, inputs, outputs, scratch=(), aliases=None, limit=8, flops=1024):
    return pl.pallas_call(
        kernel,
        in_specs=[spec for _, spec in inputs],
        out_specs=[spec for _, spec in outputs],
        out_shape=[shape for shape, _ in outputs],
        scratch_shapes=list(scratch),
        input_output_aliases=aliases or {},
        compiler_params=pltpu.CompilerParams(vmem_limit_bytes=limit * MIB),
        cost_estimate=pl.CostEstimate(flops=flops, bytes_accessed=1024, transcendentals=0),
        name=name,
    )(*[array for array, _ in inputs])


def plain(*shape, dtype=F32):
    return jax.ShapeDtypeStruct(shape, dtype)


def pinned(array, space):
    return pltpu.with_memory_space_constraint(array, space)


def to_row(column):
    return jnp.broadcast_to(column, (LANES, LANES)).T[:1]


def to_column(row):
    return jnp.broadcast_to(row, (LANES, LANES)).T[:, :1]


def line_of(at):
    return pl.ds(at * LANES, LANES)


def columns_of(at):
    return pl.ds(pl.multiple_of(at * GROUP, GROUP), GROUP)


def packed_row(values):
    lane = lax.broadcasted_iota(jnp.int32, (1, LANES), 1)
    row = jnp.zeros((1, LANES), F32)
    for at, value in enumerate(values):
        row = jnp.where(lane == at, value, row)
    return row


def row_sum(row):
    return jnp.sum(row, axis=1, keepdims=True)


def mass_kernel(logits_ref, raised_ref, mass_ref, sems):
    lines = mass_ref.shape[0]
    copies = [
        pltpu.make_async_copy(logits_ref.at[line_of(at)], raised_ref.at[line_of(at)], sems.at[at])
        for at in range(lines)
    ]
    for copy in copies:
        copy.start()
    for at, copy in enumerate(copies):
        copy.wait()
        raised = jnp.exp(raised_ref[line_of(at), :])
        raised_ref[line_of(at), :] = raised
        mass_ref[pl.ds(at, 1), :] = to_row(jnp.sum(raised, axis=1, keepdims=True))


def mass_of(logits):
    rows, width = logits.shape
    lines = rows // LANES
    return call(
        mass_kernel,
        "mass",
        [(pinned(logits, HBM), IN_PLACE)],
        [(VMEM((rows, width), F32), IN_VMEM), (plain(lines, LANES), IN_VMEM)],
        [pltpu.SemaphoreType.DMA((lines,))],
    )


def left_kernel(places, numbers_ref, expr_ref, labels_ref, left_ref, held, sems):
    _, _, cells = left_ref.shape

    def copy(n):
        return pltpu.make_async_copy(
            expr_ref.at[:, columns_of(block_at(numbers_ref, places[n]))], held.at[n % 2], sems.at[n % 2]
        )

    copy(0).start()
    for n, place in enumerate(places):
        if n + 1 < len(places):
            copy(n + 1).start()
        kind = lax.broadcasted_iota(jnp.int32, (KINDS, cells), 0) + block_at(numbers_ref, place) * KINDS
        left_ref[n, GROUP:, :] = jnp.where(kind == labels_ref[...], 1.0, 0.0).astype(BF)
        copy(n).wait()
        left_ref[n, :GROUP, :] = held[n % 2].T


def left_of(numbers, places, expression, labels):
    cells = expression.shape[0]
    count = len(places)
    return call(
        functools.partial(left_kernel, places),
        "left",
        [(numbers, IN_SMEM), (pinned(expression, HBM), IN_PLACE), (labels, IN_VMEM)],
        [(VMEM((count, GROUP + KINDS, cells), BF), IN_VMEM)],
        [pltpu.VMEM((2, cells, GROUP), BF), pltpu.SemaphoreType.DMA((2,))],
    )[0]


def first_kernel(counts_ref, raised_ref, near_ref, far_ref, left_ref, low_ref, dens_ref, factor_ref, front_ref, back_ref, total):
    cells = raised_ref.shape[0]
    lines = cells // LANES
    row = lax.broadcasted_iota(jnp.int32, (lines, LANES), 0) * LANES + lax.broadcasted_iota(
        jnp.int32, (lines, LANES), 1
    )
    factor_ref[...] = jnp.where(row < counts_ref[0], 1.0 / (near_ref[...] + far_ref[...]), 0.0)
    mass = 0.0
    for at in range(lines):
        probs = raised_ref[line_of(at), :] * to_column(factor_ref[pl.ds(at, 1), :])
        low_ref[line_of(at), :] = probs.astype(BF)
        mass = mass + jnp.sum(probs, axis=0, keepdims=True)
        if at % 2:
            part = pl.ds((at // 2) * CHUNK, CHUNK)
            more = jnp.dot(left_ref[0, :, part], low_ref[part, :], preferred_element_type=F32)
            if at == 1:
                total[...] = more
            elif at + 1 < lines:
                total[...] += more
            else:
                whole = (total[...] + more).astype(BF)
                front_ref[...] = whole[:FRONT]
                back_ref[...] = whole[FRONT:]
    dens_ref[...] = mass


def first_of(counts, raised, near, far, left):
    cells, width = raised.shape
    rows = left.shape[1]
    return call(
        first_kernel,
        "first",
        [(counts, IN_SMEM)] + [(a, IN_VMEM) for a in (raised, near, far, left)],
        [(VMEM((cells, width), BF), IN_VMEM), (plain(1, width), IN_VMEM)]
        + [(plain(*near.shape), IN_VMEM), (plain(FRONT, width, dtype=BF), IN_VMEM), (plain(BACK, width, dtype=BF), IN_VMEM)],
        [pltpu.VMEM((rows, width), F32)],
    )


def blocks_kernel(which, left_ref, low_ref, *out_refs):
    width = low_ref.shape[1]
    tile = width // 3
    for n, out_ref in zip(which, out_refs):

        def step(at, _, n=n, out_ref=out_ref):
            columns = pl.ds(pl.multiple_of(at * tile, LANES), tile)
            out_ref[:, columns] = jnp.dot(
                left_ref[n], low_ref[:, columns], preferred_element_type=F32
            ).astype(out_ref.dtype)
            return 0

        lax.fori_loop(0, 3, step, 0)


def blocks_of(left, low, which, dtype):
    cells, width = low.shape
    rows = left.shape[1]
    return call(
        functools.partial(blocks_kernel, which),
        "blocks",
        [(left, IN_VMEM), (low, IN_VMEM)],
        [(plain(rows, width, dtype=dtype), IN_VMEM)] * len(which),
        limit=6,
    )


def early_kernel(numbers_ref, target_ref, density_ref, side_ref, spot_ref, own_ref, sums_ref, held, sems):
    genes = target_ref.shape[0]
    count = genes // GROUP

    def copy(n):
        rows = pl.ds(n * GROUP, GROUP)
        return pltpu.make_async_copy(target_ref.at[rows], held.at[n % 2], sems.at[n % 2])

    mine = pltpu.make_async_copy(target_ref.at[columns_of(numbers_ref[0])], own_ref, sems.at[2])
    mine.start()
    copy(0).start()
    spot_ref[...] = jnp.zeros_like(spot_ref)
    for n in range(count):
        if n + 1 < count:
            copy(n + 1).start()
        copy(n).wait()
        target = held[n % 2].astype(F32)
        spot_ref[...] += jnp.sum(target * target, axis=0, keepdims=True)
    mine.wait()
    side = side_ref[...]
    other = 1.0 - side
    density = density_ref[...]
    target = own_ref[...].astype(F32)
    square = target * target
    lane = lax.broadcasted_iota(jnp.int32, (GROUP, LANES), 1)
    columns = jnp.where(
        lane == 0,
        jnp.sum(square * other, axis=1, keepdims=True),
        jnp.where(lane == 1, jnp.sum(square * side, axis=1, keepdims=True), 0.0),
    )
    sums_ref[0:2, :] = columns.T[:2]
    logged = density * jnp.log(density)
    known = packed_row([row_sum(value * part) for value in (1.0, density, logged) for part in (other, side)])
    sums_ref[2:3, :] = jnp.concatenate([known, jnp.zeros_like(known)], axis=1)


def early_of(numbers, target, density, side):
    width = target.shape[1]
    return call(
        early_kernel,
        "early",
        [(numbers, IN_SMEM), (pinned(target, HBM), IN_PLACE), (density, IN_VMEM), (side, IN_VMEM)],
        [(plain(1, width), IN_VMEM), (VMEM((GROUP, width), BF), IN_VMEM), (plain(3, GROUP), IN_VMEM)],
        [pltpu.VMEM((2, GROUP, width), BF), pltpu.SemaphoreType.DMA((3,))],
        limit=16,
    )


def half_kernel(kept_ref, front_ref, half_ref, front_out, back_out):
    half_ref[...] = kept_ref[...]
    half_ref[:FRONT] += front_ref[...].astype(F32)
    front_out[...] = half_ref[:FRONT].astype(BF)
    back_out[...] = half_ref[FRONT:].astype(BF)


def half_of(kept, front):
    width = kept.shape[1]
    return call(
        half_kernel,
        "half",
        [(kept, IN_VMEM), (front, IN_VMEM)],
        [(plain(*kept.shape), IN_VMEM)] + [(plain(rows, width, dtype=BF), IN_VMEM) for rows in (FRONT, BACK)],
        limit=10,
    )


def join_kernel(lines, numbers_ref, part_ref, back_ref, out_ref):
    out_ref[:FRONT] = part_ref[:FRONT].astype(BF)
    line = line_at(numbers_ref)
    here = jnp.logical_or(line == lines[0], line == lines[1])

    @pl.when(here)
    def _():
        out_ref[FRONT:] = (part_ref[FRONT:] + back_ref[...].astype(F32)).astype(BF)

    @pl.when(jnp.logical_not(here))
    def _():
        out_ref[FRONT:] = part_ref[FRONT:].astype(BF)


def join_of(numbers, part, back, lines):
    return call(
        functools.partial(join_kernel, lines),
        "join",
        [(numbers, IN_SMEM), (part, IN_VMEM), (back, IN_VMEM)],
        [(plain(*part.shape, dtype=BF), IN_VMEM)],
        limit=8,
    )[0]


def step_kernel(kept_ref, cross_ref, front_ref, back_ref, out_ref, front_out, back_out):
    for start, more_ref in ((0, front_ref), (FRONT, back_ref)):
        rows = pl.ds(start, more_ref.shape[0])
        out_ref[rows, :] = (
            kept_ref[rows, :] + cross_ref[rows, :].astype(F32) + more_ref[...].astype(F32)
        ).astype(BF)
    front_out[...] = out_ref[:FRONT]
    back_out[...] = out_ref[FRONT:]


def step_of(kept, cross, front, back):
    width = kept.shape[1]
    return call(
        step_kernel,
        "step",
        [(a, IN_VMEM) for a in (kept, cross, front, back)],
        [(plain(rows, width, dtype=BF), IN_VMEM) for rows in (ROWS, FRONT, BACK)],
        limit=12,
    )


def in_middle(numbers_ref):
    line = line_at(numbers_ref)
    return jnp.logical_or(line == 1, line == 2)


def turn_kernel(numbers_ref, kept_ref, cross_ref, early_ref, inner_ref, front_ref, back_ref, near_out, middle_out):
    middle = in_middle(numbers_ref)

    @pl.when(middle)
    def _():
        near_out[:FRONT] = (early_ref[:FRONT] + front_ref[...].astype(F32)).astype(BF)
        near_out[FRONT:] = (early_ref[FRONT:] + back_ref[...].astype(F32)).astype(BF)
        middle_out[...] = (kept_ref[...] + cross_ref[...].astype(F32) + inner_ref[...].astype(F32)).astype(BF)

    @pl.when(jnp.logical_not(middle))
    def _():
        near_out[...] = (kept_ref[...] + cross_ref[...].astype(F32)).astype(BF)
        middle_out[...] = near_out[...]


def turn_of(numbers, kept, cross, early, inner, front, back):
    return call(
        turn_kernel,
        "turn",
        [(numbers, IN_SMEM)] + [(a, IN_VMEM) for a in (kept, cross, early, inner, front, back)],
        [(plain(*inner.shape, dtype=BF), IN_VMEM)] * 2,
        limit=15,
    )


def sums_kernel(
    kept_ref, cross_ref, up_ref, down_ref, target_ref, side_ref, dens_ref,
    total_ref, low_ref, kinds_ref, gene_ref, spot_ref,
):
    total = (
        kept_ref[...] + cross_ref[...].astype(F32) + up_ref[...].astype(F32) + down_ref[...].astype(F32)
    )
    pred = total[:GROUP]
    total_ref[...] = pred
    kinds_ref[...] = total[GROUP:].astype(BF)
    low_ref[...] = pred.astype(BF)
    dot = pred * target_ref[...].astype(F32)
    square = pred * pred
    side = side_ref[...]
    spot_ref[0:1, :] = jnp.sum(dot, axis=0, keepdims=True)
    spot_ref[1:2, :] = jnp.sum(square, axis=0, keepdims=True)
    spot_ref[2:3, :] = dens_ref[...]
    sums = [
        jnp.sum(dot * (1.0 - side), axis=1, keepdims=True),
        jnp.sum(dot * side, axis=1, keepdims=True),
        jnp.sum(square * (1.0 - side), axis=1, keepdims=True),
        jnp.sum(square * side, axis=1, keepdims=True),
    ]
    lane = lax.broadcasted_iota(jnp.int32, (GROUP, LANES), 1)
    packed = jnp.zeros((GROUP, LANES), F32)
    for place, column in enumerate(sums):
        packed = jnp.where(lane == place, column, packed)
    gene_ref[...] = packed.T[:4]


def sums_of(kept, *inputs):
    rows, width = kept.shape
    return call(
        sums_kernel,
        "sums",
        [(a, IN_VMEM) for a in (kept, *inputs)],
        [(VMEM((GROUP, width), F32), IN_VMEM), (plain(GROUP, width, dtype=BF), IN_VMEM)]
        + [(plain(KINDS, width, dtype=BF), IN_VMEM)]
        + [(plain(4, GROUP), IN_VMEM), (plain(3, width), IN_VMEM)],
        limit=16,
    )


def put_sum(ref, start, value):
    high = value.astype(BF).astype(F32)
    middle = (value - high).astype(BF).astype(F32)
    low = (value - high) - middle
    row = lax.broadcasted_iota(jnp.int32, (KINDS, LANES), 0)
    tile = jnp.where(row == 0, high, jnp.where(row == 1, middle, jnp.where(row == 2, low, 0.0)))
    ref[start:, :] = jnp.zeros((KINDS, ref.shape[1]), BF)
    ref[start:, :LANES] = tile.astype(BF)


def get_sum(ref, start):
    tile = ref[start:, :LANES].astype(F32)
    return tile[0:1] + tile[1:2] + tile[2:3]


def grads_kernel(
    scale, slots, total_ref, target_ref, side_ref, density_ref, gene_ref, gene_more_ref, early_ref, spot_ref, spot_target_ref,
    more0_ref, more1_ref, more2_ref, kinds_ref, out_ref, dens_ref, cross_ref, kinds_out
):
    side = side_ref[...]
    other = 1.0 - side
    spot = spot_ref[...] + more0_ref[...] + more1_ref[...] + more2_ref[...]
    inv_spot_pred = lax.rsqrt(spot[1:2])
    inv_spot_target = lax.rsqrt(spot_target_ref[...])
    cosine = spot[0:1] * inv_spot_pred * inv_spot_target
    known = early_ref[2:3, :]
    weight = scale / (other * known[:, 0:1] + side * known[:, 1:2])
    spot_along_target = inv_spot_pred * inv_spot_target * weight
    spot_along_pred = cosine * inv_spot_pred * inv_spot_pred * weight
    gene = gene_ref[...] + gene_more_ref[...]
    inv_gene_pred = lax.rsqrt(gene[2:4])
    inv_gene_target = lax.rsqrt(early_ref[0:2, :])
    gene_cosine = gene[0:2] * inv_gene_pred * inv_gene_target
    along = jnp.concatenate(
        [
            (scale / GENES) * inv_gene_pred * inv_gene_target,
            (scale / GENES) * gene_cosine * inv_gene_pred * inv_gene_pred,
            jnp.zeros((LANES - 4, GROUP), F32),
        ],
        axis=0,
    ).T
    along_target = along[:, 0:1] * other + along[:, 1:2] * side + spot_along_target
    along_pred = along[:, 2:3] * other + along[:, 3:4] * side + spot_along_pred
    out_ref[...] = (total_ref[...] * along_pred - target_ref[...].astype(F32) * along_target).astype(BF)
    dens_pred = spot[2:3] / slots
    dens_ref[...] = dens_pred
    cross = density_ref[...] * jnp.log(dens_pred)
    cross_ref[...] = packed_row([row_sum(value * part) for value in (cross, dens_pred, cosine) for part in (other, side)])
    kinds_out[:KINDS] = kinds_ref[...]
    put_sum(kinds_out, KINDS, packed_row([row_sum(gene_cosine[0:1]), row_sum(gene_cosine[1:2])]))


def grads_of(scale, slots, total, *inputs):
    rows, width = total.shape
    return call(
        functools.partial(grads_kernel, scale, slots),
        "grads",
        [(a, IN_VMEM) for a in (total, *inputs)],
        [(plain(rows, width, dtype=BF), IN_VMEM), (plain(1, width), IN_VMEM)]
        + [(plain(1, LANES), IN_VMEM), (plain(2 * KINDS, width, dtype=BF), IN_VMEM)],
        limit=14,
    )


def density_kernel(scale, slots, early_ref, cross_ref, cross_more_ref, side_ref, density_ref, dens_ref, out_ref, cross_out):
    side = side_ref[...]
    other = 1.0 - side
    known = early_ref[2:3, :]
    cross = cross_ref[...] + cross_more_ref[...]
    cross_out[...] = cross
    inverse = other / cross[:, 2:3] + side / cross[:, 3:4]
    dens_mass = other * known[:, 2:3] + side * known[:, 3:4]
    out_ref[...] = (scale / slots) * (inverse - density_ref[...] / (dens_mass * dens_ref[...]))


def density_of(scale, slots, early, cross, cross_more, side, density, dens):
    return call(
        functools.partial(density_kernel, scale, slots),
        "density",
        [(a, IN_VMEM) for a in (early, cross, cross_more, side, density, dens)],
        [(plain(*side.shape), IN_VMEM), (plain(1, LANES), IN_VMEM)],
    )


def choose_kernel(plan, numbers_ref, *refs):
    count = max(max(choices) for choices, _, _, _, _ in plan) + 1
    sources, out_refs, sems = refs[:count], refs[count:-1], refs[-1]
    line = line_at(numbers_ref)
    for place in range(4):

        @pl.when(line == place)
        def _(place=place):
            copies = [
                pltpu.make_async_copy(
                    sources[choices[place]].at[pl.ds(start, rows)], out_refs[out].at[pl.ds(to, rows)], sems.at[n]
                )
                for n, (choices, start, rows, out, to) in enumerate(plan)
            ]
            for copy in copies:
                copy.start()
            for copy in copies:
                copy.wait()


def choose_of(numbers, arrays, outputs, plan):
    width = arrays[0].shape[1]
    return call(
        functools.partial(choose_kernel, plan),
        "choose",
        [(numbers, IN_SMEM)] + [(a, IN_PLACE) for a in arrays],
        [(plain(rows, width, dtype=BF), IN_PLACE) for rows in outputs],
        [pltpu.SemaphoreType.DMA((len(plan),))],
    )


def mine_at(numbers_ref, turn):
    return order_of(line_at(numbers_ref), turn) % 2 == numbers_ref[1] % 2


def keep(numbers_ref, turn, grads, mine_ref, *theirs_refs):
    mine = mine_at(numbers_ref, turn)

    @pl.when(mine)
    def _():
        mine_ref[...] = grads[...]

    @pl.when(jnp.logical_not(mine))
    def _():
        depth = theirs_refs[0].shape[0]
        for n, theirs_ref in enumerate(theirs_refs):
            theirs_ref[...] = grads[pl.ds(n * depth, depth), :].astype(BF)


def update_kernel(start, place, numbers_ref, expr_ref, low_ref, acc_ref, mass_ref, block_ref, *refs):
    acc_out, mass_out, mine_ref, theirs_ref, held, turned, grads, sem = refs[-8:]
    cells = low_ref.shape[0]
    copy = pltpu.make_async_copy(expr_ref.at[:, columns_of(block_at(numbers_ref, place))], held, sem)
    copy.start()
    turned[...] = block_ref[...].T
    copy.wait()
    for at in range(cells // CHUNK):
        part = pl.ds(at * CHUNK, CHUNK)
        expr = held[part, :]
        low = low_ref[part, :]
        more = jnp.dot(expr, block_ref[...], preferred_element_type=F32)
        grad = jnp.dot(low, turned[...], preferred_element_type=F32)
        grads[part, :] = grad
        mass = jnp.sum(expr.astype(F32) * grad, axis=1, keepdims=True)
        if start:
            dens = acc_ref[...]
            acc_out[part, :] = more + dens
            mass = mass + jnp.sum(low.astype(F32) * dens, axis=1, keepdims=True)
        else:
            acc_out[part, :] += more
        for half in range(CHUNK // LANES):
            line = pl.ds(at * (CHUNK // LANES) + half, 1)
            row = to_row(mass[half * LANES : (half + 1) * LANES])
            mass_out[line, :] = row if start else row + mass_ref[line, :]
    keep(numbers_ref, place[0], grads, mine_ref, theirs_ref)


def update_of(numbers, place, block, expression, low, acc, mass, start=False, kept=()):
    cells, width = low.shape
    inputs = [(numbers, IN_SMEM), (pinned(expression, HBM), IN_PLACE)]
    inputs += [(a, IN_VMEM) for a in (low, acc, mass, block, *kept)]
    aliases = {} if start else {3: 0}
    if kept:
        aliases |= {6: 2, 7: 3}
    acc, mass, *kept = call(
        functools.partial(update_kernel, start, place),
        "update",
        inputs,
        [(VMEM((cells, width), F32), IN_VMEM), (plain(*mass.shape), IN_VMEM)]
        + [(VMEM((cells, GROUP), F32), IN_VMEM), (VMEM((cells, GROUP), BF), IN_VMEM)],
        [
            pltpu.VMEM((cells, GROUP), BF),
            pltpu.VMEM((width, GROUP), BF),
            pltpu.VMEM((cells, GROUP), F32),
            pltpu.SemaphoreType.DMA,
        ],
        aliases=aliases,
        limit=6,
    )
    return acc, mass, kept


def both_kernel(places, numbers_ref, expr_ref, low_ref, mass_ref, first_ref, second_ref, *refs):
    mass_out, mine_ref, front_ref, back_ref, held, turned, grads, sems = refs
    cells = low_ref.shape[0]
    copies = [
        pltpu.make_async_copy(
            expr_ref.at[:, columns_of(block_at(numbers_ref, place))], held.at[n], sems.at[n]
        )
        for n, place in enumerate(places)
    ]
    for copy in copies:
        copy.start()
    for n, block_ref in enumerate((first_ref, second_ref)):
        turned[:, n * GROUP : (n + 1) * GROUP] = block_ref[...].T
    for copy in copies:
        copy.wait()
    for at in range(cells // CHUNK):
        part = pl.ds(at * CHUNK, CHUNK)
        grad = jnp.dot(low_ref[part, :], turned[...], preferred_element_type=F32)
        mass = 0.0
        for n in range(2):
            one = grad[:, n * GROUP : (n + 1) * GROUP]
            grads[n, part, :] = one
            mass = mass + jnp.sum(held[n, part, :].astype(F32) * one, axis=1, keepdims=True)
        for half in range(CHUNK // LANES):
            line = pl.ds(at * (CHUNK // LANES) + half, 1)
            mass_out[line, :] = mass_ref[line, :] + to_row(mass[half * LANES : (half + 1) * LANES])
    for n, (turn, _) in enumerate(places):
        keep(numbers_ref, turn, grads.at[n], mine_ref, front_ref, back_ref)


def both_of(numbers, places, blocks, expression, low, mass):
    cells, width = low.shape
    mass, mine, front, back, columns = call(
        functools.partial(both_kernel, places),
        "both",
        [(numbers, IN_SMEM), (pinned(expression, HBM), IN_PLACE)] + [(a, IN_VMEM) for a in (low, mass, *blocks)],
        [(plain(*mass.shape), IN_VMEM), (VMEM((cells, GROUP), F32), IN_VMEM)]
        + [(plain(cells // 2, GROUP, dtype=BF), IN_VMEM)] * 2
        + [(VMEM((2, cells, GROUP), BF), IN_VMEM)],
        [
            pltpu.VMEM((width, 2 * GROUP), BF),
            pltpu.VMEM((2, cells, GROUP), F32),
            pltpu.SemaphoreType.DMA((2,)),
        ],
        limit=10,
    )
    return mass, mine, (front, back), columns


def gather_kernel(columns_ref, acc_ref, first_ref, second_ref, logits_ref, *refs):
    acc_out, *fetched, sems = refs
    cells = acc_ref.shape[0]
    depth = fetched[0].shape[0]
    copies = [
        pltpu.make_async_copy(logits_ref.at[pl.ds(n * depth, depth)], piece, sems.at[n])
        for n, piece in enumerate(fetched)
    ]
    for copy in copies:
        copy.start()
    blocks = (first_ref, second_ref)
    for at in range(cells // CHUNK):
        part = pl.ds(at * CHUNK, CHUNK)
        total = acc_out[part, :]
        for n, block_ref in enumerate(blocks):
            total = total + jnp.dot(columns_ref[n, part, :], block_ref[...], preferred_element_type=F32)
        acc_out[part, :] = total
    for copy in copies:
        copy.wait()


def gather_of(columns, acc, blocks, logits):
    cells, width = acc.shape
    acc, *pieces = call(
        gather_kernel,
        "gather",
        [(a, IN_VMEM) for a in (columns, acc, *blocks)] + [(pinned(logits, HBM), IN_PLACE)],
        [(VMEM((cells, width), F32), IN_VMEM)]
        + [(VMEM((cells // PIECES, width), F32), IN_VMEM)] * PIECES,
        [pltpu.SemaphoreType.DMA((PIECES,))],
        aliases={1: 0},
        limit=5,
    )
    return acc, pieces


def part_kernel(
    place, numbers_ref, expr_ref, low_ref, mass_ref, front_ref, back_ref, *refs
):
    mass_out, mine_ref, theirs_ref, held, block, turned, grads, sem = refs
    cells = low_ref.shape[0]
    copy = pltpu.make_async_copy(expr_ref.at[:, columns_of(block_at(numbers_ref, place))], held, sem)
    copy.start()
    block[:UPPER] = front_ref[...]
    block[UPPER:] = back_ref[:UPPER]
    turned[...] = block[...].T
    copy.wait()
    for at in range(cells // CHUNK):
        part = pl.ds(at * CHUNK, CHUNK)
        grad = jnp.dot(low_ref[part, :], turned[...], preferred_element_type=F32)
        grads[part, :] = grad
        mass = jnp.sum(held[part, :].astype(F32) * grad, axis=1, keepdims=True)
        for half in range(CHUNK // LANES):
            line = pl.ds(at * (CHUNK // LANES) + half, 1)
            mass_out[line, :] = mass_ref[line, :] + to_row(mass[half * LANES : (half + 1) * LANES])
    keep(numbers_ref, place[0], grads, mine_ref, theirs_ref)


def part_of(numbers, place, front, back, expression, low, mass):
    cells, width = low.shape
    return call(
        functools.partial(part_kernel, place),
        "part",
        [(numbers, IN_SMEM), (pinned(expression, HBM), IN_PLACE)]
        + [(a, IN_VMEM) for a in (low, mass, front, back)],
        [(plain(*mass.shape), IN_VMEM)]
        + [(VMEM((cells, GROUP), F32), IN_VMEM), (VMEM((cells, GROUP), BF), IN_VMEM)]
        + [(VMEM((cells, GROUP), BF), IN_VMEM), (VMEM((GROUP, width), BF), IN_VMEM)],
        [
            pltpu.VMEM((width, GROUP), BF),
            pltpu.VMEM((cells, GROUP), F32),
            pltpu.SemaphoreType.DMA,
        ],
        limit=7,
    )


def pair_kernel(mine_ref, *refs):
    *near_refs, out_ref = refs
    depth = near_refs[0].shape[0]
    for n, near_ref in enumerate(near_refs):
        rows = pl.ds(n * depth, depth)
        out_ref[rows, :] = (mine_ref[rows, :] + near_ref[...].astype(F32)).astype(BF)
    rows = mine_ref.shape[0]
    out_ref[rows:] = jnp.zeros((PAD, out_ref.shape[1]), BF)


def pair_of(mine, nears):
    return call(
        pair_kernel,
        "pair",
        [(mine, IN_VMEM)] + [(near, IN_VMEM) for near in nears],
        [(plain(mine.shape[0] + PAD, mine.shape[1], dtype=BF), IN_VMEM)],
        limit=5,
    )[0]


def collect_kernel(plan, counts, numbers_ref, *refs):
    out_ref, total, near, far, sems = refs[-5:]
    triples, at = [], 0
    for count in counts:
        triples.append((refs[at], refs[at + 1], refs[at + 2 : at + 2 + count]))
        at += 2 + count
    rows = total.shape[1]
    rung = numbers_ref[0] % 2

    def loads(slot, pair):
        mine_ref, far_ref, near_refs = triples[pair]
        copies = [
            pltpu.make_async_copy(mine_ref, total.at[slot], sems.at[slot, 0]),
            pltpu.make_async_copy(far_ref.at[pl.ds(0, rows)], far.at[slot], sems.at[slot, 1]),
        ]
        depth = rows // len(near_refs)
        for n, near_ref in enumerate(near_refs):
            part = pl.ds(n * depth, depth)
            copies.append(pltpu.make_async_copy(near_ref, near.at[slot, part], sems.at[slot, 3 + n]))
        return copies

    for turn in sorted({turn for (turn, _), _ in plan}):
        entries = [(other, pair) for (at, other), pair in plan if at == turn]

        @pl.when(order_of(line_at(numbers_ref), turn) == numbers_ref[1])
        def _(entries=entries):
            for slot, (_, pair) in enumerate(entries):
                for copy in loads(slot, pair):
                    copy.start()
            stores = []
            for slot, (other, pair) in enumerate(entries):
                for copy in loads(slot, pair):
                    copy.wait()
                total[slot] += near[slot].astype(F32) + far[slot].astype(F32)
                columns = columns_of(1 - rung if other else rung)
                stores.append(pltpu.make_async_copy(total.at[slot], out_ref.at[:, columns], sems.at[slot, 2]))
                stores[-1].start()
            for store in stores:
                store.wait()


def collect_of(numbers, plan, triples, result=None):
    cells = triples[0][0].shape[0]
    depth = max(sum(1 for (at, _), _ in plan if at == turn) for (turn, _), _ in plan)
    inputs = [(numbers, IN_SMEM)]
    inputs += [(a, IN_PLACE) for mine, nears, far in triples for a in (mine, far, *nears)]
    aliases = {}
    if result is not None:
        aliases = {len(inputs): 0}
        inputs.append((result, IN_PLACE))
    return call(
        functools.partial(collect_kernel, plan, [len(nears) for _, nears, _ in triples]),
        "collect",
        inputs,
        [(HBM((cells, 2 * GROUP), F32), IN_PLACE)],
        [
            pltpu.VMEM((depth, cells, GROUP), F32),
            pltpu.VMEM((depth, cells, GROUP), BF),
            pltpu.VMEM((depth, cells, GROUP), BF),
            pltpu.SemaphoreType.DMA((depth, 5)),
        ],
        aliases=aliases,
        limit=1 + 4 * depth,
    )[0]


def plus_kernel(first_ref, second_ref, out_ref):
    out_ref[...] = first_ref[...] + second_ref[...]


def plus(first, second):
    return call(
        plus_kernel,
        "plus",
        [(first, IN_VMEM), (second, IN_VMEM)],
        [(plain(*first.shape), IN_VMEM)],
        limit=1,
    )[0]


def finish_kernel(columns_ref, block_ref, factor_ref, acc_ref, mass_ref, more_ref, *refs):
    *pieces, out_ref, held, sems = refs
    lines = mass_ref.shape[0]
    share = lines // len(pieces)
    depth = held.shape[0]
    copies = []
    for at in range(lines):
        if at >= depth:
            copies[at - depth].wait()
        one = pl.ds(at, 1)
        rows = line_of(at)
        grad = acc_ref[rows, :] + jnp.dot(columns_ref[rows, :], block_ref[...], preferred_element_type=F32)
        logits = pieces[at // share][line_of(at % share), :]
        probs = jnp.exp(logits) * to_column(factor_ref[one, :])
        held[at % depth] = probs * (grad - to_column(mass_ref[one, :] + more_ref[one, :]))
        copies.append(pltpu.make_async_copy(held.at[at % depth], out_ref.at[rows], sems.at[at % depth]))
        copies[-1].start()
    for copy in copies[-depth:]:
        copy.wait()


def finish_of(columns, block, pieces, factor, acc, mass, more):
    rows, width = acc.shape
    depth = 4
    inputs = (columns, block, factor, acc, mass, more, *pieces)
    return call(
        finish_kernel,
        "finish",
        [(a, IN_VMEM) for a in inputs],
        [(HBM((rows, width), F32), IN_PLACE)],
        [pltpu.VMEM((depth, LANES, width), F32), pltpu.SemaphoreType.DMA((depth,))],
        limit=6,
        flops=1024,
    )[0]


def merge_kernel(bit, numbers_ref, mine_ref, theirs_ref, out_ref):
    rows = mine_ref.shape[0] - KINDS
    skip = theirs_ref.shape[0] - mine_ref.shape[0]
    own = (numbers_ref[0] // 2**bit) % 2
    for value in range(2):

        @pl.when(own == value)
        def _(value=value):
            out_ref[value * rows : (value + 1) * rows, :] = mine_ref[:rows]
            out_ref[(1 - value) * rows : (2 - value) * rows, :] = theirs_ref[skip : skip + rows]

    put_sum(out_ref, 2 * rows, get_sum(mine_ref, rows) + get_sum(theirs_ref, skip + rows))


def merge_of(numbers, bit, mine, theirs):
    rows, width = mine.shape
    return call(
        functools.partial(merge_kernel, bit),
        "merge",
        [(numbers, IN_SMEM), (mine, IN_VMEM), (theirs, IN_VMEM)],
        [(plain(2 * rows - KINDS, width, dtype=BF), IN_VMEM)],
        limit=2,
    )[0]


def kinds_kernel(numbers_ref, mine_ref, theirs_ref, early_ref, cross_ref, out_ref, table_ref, held, sem):
    own = numbers_ref[0] % 2
    for low_bit in range(2):
        for middle in range(2):
            for high in range(2):
                source = (2 * high + middle) * KINDS
                block = (4 * high + 2 * middle + low_bit) * KINDS

                @pl.when(own == low_bit)
                def _(source=source, block=block):
                    held[block : block + KINDS, :] = mine_ref[source : source + KINDS, :].astype(F32) * NTYPE

                @pl.when(own != low_bit)
                def _(source=source, block=block):
                    held[block : block + KINDS, :] = theirs_ref[source : source + KINDS, :].astype(F32) * NTYPE

    copy = pltpu.make_async_copy(held, out_ref, sem)
    copy.start()
    loss = get_sum(mine_ref, 4 * KINDS) + get_sum(theirs_ref, 4 * KINDS)
    known = early_ref[2:3, :LANES]
    cross = cross_ref[...]
    for k in range(2):
        one = lambda row, at: row[:, 2 * at + k : 2 * at + k + 1]
        count, dens_mass, dens_log = one(known, 0), one(known, 1), one(known, 2)
        cross_log, pred_mass, cosine_sum = one(cross, 0), one(cross, 1), one(cross, 2)
        divergence = (dens_log - cross_log) / dens_mass - jnp.log(dens_mass) + jnp.log(pred_mass)
        row = packed_row([loss[:, k : k + 1] / GENES, cosine_sum / count, divergence])
        table_ref[k : k + 1, :] = row[:, :3]
    copy.wait()


def kinds_of(numbers, mine, theirs, early, cross):
    width = mine.shape[1]
    return call(
        kinds_kernel,
        "kinds",
        [(numbers, IN_SMEM)] + [(a, IN_VMEM) for a in (mine, theirs, early, cross)],
        [(HBM((NTYPE, width), F32), IN_PLACE), (plain(2, 3), IN_VMEM)],
        [pltpu.VMEM((NTYPE, width), F32), pltpu.SemaphoreType.DMA],
        limit=3,
    )


tied = lax.optimization_barrier


def across(array):
    return lax.ppermute(array, "cells", [(at, at ^ 1) for at in range(8)])


def inward(array):
    return lax.ppermute(array, "cells", [(at, at ^ 2) for at in (0, 1, 6, 7)])


def between(array):
    return lax.ppermute(array, "cells", [(at, at ^ 6) for at in range(2, 6)])


def outward(array):
    return lax.ppermute(array, "cells", [(at ^ 2, at) for at in (0, 1, 6, 7)])


def on_line(array, step):
    return lax.ppermute(array, "cells", [(at, at ^ (2 * step)) for at in range(8)])


def swapped(array, step):
    return lax.ppermute(array, "spots", [(at, at ^ step) for at in range(4)])


def near_of(theirs, turns):
    pairs = [
        (at * 4 + place, at * 4 + (place ^ 1))
        for at in range(8)
        for place in range(4)
        if any(order_of(at // 2, turn) % 2 != place % 2 for turn in turns)
    ]
    return [lax.ppermute(piece, ("cells", "spots"), pairs) for piece in theirs]


def far_of(pair, turns):
    pairs = []
    for at in range(8):
        for owner in (order_of(at // 2, turn) for turn in turns):
            pairs.append((at * 4 + (owner ^ 2), at * 4 + owner))
    return lax.ppermute(pair, ("cells", "spots"), pairs)


def ladder(logits, expression, target, density, assignment, labels, counts):
    cells, width = logits.shape
    slots = float(cells * lax.axis_size("cells"))
    scale = float(cells * lax.axis_size("cells") * width * lax.axis_size("spots"))
    numbers = jnp.stack([lax.axis_index("cells"), lax.axis_index("spots")]).astype(jnp.int32)
    logits, numbers = tied((logits, numbers))
    side = (assignment == 1).astype(F32)[None, :]
    density = density[None, :]
    labels = labels[None, :]

    raised, mass = mass_of(logits)
    left_a = left_of(numbers, ((3, 1), (3, 0)), expression, labels)
    mass_near = mass + swapped(mass, 1)
    mass_near, left_a = tied((mass_near, left_a))
    mass_far = swapped(mass_near, 2)
    left_b = left_of(numbers, ((2, 1), (2, 0)), expression, labels)
    mass_far, left_b = tied((mass_far, left_b))
    low, dens_part, factor, front, back = first_of(counts, raised, mass_near, mass_far, left_a)

    front = across(front)
    back = on_line(back, 1)
    (kept3,) = blocks_of(left_a, low, (1,), F32)
    (send2,) = blocks_of(left_b, low, (0,), F32)
    left_c = left_of(numbers, ((1, 1), (1, 0), (0, 1), (0, 0)), expression, labels)
    front, back, kept3, send2, left_c = tied((front, back, kept3, send2, left_c))
    send2 = join_of(numbers, send2, back, (1, 2))
    cross2 = across(send2)
    front, send2 = tied((front, send2))
    half3, half3_f, half3_b = half_of(kept3, front)
    more_f = inward(half3_f)
    more_b = inward(half3_b)
    (kept2,) = blocks_of(left_b, low, (1,), F32)
    (send1,) = blocks_of(left_c, low, (0,), BF)
    cross1 = across(send1)
    (kept1,) = blocks_of(left_c, low, (1,), F32)
    (send0,) = blocks_of(left_c, low, (2,), F32)
    send0 = join_of(numbers, send0, back, (0, 3))
    more_f, more_b, cross2, kept2, kept1, send0 = tied((more_f, more_b, cross2, kept2, kept1, send0))
    more, more_f, more_b = step_of(kept2, cross2, more_f, more_b)
    inner = inward(more)
    mid_f = between(more_f)
    mid_b = between(more_b)
    cross0 = across(send0)
    (kept0,) = blocks_of(left_c, low, (3,), F32)
    spot_target, own_target, early = early_of(numbers, target, density, side)
    early = early + swapped(early, 1)
    early = early + swapped(early, 2)
    inner, mid_f, mid_b, cross1, early, kept0 = tied((inner, mid_f, mid_b, cross1, early, kept0))
    close, mid = turn_of(numbers, kept1, cross1, half3, inner, mid_f, mid_b)
    close = on_line(close, 1)
    mid = between(mid)
    close, mid, cross0 = tied((close, mid, cross0))

    total, predicted, kinds, gene, spots = sums_of(kept0, cross0, close, mid, own_target, side, dens_part)
    spots_more = across(spots)
    gene_more = swapped(gene, 1)
    spots_more, gene_more = tied((spots_more, gene_more))
    gene = gene + gene_more
    gene_more = swapped(gene, 2)
    spots = spots + spots_more
    mores = [on_line(spots, step) for step in (3, 2, 1)]
    own, dens, cross, kinds = grads_of(
        scale, slots, total, own_target, side, density, gene, gene_more, early, spots, spot_target, *mores, kinds
    )

    def update(place, block, acc, mass, **options):
        return update_of(numbers, place, block, expression, low, acc, mass, **options)

    cross0 = across(own)
    close0 = on_line(own, 1)
    mid0 = between(own)
    cross = cross + swapped(cross, 1)
    dens_row, cross = density_of(scale, slots, early, cross, swapped(cross, 2), side, density, dens)
    acc, mass, (mine0, theirs0) = update((0, 0), own, dens_row, mass, start=True)
    near0 = near_of([theirs0], (0,))
    close0, mid0, cross0, mass, near0 = tied((close0, mid0, cross0, mass, near0))

    whole = [((0, 1, 1, 0), 0, GROUP, 0, 0)]
    (block1,) = choose_of(numbers, (close0, mid0), (GROUP,), whole)
    cross1 = across(block1)
    mid1 = between(close0)
    outer1 = outward(mid0)
    far0 = far_of(pair_of(mine0, near0), (0,))
    acc, mass, kept = update((0, 1), cross0, acc, mass)
    acc, mass, (mine1, theirs1) = update((1, 0), block1, acc, mass, kept=kept)
    near1 = near_of([theirs1], (0, 1))
    outer1, mid1, cross1, mass, near1, far0 = tied((outer1, mid1, cross1, mass, near1, far0))

    (block2,) = choose_of(numbers, (outer1, mid1), (GROUP,), whole)
    last = outward(mid1)
    cross2 = across(block2)
    far1 = far_of(pair_of(mine1, near1), (0, 1))
    acc, mass, kept = update((2, 0), block2, acc, mass)
    acc, mass, (mine2, theirs2) = update((1, 1), cross1, acc, mass, kept=kept)
    near2 = near_of([theirs2], (1, 2))
    last, cross2, mass, near2, far1 = tied((last, cross2, mass, near2, far1))

    block3, front, back = choose_of(
        numbers,
        (close0, last, cross0, cross2, kinds),
        (GROUP, UPPER, UPPER + 2 * KINDS),
        [
            ((1, 0, 0, 1), 0, GROUP, 0, 0),
            ((1, 0, 0, 1), 0, UPPER, 1, 0),
            ((2, 3, 3, 2), UPPER, UPPER, 2, 0),
            ((4, 4, 4, 4), 0, 2 * KINDS, 2, UPPER),
        ],
    )
    front = across(front)
    back = on_line(back, 1)
    far2 = far_of(pair_of(mine2, near2), (1, 2))
    mass, mine3, theirs3, columns3 = both_of(numbers, ((2, 1), (3, 0)), (cross2, block3), expression, low, mass)
    near3 = near_of(theirs3, (2, 3))
    pair3 = pair_of(mine3, near3)
    front, back, mass, pair3, far2 = tied((front, back, mass, pair3, far2))

    mass, mine4, theirs4, columns, block = part_of(numbers, (3, 1), front, back, expression, low, mass)
    mass_far = swapped(mass, 2)
    far3 = far_of(pair3, (2, 3))
    near4 = near_of([theirs4], (3,))
    pair4 = pair_of(mine4, near4)
    kinds = merge_of(numbers, 1, kinds, back)
    kinds_more = on_line(kinds, 2)
    acc, fetched = gather_of(columns3, acc, (cross2, block3), logits)
    mass_far, far3, pair4, kinds_more, acc = tied((mass_far, far3, pair4, kinds_more, acc))
    mass = plus(mass, mass_far)
    mass_near = swapped(mass, 1)
    far4 = far_of(pair4, (3,))
    kinds = merge_of(numbers, 2, kinds, kinds_more)
    kinds_more = across(kinds)
    grad_logits = finish_of(columns, block, fetched, factor, acc, mass, mass_near)
    grad_logits, far3 = tied((grad_logits, far3))
    triples = [(mine0, near0, far0), (mine1, near1, far1), (mine2, near2, far2), (mine3, near3, far3)]
    plan = [((turn, 0), turn) for turn in range(4)] + [((turn, 1), turn + 1) for turn in range(3)]
    result = collect_of(numbers, plan, triples)
    types, table = kinds_of(numbers, kinds, kinds_more, early, cross)
    result = collect_of(numbers, [((3, 1), 0)], [(mine4, near4, far4)], result)
    return (predicted, grad_logits, result, table, types)


def solution(mesh):
    in_specs = (
        P("cells", "spots"),
        P("cells", None),
        P(None, "spots"),
        P("spots"),
        P("spots"),
        P("cells"),
        P("cells"),
    )
    out_specs = (
        P("cells", "spots"),
        P("cells", "spots"),
        P("cells", "spots"),
        P(),
        P(None, "spots"),
    )
    fits = mesh.shape["cells"] == 8 and mesh.shape["spots"] == 4
    return jax.shard_map(
        ladder if fits else general, mesh=mesh, in_specs=in_specs, out_specs=out_specs, check_vma=False
    )
```

```python
import functools
import math

import jax
import jax.numpy as jnp
import numpy as np
from jax import lax
from jax.experimental import pallas as pl
from jax.experimental.pallas import tpu as pltpu
from jax.sharding import PartitionSpec as P

GENES = 2048
NTYPE = 128
LANES = 128
BF = jnp.bfloat16
F32 = jnp.float32
highest = lax.Precision.HIGHEST


def over_rows(left_side, right_side):
    return lax.dot_general(
        left_side, right_side, (((0,), (0,)), ((), ())), preferred_element_type=F32
    )


def over_columns(left_side, right_side):
    return lax.dot_general(
        left_side, right_side, (((1,), (1,)), ((), ())), preferred_element_type=F32
    )


def general(logits, expression, target, density, assignment, labels, counts):
    row_count = logits.shape[0]
    spot_width = logits.shape[1]
    cell_devices = lax.axis_size("cells")
    slot_total = float(row_count * cell_devices)
    scale = float(row_count * cell_devices * spot_width * lax.axis_size("spots"))
    live = (jnp.arange(row_count, dtype=jnp.int32) < counts[0])[:, None]
    raised = jnp.exp(logits)
    row_mass = lax.psum(jnp.sum(raised, axis=1), "spots")
    probs = jnp.where(live, raised / row_mass[:, None], 0.0)
    probs_low = probs.astype(BF)
    one_hot = (labels[:, None] == jnp.arange(NTYPE, dtype=jnp.int32)[None, :]).astype(BF)
    type_total, dens_total = lax.psum((over_rows(one_hot, probs_low), jnp.sum(probs, axis=0)), "cells")
    gene_rows = GENES // cell_devices
    predicted = lax.psum_scatter(
        over_rows(expression, probs_low), "cells", scatter_dimension=0, tiled=True
    )
    target_full = lax.dynamic_slice_in_dim(
        target, lax.axis_index("cells") * gene_rows, gene_rows, 0
    ).astype(F32)
    spot_dot, spot_pred, spot_target = lax.psum(
        (
            jnp.sum(predicted * target_full, axis=0),
            jnp.sum(predicted * predicted, axis=0),
            jnp.sum(target_full * target_full, axis=0),
        ),
        "cells",
    )
    dens_pred = dens_total / slot_total
    sides = jnp.stack([assignment == 0, assignment == 1]).astype(F32)
    inv_spot_pred = lax.rsqrt(spot_pred)
    inv_spot_target = lax.rsqrt(spot_target)
    spot_cosine = spot_dot * inv_spot_pred * inv_spot_target
    columns = jnp.stack(
        [
            jnp.ones_like(density),
            density,
            density * jnp.log(density),
            density * jnp.log(dens_pred),
            dens_pred,
            spot_cosine,
        ]
    )
    slide_part = jnp.dot(sides, columns.T, precision=highest)
    gene_part = jnp.stack(
        [
            jnp.dot(predicted * target_full, sides.T, precision=highest),
            jnp.dot(predicted * predicted, sides.T, precision=highest),
            jnp.dot(target_full * target_full, sides.T, precision=highest),
        ]
    )
    slide_sums, gene_sums = lax.psum((slide_part, gene_part), "spots")
    spot_count, dens_mass, dens_log, cross_log, pred_mass, cosine_sum = [
        slide_sums[:, at] for at in range(6)
    ]
    inv_gene_pred = lax.rsqrt(gene_sums[1])
    inv_gene_target = lax.rsqrt(gene_sums[2])
    gene_cosine = gene_sums[0] * inv_gene_pred * inv_gene_target
    gene_along_target = jnp.dot(inv_gene_pred * inv_gene_target, sides, precision=highest)
    gene_along_pred = jnp.dot(gene_cosine * inv_gene_pred * inv_gene_pred, sides, precision=highest)
    spot_weight = 1.0 / jnp.dot(spot_count, sides, precision=highest)
    spot_along_target = inv_spot_pred * inv_spot_target * spot_weight
    spot_along_pred = spot_cosine * inv_spot_pred * inv_spot_pred * spot_weight
    grad_dens = scale * (
        jnp.dot(1.0 / pred_mass, sides, precision=highest)
        - density / (jnp.dot(dens_mass, sides, precision=highest) * dens_pred)
    )
    grad_pred = scale * (
        -(target_full * gene_along_target - predicted * gene_along_pred) / GENES
        - (target_full * spot_along_target[None, :] - predicted * spot_along_pred[None, :])
    )
    grad_low = lax.all_gather(grad_pred.astype(BF), "cells", axis=0, tiled=True)
    grad_probs = jnp.dot(expression, grad_low, preferred_element_type=F32)
    grad_expr_part = over_columns(probs_low, grad_low)
    gene_loss = lax.psum(jnp.sum(gene_cosine, axis=0), "cells")
    grad_probs = grad_probs + (grad_dens / slot_total)[None, :]
    row_total = lax.psum(jnp.sum(probs * grad_probs, axis=1), "spots")
    grad_logits = probs * (grad_probs - row_total[:, None])
    grad_expression = lax.psum_scatter(grad_expr_part, "spots", scatter_dimension=1, tiled=True)
    divergence = (dens_log - cross_log) / dens_mass - jnp.log(dens_mass) + jnp.log(pred_mass)
    table = jnp.stack([gene_loss / GENES, cosine_sum / spot_count, divergence], axis=1)
    return (predicted.astype(BF), grad_logits, grad_expression, table, type_total * NTYPE)


VMEM = pltpu.MemorySpace.VMEM
HBM = pltpu.MemorySpace.HBM
IN_VMEM = pl.BlockSpec(memory_space=VMEM)
IN_SMEM = pl.BlockSpec(memory_space=pltpu.MemorySpace.SMEM)
IN_PLACE = pl.BlockSpec(memory_space=pl.ANY)
CHUNK = 2 * LANES
MIB = 1024 * 1024
GROUP = GENES // 8
KINDS = NTYPE // 8
PIECES = 4
PAD = 16

FRONT = 144
ROWS = GROUP + KINDS
BACK = ROWS - FRONT
UPPER = 144
LOWER = GROUP - UPPER


def line_at(numbers_ref):
    return numbers_ref[0] // 2


def order_of(line, turn):
    return (line, 1 + line % 2, (line + 2) % 4, 3 - 3 * (line % 2))[turn]


def block_at(numbers_ref, place):
    turn, other = place
    rung = numbers_ref[0] % 2
    return 2 * order_of(line_at(numbers_ref), turn) + (1 - rung if other else rung)


def call(kernel, name, inputs, outputs, scratch=(), aliases=None, limit=8, flops=1024):
    return pl.pallas_call(
        kernel,
        in_specs=[spec for _, spec in inputs],
        out_specs=[spec for _, spec in outputs],
        out_shape=[shape for shape, _ in outputs],
        scratch_shapes=list(scratch),
        input_output_aliases=aliases or {},
        compiler_params=pltpu.CompilerParams(vmem_limit_bytes=limit * MIB),
        cost_estimate=pl.CostEstimate(flops=flops, bytes_accessed=1024, transcendentals=0),
        name=name,
    )(*[array for array, _ in inputs])


def plain(*shape, dtype=F32):
    return jax.ShapeDtypeStruct(shape, dtype)


def pinned(array, space):
    return pltpu.with_memory_space_constraint(array, space)


def to_row(column):
    return jnp.broadcast_to(column, (LANES, LANES)).T[:1]


def to_column(row):
    return jnp.broadcast_to(row, (LANES, LANES)).T[:, :1]


def line_of(at):
    return pl.ds(at * LANES, LANES)


def columns_of(at):
    return pl.ds(pl.multiple_of(at * GROUP, GROUP), GROUP)


def packed_row(values):
    lane = lax.broadcasted_iota(jnp.int32, (1, LANES), 1)
    row = jnp.zeros((1, LANES), F32)
    for at, value in enumerate(values):
        row = jnp.where(lane == at, value, row)
    return row


def row_sum(row):
    return jnp.sum(row, axis=1, keepdims=True)


def mass_kernel(logits_ref, raised_ref, mass_ref, sems):
    lines = mass_ref.shape[0]
    copies = [
        pltpu.make_async_copy(logits_ref.at[line_of(at)], raised_ref.at[line_of(at)], sems.at[at])
        for at in range(lines)
    ]
    for copy in copies:
        copy.start()
    for at, copy in enumerate(copies):
        copy.wait()
        raised = jnp.exp(raised_ref[line_of(at), :])
        raised_ref[line_of(at), :] = raised
        mass_ref[pl.ds(at, 1), :] = to_row(jnp.sum(raised, axis=1, keepdims=True))


def mass_of(logits):
    rows, width = logits.shape
    lines = rows // LANES
    return call(
        mass_kernel,
        "mass",
        [(pinned(logits, HBM), IN_PLACE)],
        [(VMEM((rows, width), F32), IN_VMEM), (plain(lines, LANES), IN_VMEM)],
        [pltpu.SemaphoreType.DMA((lines,))],
    )


def left_kernel(places, numbers_ref, expr_ref, labels_ref, left_ref, held, sems):
    _, _, cells = left_ref.shape

    def copy(n):
        return pltpu.make_async_copy(
            expr_ref.at[:, columns_of(block_at(numbers_ref, places[n]))], held.at[n % 2], sems.at[n % 2]
        )

    copy(0).start()
    for n, place in enumerate(places):
        if n + 1 < len(places):
            copy(n + 1).start()
        kind = lax.broadcasted_iota(jnp.int32, (KINDS, cells), 0) + block_at(numbers_ref, place) * KINDS
        left_ref[n, GROUP:, :] = jnp.where(kind == labels_ref[...], 1.0, 0.0).astype(BF)
        copy(n).wait()
        left_ref[n, :GROUP, :] = held[n % 2].T


def left_of(numbers, places, expression, labels):
    cells = expression.shape[0]
    count = len(places)
    return call(
        functools.partial(left_kernel, places),
        "left",
        [(numbers, IN_SMEM), (pinned(expression, HBM), IN_PLACE), (labels, IN_VMEM)],
        [(VMEM((count, GROUP + KINDS, cells), BF), IN_VMEM)],
        [pltpu.VMEM((2, cells, GROUP), BF), pltpu.SemaphoreType.DMA((2,))],
    )[0]


def first_kernel(counts_ref, raised_ref, near_ref, far_ref, left_ref, low_ref, dens_ref, factor_ref, front_ref, back_ref, total):
    cells = raised_ref.shape[0]
    lines = cells // LANES
    row = lax.broadcasted_iota(jnp.int32, (lines, LANES), 0) * LANES + lax.broadcasted_iota(
        jnp.int32, (lines, LANES), 1
    )
    factor_ref[...] = jnp.where(row < counts_ref[0], 1.0 / (near_ref[...] + far_ref[...]), 0.0)
    mass = 0.0
    for at in range(lines):
        probs = raised_ref[line_of(at), :] * to_column(factor_ref[pl.ds(at, 1), :])
        low_ref[line_of(at), :] = probs.astype(BF)
        mass = mass + jnp.sum(probs, axis=0, keepdims=True)
        if at % 2:
            part = pl.ds((at // 2) * CHUNK, CHUNK)
            more = jnp.dot(left_ref[0, :, part], low_ref[part, :], preferred_element_type=F32)
            if at == 1:
                total[...] = more
            elif at + 1 < lines:
                total[...] += more
            else:
                whole = (total[...] + more).astype(BF)
                front_ref[...] = whole[:FRONT]
                back_ref[...] = whole[FRONT:]
    dens_ref[...] = mass


def first_of(counts, raised, near, far, left):
    cells, width = raised.shape
    rows = left.shape[1]
    return call(
        first_kernel,
        "first",
        [(counts, IN_SMEM)] + [(a, IN_VMEM) for a in (raised, near, far, left)],
        [(VMEM((cells, width), BF), IN_VMEM), (plain(1, width), IN_VMEM)]
        + [(plain(*near.shape), IN_VMEM), (plain(FRONT, width, dtype=BF), IN_VMEM), (plain(BACK, width, dtype=BF), IN_VMEM)],
        [pltpu.VMEM((rows, width), F32)],
    )


def blocks_kernel(which, left_ref, low_ref, *out_refs):
    width = low_ref.shape[1]
    tile = width // 3
    for n, out_ref in zip(which, out_refs):

        def step(at, _, n=n, out_ref=out_ref):
            columns = pl.ds(pl.multiple_of(at * tile, LANES), tile)
            out_ref[:, columns] = jnp.dot(
                left_ref[n], low_ref[:, columns], preferred_element_type=F32
            ).astype(out_ref.dtype)
            return 0

        lax.fori_loop(0, 3, step, 0)


def blocks_of(left, low, which, dtype):
    cells, width = low.shape
    rows = left.shape[1]
    return call(
        functools.partial(blocks_kernel, which),
        "blocks",
        [(left, IN_VMEM), (low, IN_VMEM)],
        [(plain(rows, width, dtype=dtype), IN_VMEM)] * len(which),
        limit=6,
    )


def early_kernel(numbers_ref, target_ref, density_ref, side_ref, spot_ref, own_ref, sums_ref, held, sems):
    genes = target_ref.shape[0]
    count = genes // GROUP

    def copy(n):
        rows = pl.ds(n * GROUP, GROUP)
        return pltpu.make_async_copy(target_ref.at[rows], held.at[n % 2], sems.at[n % 2])

    mine = pltpu.make_async_copy(target_ref.at[columns_of(numbers_ref[0])], own_ref, sems.at[2])
    mine.start()
    copy(0).start()
    spot_ref[...] = jnp.zeros_like(spot_ref)
    for n in range(count):
        if n + 1 < count:
            copy(n + 1).start()
        copy(n).wait()
        target = held[n % 2].astype(F32)
        spot_ref[...] += jnp.sum(target * target, axis=0, keepdims=True)
    mine.wait()
    side = side_ref[...]
    other = 1.0 - side
    density = density_ref[...]
    target = own_ref[...].astype(F32)
    square = target * target
    lane = lax.broadcasted_iota(jnp.int32, (GROUP, LANES), 1)
    columns = jnp.where(
        lane == 0,
        jnp.sum(square * other, axis=1, keepdims=True),
        jnp.where(lane == 1, jnp.sum(square * side, axis=1, keepdims=True), 0.0),
    )
    sums_ref[0:2, :] = columns.T[:2]
    logged = density * jnp.log(density)
    known = packed_row([row_sum(value * part) for value in (1.0, density, logged) for part in (other, side)])
    sums_ref[2:3, :] = jnp.concatenate([known, jnp.zeros_like(known)], axis=1)


def early_of(numbers, target, density, side):
    width = target.shape[1]
    return call(
        early_kernel,
        "early",
        [(numbers, IN_SMEM), (pinned(target, HBM), IN_PLACE), (density, IN_VMEM), (side, IN_VMEM)],
        [(plain(1, width), IN_VMEM), (VMEM((GROUP, width), BF), IN_VMEM), (plain(3, GROUP), IN_VMEM)],
        [pltpu.VMEM((2, GROUP, width), BF), pltpu.SemaphoreType.DMA((3,))],
        limit=16,
    )


def half_kernel(kept_ref, front_ref, half_ref, front_out, back_out):
    half_ref[...] = kept_ref[...]
    half_ref[:FRONT] += front_ref[...].astype(F32)
    front_out[...] = half_ref[:FRONT].astype(BF)
    back_out[...] = half_ref[FRONT:].astype(BF)


def half_of(kept, front):
    width = kept.shape[1]
    return call(
        half_kernel,
        "half",
        [(kept, IN_VMEM), (front, IN_VMEM)],
        [(plain(*kept.shape), IN_VMEM)] + [(plain(rows, width, dtype=BF), IN_VMEM) for rows in (FRONT, BACK)],
        limit=10,
    )


def join_kernel(lines, numbers_ref, part_ref, back_ref, out_ref):
    out_ref[:FRONT] = part_ref[:FRONT].astype(BF)
    line = line_at(numbers_ref)
    here = jnp.logical_or(line == lines[0], line == lines[1])

    @pl.when(here)
    def _():
        out_ref[FRONT:] = (part_ref[FRONT:] + back_ref[...].astype(F32)).astype(BF)

    @pl.when(jnp.logical_not(here))
    def _():
        out_ref[FRONT:] = part_ref[FRONT:].astype(BF)


def join_of(numbers, part, back, lines):
    return call(
        functools.partial(join_kernel, lines),
        "join",
        [(numbers, IN_SMEM), (part, IN_VMEM), (back, IN_VMEM)],
        [(plain(*part.shape, dtype=BF), IN_VMEM)],
        limit=8,
    )[0]


def step_kernel(kept_ref, cross_ref, front_ref, back_ref, out_ref, front_out, back_out):
    for start, more_ref in ((0, front_ref), (FRONT, back_ref)):
        rows = pl.ds(start, more_ref.shape[0])
        out_ref[rows, :] = (
            kept_ref[rows, :] + cross_ref[rows, :].astype(F32) + more_ref[...].astype(F32)
        ).astype(BF)
    front_out[...] = out_ref[:FRONT]
    back_out[...] = out_ref[FRONT:]


def step_of(kept, cross, front, back):
    width = kept.shape[1]
    return call(
        step_kernel,
        "step",
        [(a, IN_VMEM) for a in (kept, cross, front, back)],
        [(plain(rows, width, dtype=BF), IN_VMEM) for rows in (ROWS, FRONT, BACK)],
        limit=12,
    )


def in_middle(numbers_ref):
    line = line_at(numbers_ref)
    return jnp.logical_or(line == 1, line == 2)


def turn_kernel(numbers_ref, kept_ref, cross_ref, early_ref, inner_ref, front_ref, back_ref, near_out, middle_out):
    middle = in_middle(numbers_ref)

    @pl.when(middle)
    def _():
        near_out[:FRONT] = (early_ref[:FRONT] + front_ref[...].astype(F32)).astype(BF)
        near_out[FRONT:] = (early_ref[FRONT:] + back_ref[...].astype(F32)).astype(BF)
        middle_out[...] = (kept_ref[...] + cross_ref[...].astype(F32) + inner_ref[...].astype(F32)).astype(BF)

    @pl.when(jnp.logical_not(middle))
    def _():
        near_out[...] = (kept_ref[...] + cross_ref[...].astype(F32)).astype(BF)
        middle_out[...] = near_out[...]


def turn_of(numbers, kept, cross, early, inner, front, back):
    return call(
        turn_kernel,
        "turn",
        [(numbers, IN_SMEM)] + [(a, IN_VMEM) for a in (kept, cross, early, inner, front, back)],
        [(plain(*inner.shape, dtype=BF), IN_VMEM)] * 2,
        limit=15,
    )


def sums_kernel(
    kept_ref, cross_ref, up_ref, down_ref, target_ref, side_ref, dens_ref,
    total_ref, low_ref, kinds_ref, gene_ref, spot_ref,
):
    total = (
        kept_ref[...] + cross_ref[...].astype(F32) + up_ref[...].astype(F32) + down_ref[...].astype(F32)
    )
    pred = total[:GROUP]
    total_ref[...] = pred
    kinds_ref[...] = total[GROUP:].astype(BF)
    low_ref[...] = pred.astype(BF)
    dot = pred * target_ref[...].astype(F32)
    square = pred * pred
    side = side_ref[...]
    spot_ref[0:1, :] = jnp.sum(dot, axis=0, keepdims=True)
    spot_ref[1:2, :] = jnp.sum(square, axis=0, keepdims=True)
    spot_ref[2:3, :] = dens_ref[...]
    sums = [
        jnp.sum(dot * (1.0 - side), axis=1, keepdims=True),
        jnp.sum(dot * side, axis=1, keepdims=True),
        jnp.sum(square * (1.0 - side), axis=1, keepdims=True),
        jnp.sum(square * side, axis=1, keepdims=True),
    ]
    lane = lax.broadcasted_iota(jnp.int32, (GROUP, LANES), 1)
    packed = jnp.zeros((GROUP, LANES), F32)
    for place, column in enumerate(sums):
        packed = jnp.where(lane == place, column, packed)
    gene_ref[...] = packed.T[:4]


def sums_of(kept, *inputs):
    rows, width = kept.shape
    return call(
        sums_kernel,
        "sums",
        [(a, IN_VMEM) for a in (kept, *inputs)],
        [(VMEM((GROUP, width), F32), IN_VMEM), (plain(GROUP, width, dtype=BF), IN_VMEM)]
        + [(plain(KINDS, width, dtype=BF), IN_VMEM)]
        + [(plain(4, GROUP), IN_VMEM), (plain(3, width), IN_VMEM)],
        limit=16,
    )


def put_sum(ref, start, value):
    high = value.astype(BF).astype(F32)
    middle = (value - high).astype(BF).astype(F32)
    low = (value - high) - middle
    row = lax.broadcasted_iota(jnp.int32, (KINDS, LANES), 0)
    tile = jnp.where(row == 0, high, jnp.where(row == 1, middle, jnp.where(row == 2, low, 0.0)))
    ref[start:, :] = jnp.zeros((KINDS, ref.shape[1]), BF)
    ref[start:, :LANES] = tile.astype(BF)


def get_sum(ref, start):
    tile = ref[start:, :LANES].astype(F32)
    return tile[0:1] + tile[1:2] + tile[2:3]


def grads_kernel(
    scale, slots, total_ref, target_ref, side_ref, density_ref, gene_ref, gene_more_ref, early_ref, spot_ref, spot_target_ref,
    more0_ref, more1_ref, more2_ref, kinds_ref, out_ref, dens_ref, cross_ref, kinds_out
):
    side = side_ref[...]
    other = 1.0 - side
    spot = spot_ref[...] + more0_ref[...] + more1_ref[...] + more2_ref[...]
    inv_spot_pred = lax.rsqrt(spot[1:2])
    inv_spot_target = lax.rsqrt(spot_target_ref[...])
    cosine = spot[0:1] * inv_spot_pred * inv_spot_target
    known = early_ref[2:3, :]
    weight = scale / (other * known[:, 0:1] + side * known[:, 1:2])
    spot_along_target = inv_spot_pred * inv_spot_target * weight
    spot_along_pred = cosine * inv_spot_pred * inv_spot_pred * weight
    gene = gene_ref[...] + gene_more_ref[...]
    inv_gene_pred = lax.rsqrt(gene[2:4])
    inv_gene_target = lax.rsqrt(early_ref[0:2, :])
    gene_cosine = gene[0:2] * inv_gene_pred * inv_gene_target
    along = jnp.concatenate(
        [
            (scale / GENES) * inv_gene_pred * inv_gene_target,
            (scale / GENES) * gene_cosine * inv_gene_pred * inv_gene_pred,
            jnp.zeros((LANES - 4, GROUP), F32),
        ],
        axis=0,
    ).T
    along_target = along[:, 0:1] * other + along[:, 1:2] * side + spot_along_target
    along_pred = along[:, 2:3] * other + along[:, 3:4] * side + spot_along_pred
    out_ref[...] = (total_ref[...] * along_pred - target_ref[...].astype(F32) * along_target).astype(BF)
    dens_pred = spot[2:3] / slots
    dens_ref[...] = dens_pred
    cross = density_ref[...] * jnp.log(dens_pred)
    cross_ref[...] = packed_row([row_sum(value * part) for value in (cross, dens_pred, cosine) for part in (other, side)])
    kinds_out[:KINDS] = kinds_ref[...]
    put_sum(kinds_out, KINDS, packed_row([row_sum(gene_cosine[0:1]), row_sum(gene_cosine[1:2])]))


def grads_of(scale, slots, total, *inputs):
    rows, width = total.shape
    return call(
        functools.partial(grads_kernel, scale, slots),
        "grads",
        [(a, IN_VMEM) for a in (total, *inputs)],
        [(plain(rows, width, dtype=BF), IN_VMEM), (plain(1, width), IN_VMEM)]
        + [(plain(1, LANES), IN_VMEM), (plain(2 * KINDS, width, dtype=BF), IN_VMEM)],
        limit=14,
    )


def density_kernel(scale, slots, early_ref, cross_ref, cross_more_ref, side_ref, density_ref, dens_ref, out_ref, cross_out):
    side = side_ref[...]
    other = 1.0 - side
    known = early_ref[2:3, :]
    cross = cross_ref[...] + cross_more_ref[...]
    cross_out[...] = cross
    inverse = other / cross[:, 2:3] + side / cross[:, 3:4]
    dens_mass = other * known[:, 2:3] + side * known[:, 3:4]
    out_ref[...] = (scale / slots) * (inverse - density_ref[...] / (dens_mass * dens_ref[...]))


def density_of(scale, slots, early, cross, cross_more, side, density, dens):
    return call(
        functools.partial(density_kernel, scale, slots),
        "density",
        [(a, IN_VMEM) for a in (early, cross, cross_more, side, density, dens)],
        [(plain(*side.shape), IN_VMEM), (plain(1, LANES), IN_VMEM)],
    )


def choose_kernel(plan, numbers_ref, *refs):
    count = max(max(choices) for choices, _, _, _, _ in plan) + 1
    sources, out_refs, sems = refs[:count], refs[count:-1], refs[-1]
    line = line_at(numbers_ref)
    for place in range(4):

        @pl.when(line == place)
        def _(place=place):
            copies = [
                pltpu.make_async_copy(
                    sources[choices[place]].at[pl.ds(start, rows)], out_refs[out].at[pl.ds(to, rows)], sems.at[n]
                )
                for n, (choices, start, rows, out, to) in enumerate(plan)
            ]
            for copy in copies:
                copy.start()
            for copy in copies:
                copy.wait()


def choose_of(numbers, arrays, outputs, plan):
    width = arrays[0].shape[1]
    return call(
        functools.partial(choose_kernel, plan),
        "choose",
        [(numbers, IN_SMEM)] + [(a, IN_PLACE) for a in arrays],
        [(plain(rows, width, dtype=BF), IN_PLACE) for rows in outputs],
        [pltpu.SemaphoreType.DMA((len(plan),))],
    )


def mine_at(numbers_ref, turn):
    return order_of(line_at(numbers_ref), turn) % 2 == numbers_ref[1] % 2


def keep(numbers_ref, turn, grads, mine_ref, *theirs_refs):
    mine = mine_at(numbers_ref, turn)

    @pl.when(mine)
    def _():
        mine_ref[...] = grads[...]

    @pl.when(jnp.logical_not(mine))
    def _():
        depth = theirs_refs[0].shape[0]
        for n, theirs_ref in enumerate(theirs_refs):
            theirs_ref[...] = grads[pl.ds(n * depth, depth), :].astype(BF)


def update_kernel(start, place, numbers_ref, expr_ref, low_ref, acc_ref, mass_ref, block_ref, *refs):
    acc_out, mass_out, mine_ref, theirs_ref, held, turned, grads, sem = refs[-8:]
    cells = low_ref.shape[0]
    copy = pltpu.make_async_copy(expr_ref.at[:, columns_of(block_at(numbers_ref, place))], held, sem)
    copy.start()
    turned[...] = block_ref[...].T
    copy.wait()
    for at in range(cells // CHUNK):
        part = pl.ds(at * CHUNK, CHUNK)
        expr = held[part, :]
        low = low_ref[part, :]
        more = jnp.dot(expr, block_ref[...], preferred_element_type=F32)
        grad = jnp.dot(low, turned[...], preferred_element_type=F32)
        grads[part, :] = grad
        mass = jnp.sum(expr.astype(F32) * grad, axis=1, keepdims=True)
        if start:
            dens = acc_ref[...]
            acc_out[part, :] = more + dens
            mass = mass + jnp.sum(low.astype(F32) * dens, axis=1, keepdims=True)
        else:
            acc_out[part, :] += more
        for half in range(CHUNK // LANES):
            line = pl.ds(at * (CHUNK // LANES) + half, 1)
            row = to_row(mass[half * LANES : (half + 1) * LANES])
            mass_out[line, :] = row if start else row + mass_ref[line, :]
    keep(numbers_ref, place[0], grads, mine_ref, theirs_ref)


def update_of(numbers, place, block, expression, low, acc, mass, start=False, kept=()):
    cells, width = low.shape
    inputs = [(numbers, IN_SMEM), (pinned(expression, HBM), IN_PLACE)]
    inputs += [(a, IN_VMEM) for a in (low, acc, mass, block, *kept)]
    aliases = {} if start else {3: 0}
    if kept:
        aliases |= {6: 2, 7: 3}
    acc, mass, *kept = call(
        functools.partial(update_kernel, start, place),
        "update",
        inputs,
        [(VMEM((cells, width), F32), IN_VMEM), (plain(*mass.shape), IN_VMEM)]
        + [(VMEM((cells, GROUP), F32), IN_VMEM), (VMEM((cells, GROUP), BF), IN_VMEM)],
        [
            pltpu.VMEM((cells, GROUP), BF),
            pltpu.VMEM((width, GROUP), BF),
            pltpu.VMEM((cells, GROUP), F32),
            pltpu.SemaphoreType.DMA,
        ],
        aliases=aliases,
        limit=6,
    )
    return acc, mass, kept


def both_kernel(places, numbers_ref, expr_ref, low_ref, mass_ref, first_ref, second_ref, *refs):
    mass_out, mine_ref, front_ref, back_ref, held, turned, grads, sems = refs
    cells = low_ref.shape[0]
    copies = [
        pltpu.make_async_copy(
            expr_ref.at[:, columns_of(block_at(numbers_ref, place))], held.at[n], sems.at[n]
        )
        for n, place in enumerate(places)
    ]
    for copy in copies:
        copy.start()
    for n, block_ref in enumerate((first_ref, second_ref)):
        turned[:, n * GROUP : (n + 1) * GROUP] = block_ref[...].T
    for copy in copies:
        copy.wait()
    for at in range(cells // CHUNK):
        part = pl.ds(at * CHUNK, CHUNK)
        grad = jnp.dot(low_ref[part, :], turned[...], preferred_element_type=F32)
        mass = 0.0
        for n in range(2):
            one = grad[:, n * GROUP : (n + 1) * GROUP]
            grads[n, part, :] = one
            mass = mass + jnp.sum(held[n, part, :].astype(F32) * one, axis=1, keepdims=True)
        for half in range(CHUNK // LANES):
            line = pl.ds(at * (CHUNK // LANES) + half, 1)
            mass_out[line, :] = mass_ref[line, :] + to_row(mass[half * LANES : (half + 1) * LANES])
    for n, (turn, _) in enumerate(places):
        keep(numbers_ref, turn, grads.at[n], mine_ref, front_ref, back_ref)


def both_of(numbers, places, blocks, expression, low, mass):
    cells, width = low.shape
    mass, mine, front, back, columns = call(
        functools.partial(both_kernel, places),
        "both",
        [(numbers, IN_SMEM), (pinned(expression, HBM), IN_PLACE)] + [(a, IN_VMEM) for a in (low, mass, *blocks)],
        [(plain(*mass.shape), IN_VMEM), (VMEM((cells, GROUP), F32), IN_VMEM)]
        + [(plain(cells // 2, GROUP, dtype=BF), IN_VMEM)] * 2
        + [(VMEM((2, cells, GROUP), BF), IN_VMEM)],
        [
            pltpu.VMEM((width, 2 * GROUP), BF),
            pltpu.VMEM((2, cells, GROUP), F32),
            pltpu.SemaphoreType.DMA((2,)),
        ],
        limit=10,
    )
    return mass, mine, (front, back), columns


def gather_kernel(columns_ref, acc_ref, first_ref, second_ref, logits_ref, *refs):
    acc_out, *fetched, sems = refs
    cells = acc_ref.shape[0]
    depth = fetched[0].shape[0]
    copies = [
        pltpu.make_async_copy(logits_ref.at[pl.ds(n * depth, depth)], piece, sems.at[n])
        for n, piece in enumerate(fetched)
    ]
    for copy in copies:
        copy.start()
    blocks = (first_ref, second_ref)
    for at in range(cells // CHUNK):
        part = pl.ds(at * CHUNK, CHUNK)
        total = acc_out[part, :]
        for n, block_ref in enumerate(blocks):
            total = total + jnp.dot(columns_ref[n, part, :], block_ref[...], preferred_element_type=F32)
        acc_out[part, :] = total
    for copy in copies:
        copy.wait()


def gather_of(columns, acc, blocks, logits):
    cells, width = acc.shape
    acc, *pieces = call(
        gather_kernel,
        "gather",
        [(a, IN_VMEM) for a in (columns, acc, *blocks)] + [(pinned(logits, HBM), IN_PLACE)],
        [(VMEM((cells, width), F32), IN_VMEM)]
        + [(VMEM((cells // PIECES, width), F32), IN_VMEM)] * PIECES,
        [pltpu.SemaphoreType.DMA((PIECES,))],
        aliases={1: 0},
        limit=5,
    )
    return acc, pieces


def part_kernel(
    place, numbers_ref, expr_ref, low_ref, mass_ref, front_ref, back_ref, *refs
):
    mass_out, mine_ref, theirs_ref, held, block, turned, grads, sem = refs
    cells = low_ref.shape[0]
    copy = pltpu.make_async_copy(expr_ref.at[:, columns_of(block_at(numbers_ref, place))], held, sem)
    copy.start()
    block[:UPPER] = front_ref[...]
    block[UPPER:] = back_ref[:LOWER]
    turned[...] = block[...].T
    copy.wait()
    for at in range(cells // CHUNK):
        part = pl.ds(at * CHUNK, CHUNK)
        grad = jnp.dot(low_ref[part, :], turned[...], preferred_element_type=F32)
        grads[part, :] = grad
        mass = jnp.sum(held[part, :].astype(F32) * grad, axis=1, keepdims=True)
        for half in range(CHUNK // LANES):
            line = pl.ds(at * (CHUNK // LANES) + half, 1)
            mass_out[line, :] = mass_ref[line, :] + to_row(mass[half * LANES : (half + 1) * LANES])
    keep(numbers_ref, place[0], grads, mine_ref, theirs_ref)


def part_of(numbers, place, front, back, expression, low, mass):
    cells, width = low.shape
    return call(
        functools.partial(part_kernel, place),
        "part",
        [(numbers, IN_SMEM), (pinned(expression, HBM), IN_PLACE)]
        + [(a, IN_VMEM) for a in (low, mass, front, back)],
        [(plain(*mass.shape), IN_VMEM)]
        + [(VMEM((cells, GROUP), F32), IN_VMEM), (VMEM((cells, GROUP), BF), IN_VMEM)]
        + [(VMEM((cells, GROUP), BF), IN_VMEM), (VMEM((GROUP, width), BF), IN_VMEM)],
        [
            pltpu.VMEM((width, GROUP), BF),
            pltpu.VMEM((cells, GROUP), F32),
            pltpu.SemaphoreType.DMA,
        ],
        limit=7,
    )


def pair_kernel(count, mine_ref, *refs):
    near_refs, out_refs = refs[:-count], refs[-count:]
    rows = mine_ref.shape[0]
    pieces = max(len(near_refs), count)
    depth = rows // pieces
    for n in range(pieces):
        near_ref = near_refs[n * len(near_refs) // pieces]
        out_ref = out_refs[n * count // pieces]
        near_at = n * depth % near_ref.shape[0]
        out_at = n * depth % (rows // count)
        out_ref[pl.ds(out_at, depth), :] = (
            mine_ref[pl.ds(n * depth, depth), :] + near_ref[pl.ds(near_at, depth), :].astype(F32)
        ).astype(BF)
    if count == 1:
        out_refs[0][rows:] = jnp.zeros((PAD, mine_ref.shape[1]), BF)


def pair_of(mine, nears, count=1):
    rows, columns = mine.shape
    return call(
        functools.partial(pair_kernel, count),
        "pair",
        [(mine, IN_VMEM)] + [(near, IN_VMEM) for near in nears],
        [(plain(rows // count + (PAD if count == 1 else 0), columns, dtype=BF), IN_VMEM)] * count,
        limit=5,
    )


def collect_kernel(plan, counts, numbers_ref, *refs):
    out_ref, total, near, far, sems = refs[-5:]
    triples, at = [], 0
    for near_count, far_count in counts:
        end = at + 1 + near_count
        triples.append((refs[at], refs[at + 1 : end], refs[end : end + far_count]))
        at = end + far_count
    rows = total.shape[1]
    rung = numbers_ref[0] % 2

    def loads(slot, pair):
        mine_ref, near_refs, far_refs = triples[pair]
        copies = [pltpu.make_async_copy(mine_ref, total.at[slot], sems.at[slot, 0])]
        for sources, buffer in ((near_refs, near), (far_refs, far)):
            depth = rows // len(sources)
            for n, source in enumerate(sources):
                copies.append(
                    pltpu.make_async_copy(
                        source.at[pl.ds(0, depth)],
                        buffer.at[slot, pl.ds(n * depth, depth)],
                        sems.at[slot, 1 + len(copies)],
                    )
                )
        return copies

    for turn in sorted({turn for (turn, _), _ in plan}):
        entries = [(other, pair) for (at, other), pair in plan if at == turn]

        @pl.when(order_of(line_at(numbers_ref), turn) == numbers_ref[1])
        def _(entries=entries):
            for slot, (_, pair) in enumerate(entries):
                for copy in loads(slot, pair):
                    copy.start()
            stores = []
            for slot, (other, pair) in enumerate(entries):
                for copy in loads(slot, pair):
                    copy.wait()
                total[slot] += near[slot].astype(F32) + far[slot].astype(F32)
                columns = columns_of(1 - rung if other else rung)
                stores.append(pltpu.make_async_copy(total.at[slot], out_ref.at[:, columns], sems.at[slot, 1]))
                stores[-1].start()
            for store in stores:
                store.wait()


def collect_of(numbers, plan, triples, result=None):
    cells = triples[0][0].shape[0]
    depth = max(sum(1 for (at, _), _ in plan if at == turn) for (turn, _), _ in plan)
    inputs = [(numbers, IN_SMEM)]
    inputs += [(a, IN_PLACE) for mine, nears, fars in triples for a in (mine, *nears, *fars)]
    aliases = {}
    if result is not None:
        aliases = {len(inputs): 0}
        inputs.append((result, IN_PLACE))
    return call(
        functools.partial(collect_kernel, plan, [(len(nears), len(fars)) for _, nears, fars in triples]),
        "collect",
        inputs,
        [(HBM((cells, 2 * GROUP), F32), IN_PLACE)],
        [
            pltpu.VMEM((depth, cells, GROUP), F32),
            pltpu.VMEM((depth, cells, GROUP), BF),
            pltpu.VMEM((depth, cells, GROUP), BF),
            pltpu.SemaphoreType.DMA((depth, 6)),
        ],
        aliases=aliases,
        limit=1 + 4 * depth,
    )[0]


def plus_kernel(first_ref, second_ref, out_ref):
    out_ref[...] = first_ref[...] + second_ref[...]


def plus(first, second):
    return call(
        plus_kernel,
        "plus",
        [(first, IN_VMEM), (second, IN_VMEM)],
        [(plain(*first.shape), IN_VMEM)],
        limit=1,
    )[0]


def finish_kernel(columns_ref, block_ref, factor_ref, acc_ref, mass_ref, more_ref, *refs):
    *pieces, out_ref, held, sems = refs
    lines = mass_ref.shape[0]
    share = lines // len(pieces)
    depth = held.shape[0]
    copies = []
    for at in range(lines):
        if at >= depth:
            copies[at - depth].wait()
        one = pl.ds(at, 1)
        rows = line_of(at)
        grad = acc_ref[rows, :] + jnp.dot(columns_ref[rows, :], block_ref[...], preferred_element_type=F32)
        logits = pieces[at // share][line_of(at % share), :]
        probs = jnp.exp(logits) * to_column(factor_ref[one, :])
        held[at % depth] = probs * (grad - to_column(mass_ref[one, :] + more_ref[one, :]))
        copies.append(pltpu.make_async_copy(held.at[at % depth], out_ref.at[rows], sems.at[at % depth]))
        copies[-1].start()
    for copy in copies[-depth:]:
        copy.wait()


def finish_of(columns, block, pieces, factor, acc, mass, more):
    rows, width = acc.shape
    depth = 4
    inputs = (columns, block, factor, acc, mass, more, *pieces)
    return call(
        finish_kernel,
        "finish",
        [(a, IN_VMEM) for a in inputs],
        [(HBM((rows, width), F32), IN_PLACE)],
        [pltpu.VMEM((depth, LANES, width), F32), pltpu.SemaphoreType.DMA((depth,))],
        limit=6,
        flops=1024,
    )[0]


def merge_kernel(bit, numbers_ref, mine_ref, theirs_ref, out_ref):
    rows = mine_ref.shape[0] - KINDS
    skip = theirs_ref.shape[0] - mine_ref.shape[0]
    own = (numbers_ref[0] // 2**bit) % 2
    for value in range(2):

        @pl.when(own == value)
        def _(value=value):
            out_ref[value * rows : (value + 1) * rows, :] = mine_ref[:rows]
            out_ref[(1 - value) * rows : (2 - value) * rows, :] = theirs_ref[skip : skip + rows]

    put_sum(out_ref, 2 * rows, get_sum(mine_ref, rows) + get_sum(theirs_ref, skip + rows))


def merge_of(numbers, bit, mine, theirs):
    rows, width = mine.shape
    return call(
        functools.partial(merge_kernel, bit),
        "merge",
        [(numbers, IN_SMEM), (mine, IN_VMEM), (theirs, IN_VMEM)],
        [(plain(2 * rows - KINDS, width, dtype=BF), IN_VMEM)],
        limit=2,
    )[0]


def kinds_kernel(numbers_ref, mine_ref, theirs_ref, early_ref, cross_ref, out_ref, table_ref, held, sem):
    own = numbers_ref[0] % 2
    for low_bit in range(2):
        for middle in range(2):
            for high in range(2):
                source = (2 * high + middle) * KINDS
                block = (4 * high + 2 * middle + low_bit) * KINDS

                @pl.when(own == low_bit)
                def _(source=source, block=block):
                    held[block : block + KINDS, :] = mine_ref[source : source + KINDS, :].astype(F32) * NTYPE

                @pl.when(own != low_bit)
                def _(source=source, block=block):
                    held[block : block + KINDS, :] = theirs_ref[source : source + KINDS, :].astype(F32) * NTYPE

    copy = pltpu.make_async_copy(held, out_ref, sem)
    copy.start()
    loss = get_sum(mine_ref, 4 * KINDS) + get_sum(theirs_ref, 4 * KINDS)
    known = early_ref[2:3, :LANES]
    cross = cross_ref[...]
    for k in range(2):
        one = lambda row, at: row[:, 2 * at + k : 2 * at + k + 1]
        count, dens_mass, dens_log = one(known, 0), one(known, 1), one(known, 2)
        cross_log, pred_mass, cosine_sum = one(cross, 0), one(cross, 1), one(cross, 2)
        divergence = (dens_log - cross_log) / dens_mass - jnp.log(dens_mass) + jnp.log(pred_mass)
        row = packed_row([loss[:, k : k + 1] / GENES, cosine_sum / count, divergence])
        table_ref[k : k + 1, :] = row[:, :3]
    copy.wait()


def kinds_of(numbers, mine, theirs, early, cross):
    width = mine.shape[1]
    return call(
        kinds_kernel,
        "kinds",
        [(numbers, IN_SMEM)] + [(a, IN_VMEM) for a in (mine, theirs, early, cross)],
        [(HBM((NTYPE, width), F32), IN_PLACE), (plain(2, 3), IN_VMEM)],
        [pltpu.VMEM((NTYPE, width), F32), pltpu.SemaphoreType.DMA],
        limit=3,
    )


tied = lax.optimization_barrier


def across(array):
    return lax.ppermute(array, "cells", [(at, at ^ 1) for at in range(8)])


def inward(array):
    return lax.ppermute(array, "cells", [(at, at ^ 2) for at in (0, 1, 6, 7)])


def between(array):
    return lax.ppermute(array, "cells", [(at, at ^ 6) for at in range(2, 6)])


def outward(array):
    return lax.ppermute(array, "cells", [(at ^ 2, at) for at in (0, 1, 6, 7)])


def on_line(array, step):
    return lax.ppermute(array, "cells", [(at, at ^ (2 * step)) for at in range(8)])


def swapped(array, step):
    return lax.ppermute(array, "spots", [(at, at ^ step) for at in range(4)])


def near_of(theirs, turns):
    pairs = [
        (at * 4 + place, at * 4 + (place ^ 1))
        for at in range(8)
        for place in range(4)
        if any(order_of(at // 2, turn) % 2 != place % 2 for turn in turns)
    ]
    return [lax.ppermute(piece, ("cells", "spots"), pairs) for piece in theirs]


def far_of(pair, turns):
    pairs = []
    for at in range(8):
        for owner in (order_of(at // 2, turn) for turn in turns):
            pairs.append((at * 4 + (owner ^ 2), at * 4 + owner))
    return [lax.ppermute(piece, ("cells", "spots"), pairs) for piece in pair]


def ladder(logits, expression, target, density, assignment, labels, counts):
    cells, width = logits.shape
    slots = float(cells * lax.axis_size("cells"))
    scale = float(cells * lax.axis_size("cells") * width * lax.axis_size("spots"))
    numbers = jnp.stack([lax.axis_index("cells"), lax.axis_index("spots")]).astype(jnp.int32)
    logits, numbers = tied((logits, numbers))
    side = (assignment == 1).astype(F32)[None, :]
    density = density[None, :]
    labels = labels[None, :]

    raised, mass = mass_of(logits)
    left_a = left_of(numbers, ((3, 1), (3, 0)), expression, labels)
    mass_near = mass + swapped(mass, 1)
    mass_near, left_a = tied((mass_near, left_a))
    mass_far = swapped(mass_near, 2)
    left_b = left_of(numbers, ((2, 1), (2, 0)), expression, labels)
    mass_far, left_b = tied((mass_far, left_b))
    low, dens_part, factor, front, back = first_of(counts, raised, mass_near, mass_far, left_a)

    front = across(front)
    back = on_line(back, 1)
    (kept3,) = blocks_of(left_a, low, (1,), F32)
    (send2,) = blocks_of(left_b, low, (0,), F32)
    left_c = left_of(numbers, ((1, 1), (1, 0), (0, 1), (0, 0)), expression, labels)
    front, back, kept3, send2, left_c = tied((front, back, kept3, send2, left_c))
    send2 = join_of(numbers, send2, back, (1, 2))
    cross2 = across(send2)
    front, send2 = tied((front, send2))
    half3, half3_f, half3_b = half_of(kept3, front)
    more_f = inward(half3_f)
    more_b = inward(half3_b)
    (kept2,) = blocks_of(left_b, low, (1,), F32)
    (send1,) = blocks_of(left_c, low, (0,), BF)
    cross1 = across(send1)
    (kept1,) = blocks_of(left_c, low, (1,), F32)
    (send0,) = blocks_of(left_c, low, (2,), F32)
    send0 = join_of(numbers, send0, back, (0, 3))
    more_f, more_b, cross2, kept2, kept1, send0 = tied((more_f, more_b, cross2, kept2, kept1, send0))
    more, more_f, more_b = step_of(kept2, cross2, more_f, more_b)
    inner = inward(more)
    mid_f = between(more_f)
    mid_b = between(more_b)
    cross0 = across(send0)
    (kept0,) = blocks_of(left_c, low, (3,), F32)
    spot_target, own_target, early = early_of(numbers, target, density, side)
    early = early + swapped(early, 1)
    early = early + swapped(early, 2)
    inner, mid_f, mid_b, cross1, early, kept0 = tied((inner, mid_f, mid_b, cross1, early, kept0))
    close, mid = turn_of(numbers, kept1, cross1, half3, inner, mid_f, mid_b)
    close = on_line(close, 1)
    mid = between(mid)
    close, mid, cross0 = tied((close, mid, cross0))

    total, predicted, kinds, gene, spots = sums_of(kept0, cross0, close, mid, own_target, side, dens_part)
    spots_more = across(spots)
    gene_more = swapped(gene, 1)
    spots_more, gene_more = tied((spots_more, gene_more))
    gene = gene + gene_more
    gene_more = swapped(gene, 2)
    spots = spots + spots_more
    mores = [on_line(spots, step) for step in (1,2,3)]
    own, dens, cross, kinds = grads_of(
        scale, slots, total, own_target, side, density, gene, gene_more, early, spots, spot_target, *mores, kinds
    )

    def update(place, block, acc, mass, **options):
        return update_of(numbers, place, block, expression, low, acc, mass, **options)

    cross0 = across(own)
    close0 = on_line(own, 1)
    mid0 = between(own)
    cross = cross + swapped(cross, 1)
    dens_row, cross = density_of(scale, slots, early, cross, swapped(cross, 2), side, density, dens)
    acc, mass, (mine0, theirs0) = update((0, 0), own, dens_row, mass, start=True)
    near0 = near_of([theirs0], (0,))
    close0, mid0, cross0, mass, near0 = tied((close0, mid0, cross0, mass, near0))

    whole = [((0, 1, 1, 0), 0, GROUP, 0, 0)]
    (block1,) = choose_of(numbers, (close0, mid0), (GROUP,), whole)
    cross1 = across(block1)
    mid1 = between(close0)
    outer1 = outward(mid0)
    far0 = far_of(pair_of(mine0, near0), (0,))
    acc, mass, kept = update((0, 1), cross0, acc, mass)
    acc, mass, (mine1, theirs1) = update((1, 0), block1, acc, mass, kept=kept)
    near1 = near_of([theirs1], (0, 1))
    outer1, mid1, cross1, mass, near1, far0 = tied((outer1, mid1, cross1, mass, near1, far0))

    (block2,) = choose_of(numbers, (outer1, mid1), (GROUP,), whole)
    last = outward(mid1)
    cross2 = across(block2)
    far1 = far_of(pair_of(mine1, near1), (0, 1))
    acc, mass, kept = update((2, 0), block2, acc, mass)
    acc, mass, (mine2, theirs2) = update((1, 1), cross1, acc, mass, kept=kept)
    near2 = near_of([theirs2], (1, 2))
    last, cross2, mass, near2, far1 = tied((last, cross2, mass, near2, far1))

    front, back = choose_of(
        numbers,
        (close0, last, cross0, cross2, kinds),
        (UPPER, LOWER + 2 * KINDS),
        [
            ((1, 0, 0, 1), 0, UPPER, 0, 0),
            ((2, 3, 3, 2), UPPER, LOWER, 1, 0),
            ((4, 4, 4, 4), 0, 2 * KINDS, 1, LOWER),
        ],
    )
    (block3,) = choose_of(numbers, (close0, last), (GROUP,), [((1, 0, 0, 1), 0, GROUP, 0, 0)])
    front = across(front)
    back = on_line(back, 1)
    far2 = far_of(pair_of(mine2, near2, 1), (1, 2))
    mass, mine3, theirs3, columns3 = both_of(numbers, ((2, 1), (3, 0)), (cross2, block3), expression, low, mass)
    near3 = near_of(theirs3, (2, 3))
    pair3 = pair_of(mine3, near3)
    front, back, mass, pair3, far2 = tied((front, back, mass, pair3, far2))

    mass, mine4, theirs4, columns, block = part_of(numbers, (3, 1), front, back, expression, low, mass)
    mass_far = swapped(mass, 2)
    far3 = far_of(pair3, (2, 3))
    near4 = near_of([theirs4], (3,))
    pair4 = pair_of(mine4, near4)
    kinds = merge_of(numbers, 1, kinds, back)
    kinds_more = on_line(kinds, 2)
    acc, fetched = gather_of(columns3, acc, (cross2, block3), logits)
    mass_far, far3, pair4, kinds_more, acc = tied((mass_far, far3, pair4, kinds_more, acc))
    mass = plus(mass, mass_far)
    mass_near = swapped(mass, 1)
    far4 = far_of(pair4, (3,))
    kinds = merge_of(numbers, 2, kinds, kinds_more)
    kinds_more = across(kinds)
    grad_logits = finish_of(columns, block, fetched, factor, acc, mass, mass_near)
    grad_logits, far3 = tied((grad_logits, far3))
    triples = [(mine0, near0, far0), (mine1, near1, far1), (mine2, near2, far2), (mine3, near3, far3)]
    plan = [((turn, 0), turn) for turn in range(4)] + [((turn, 1), turn + 1) for turn in range(3)]
    result = collect_of(numbers, plan, triples)
    types, table = kinds_of(numbers, kinds, kinds_more, early, cross)
    result = collect_of(numbers, [((3, 1), 0)], [(mine4, near4, far4)], result)
    return (predicted, grad_logits, result, table, types)


def solution(mesh):
    in_specs = (
        P("cells", "spots"),
        P("cells", None),
        P(None, "spots"),
        P("spots"),
        P("spots"),
        P("cells"),
        P("cells"),
    )
    out_specs = (
        P("cells", "spots"),
        P("cells", "spots"),
        P("cells", "spots"),
        P(),
        P(None, "spots"),
    )
    fits = mesh.shape["cells"] == 8 and mesh.shape["spots"] == 4
    return jax.shard_map(
        ladder if fits else general, mesh=mesh, in_specs=in_specs, out_specs=out_specs, check_vma=False
    )
```

```python
import functools
import math

import jax
import jax.numpy as jnp
import numpy as np
from jax import lax
from jax.experimental import pallas as pl
from jax.experimental.pallas import tpu as pltpu
from jax.sharding import PartitionSpec as P

GENES = 2048
NTYPE = 128
LANES = 128
BF = jnp.bfloat16
F32 = jnp.float32
highest = lax.Precision.HIGHEST


def over_rows(left_side, right_side):
    return lax.dot_general(
        left_side, right_side, (((0,), (0,)), ((), ())), preferred_element_type=F32
    )


def over_columns(left_side, right_side):
    return lax.dot_general(
        left_side, right_side, (((1,), (1,)), ((), ())), preferred_element_type=F32
    )


def general(logits, expression, target, density, assignment, labels, counts):
    row_count = logits.shape[0]
    spot_width = logits.shape[1]
    cell_devices = lax.axis_size("cells")
    slot_total = float(row_count * cell_devices)
    scale = float(row_count * cell_devices * spot_width * lax.axis_size("spots"))
    live = (jnp.arange(row_count, dtype=jnp.int32) < counts[0])[:, None]
    raised = jnp.exp(logits)
    row_mass = lax.psum(jnp.sum(raised, axis=1), "spots")
    probs = jnp.where(live, raised / row_mass[:, None], 0.0)
    probs_low = probs.astype(BF)
    one_hot = (labels[:, None] == jnp.arange(NTYPE, dtype=jnp.int32)[None, :]).astype(BF)
    type_total, dens_total = lax.psum((over_rows(one_hot, probs_low), jnp.sum(probs, axis=0)), "cells")
    gene_rows = GENES // cell_devices
    predicted = lax.psum_scatter(
        over_rows(expression, probs_low), "cells", scatter_dimension=0, tiled=True
    )
    target_full = lax.dynamic_slice_in_dim(
        target, lax.axis_index("cells") * gene_rows, gene_rows, 0
    ).astype(F32)
    spot_dot, spot_pred, spot_target = lax.psum(
        (
            jnp.sum(predicted * target_full, axis=0),
            jnp.sum(predicted * predicted, axis=0),
            jnp.sum(target_full * target_full, axis=0),
        ),
        "cells",
    )
    dens_pred = dens_total / slot_total
    sides = jnp.stack([assignment == 0, assignment == 1]).astype(F32)
    inv_spot_pred = lax.rsqrt(spot_pred)
    inv_spot_target = lax.rsqrt(spot_target)
    spot_cosine = spot_dot * inv_spot_pred * inv_spot_target
    columns = jnp.stack(
        [
            jnp.ones_like(density),
            density,
            density * jnp.log(density),
            density * jnp.log(dens_pred),
            dens_pred,
            spot_cosine,
        ]
    )
    slide_part = jnp.dot(sides, columns.T, precision=highest)
    gene_part = jnp.stack(
        [
            jnp.dot(predicted * target_full, sides.T, precision=highest),
            jnp.dot(predicted * predicted, sides.T, precision=highest),
            jnp.dot(target_full * target_full, sides.T, precision=highest),
        ]
    )
    slide_sums, gene_sums = lax.psum((slide_part, gene_part), "spots")
    spot_count, dens_mass, dens_log, cross_log, pred_mass, cosine_sum = [
        slide_sums[:, at] for at in range(6)
    ]
    inv_gene_pred = lax.rsqrt(gene_sums[1])
    inv_gene_target = lax.rsqrt(gene_sums[2])
    gene_cosine = gene_sums[0] * inv_gene_pred * inv_gene_target
    gene_along_target = jnp.dot(inv_gene_pred * inv_gene_target, sides, precision=highest)
    gene_along_pred = jnp.dot(gene_cosine * inv_gene_pred * inv_gene_pred, sides, precision=highest)
    spot_weight = 1.0 / jnp.dot(spot_count, sides, precision=highest)
    spot_along_target = inv_spot_pred * inv_spot_target * spot_weight
    spot_along_pred = spot_cosine * inv_spot_pred * inv_spot_pred * spot_weight
    grad_dens = scale * (
        jnp.dot(1.0 / pred_mass, sides, precision=highest)
        - density / (jnp.dot(dens_mass, sides, precision=highest) * dens_pred)
    )
    grad_pred = scale * (
        -(target_full * gene_along_target - predicted * gene_along_pred) / GENES
        - (target_full * spot_along_target[None, :] - predicted * spot_along_pred[None, :])
    )
    grad_low = lax.all_gather(grad_pred.astype(BF), "cells", axis=0, tiled=True)
    grad_probs = jnp.dot(expression, grad_low, preferred_element_type=F32)
    grad_expr_part = over_columns(probs_low, grad_low)
    gene_loss = lax.psum(jnp.sum(gene_cosine, axis=0), "cells")
    grad_probs = grad_probs + (grad_dens / slot_total)[None, :]
    row_total = lax.psum(jnp.sum(probs * grad_probs, axis=1), "spots")
    grad_logits = probs * (grad_probs - row_total[:, None])
    grad_expression = lax.psum_scatter(grad_expr_part, "spots", scatter_dimension=1, tiled=True)
    divergence = (dens_log - cross_log) / dens_mass - jnp.log(dens_mass) + jnp.log(pred_mass)
    table = jnp.stack([gene_loss / GENES, cosine_sum / spot_count, divergence], axis=1)
    return (predicted.astype(BF), grad_logits, grad_expression, table, type_total * NTYPE)


VMEM = pltpu.MemorySpace.VMEM
HBM = pltpu.MemorySpace.HBM
IN_VMEM = pl.BlockSpec(memory_space=VMEM)
IN_SMEM = pl.BlockSpec(memory_space=pltpu.MemorySpace.SMEM)
IN_PLACE = pl.BlockSpec(memory_space=pl.ANY)
CHUNK = 2 * LANES
MIB = 1024 * 1024
GROUP = GENES // 8
KINDS = NTYPE // 8
PIECES = 4
PAD = 16

FRONT = 144
ROWS = GROUP + KINDS
BACK = ROWS - FRONT
UPPER = 144
LOWER = GROUP - UPPER


def line_at(numbers_ref):
    return numbers_ref[0] // 2


def order_of(line, turn):
    return (line, 1 + line % 2, (line + 2) % 4, 3 - 3 * (line % 2))[turn]


def block_at(numbers_ref, place):
    turn, other = place
    rung = numbers_ref[0] % 2
    return 2 * order_of(line_at(numbers_ref), turn) + (1 - rung if other else rung)


def call(kernel, name, inputs, outputs, scratch=(), aliases=None, limit=8, flops=1024):
    return pl.pallas_call(
        kernel,
        in_specs=[spec for _, spec in inputs],
        out_specs=[spec for _, spec in outputs],
        out_shape=[shape for shape, _ in outputs],
        scratch_shapes=list(scratch),
        input_output_aliases=aliases or {},
        compiler_params=pltpu.CompilerParams(vmem_limit_bytes=limit * MIB),
        cost_estimate=pl.CostEstimate(flops=flops, bytes_accessed=1024, transcendentals=0),
        name=name,
    )(*[array for array, _ in inputs])


def plain(*shape, dtype=F32):
    return jax.ShapeDtypeStruct(shape, dtype)


def pinned(array, space):
    return pltpu.with_memory_space_constraint(array, space)


def to_row(column):
    return jnp.broadcast_to(column, (LANES, LANES)).T[:1]


def to_column(row):
    return jnp.broadcast_to(row, (LANES, LANES)).T[:, :1]


def line_of(at):
    return pl.ds(at * LANES, LANES)


def columns_of(at):
    return pl.ds(pl.multiple_of(at * GROUP, GROUP), GROUP)


def packed_row(values):
    lane = lax.broadcasted_iota(jnp.int32, (1, LANES), 1)
    row = jnp.zeros((1, LANES), F32)
    for at, value in enumerate(values):
        row = jnp.where(lane == at, value, row)
    return row


def row_sum(row):
    return jnp.sum(row, axis=1, keepdims=True)


def mass_kernel(logits_ref, raised_ref, mass_ref, sems):
    lines = mass_ref.shape[0]
    copies = [
        pltpu.make_async_copy(logits_ref.at[line_of(at)], raised_ref.at[line_of(at)], sems.at[at])
        for at in range(lines)
    ]
    for copy in copies:
        copy.start()
    for at, copy in enumerate(copies):
        copy.wait()
        raised = jnp.exp(raised_ref[line_of(at), :])
        raised_ref[line_of(at), :] = raised
        mass_ref[pl.ds(at, 1), :] = to_row(jnp.sum(raised, axis=1, keepdims=True))


def mass_of(logits):
    rows, width = logits.shape
    lines = rows // LANES
    return call(
        mass_kernel,
        "mass",
        [(pinned(logits, HBM), IN_PLACE)],
        [(VMEM((rows, width), F32), IN_VMEM), (plain(lines, LANES), IN_VMEM)],
        [pltpu.SemaphoreType.DMA((lines,))],
    )


def left_kernel(places, numbers_ref, expr_ref, labels_ref, left_ref, held, sems):
    _, _, cells = left_ref.shape

    def copy(n):
        return pltpu.make_async_copy(
            expr_ref.at[:, columns_of(block_at(numbers_ref, places[n]))], held.at[n % 2], sems.at[n % 2]
        )

    copy(0).start()
    for n, place in enumerate(places):
        if n + 1 < len(places):
            copy(n + 1).start()
        kind = lax.broadcasted_iota(jnp.int32, (KINDS, cells), 0) + block_at(numbers_ref, place) * KINDS
        left_ref[n, GROUP:, :] = jnp.where(kind == labels_ref[...], 1.0, 0.0).astype(BF)
        copy(n).wait()
        left_ref[n, :GROUP, :] = held[n % 2].T


def left_of(numbers, places, expression, labels):
    cells = expression.shape[0]
    count = len(places)
    return call(
        functools.partial(left_kernel, places),
        "left",
        [(numbers, IN_SMEM), (pinned(expression, HBM), IN_PLACE), (labels, IN_VMEM)],
        [(VMEM((count, GROUP + KINDS, cells), BF), IN_VMEM)],
        [pltpu.VMEM((2, cells, GROUP), BF), pltpu.SemaphoreType.DMA((2,))],
    )[0]


def first_kernel(counts_ref, raised_ref, near_ref, far_ref, left_ref, low_ref, dens_ref, factor_ref, front_ref, back_ref, total):
    cells = raised_ref.shape[0]
    lines = cells // LANES
    row = lax.broadcasted_iota(jnp.int32, (lines, LANES), 0) * LANES + lax.broadcasted_iota(
        jnp.int32, (lines, LANES), 1
    )
    factor_ref[...] = jnp.where(row < counts_ref[0], 1.0 / (near_ref[...] + far_ref[...]), 0.0)
    mass = 0.0
    for at in range(lines):
        probs = raised_ref[line_of(at), :] * to_column(factor_ref[pl.ds(at, 1), :])
        low_ref[line_of(at), :] = probs.astype(BF)
        mass = mass + jnp.sum(probs, axis=0, keepdims=True)
        if at % 2:
            part = pl.ds((at // 2) * CHUNK, CHUNK)
            more = jnp.dot(left_ref[0, :, part], low_ref[part, :], preferred_element_type=F32)
            if at == 1:
                total[...] = more
            elif at + 1 < lines:
                total[...] += more
            else:
                whole = (total[...] + more).astype(BF)
                front_ref[...] = whole[:FRONT]
                back_ref[...] = whole[FRONT:]
    dens_ref[...] = mass


def first_of(counts, raised, near, far, left):
    cells, width = raised.shape
    rows = left.shape[1]
    return call(
        first_kernel,
        "first",
        [(counts, IN_SMEM)] + [(a, IN_VMEM) for a in (raised, near, far, left)],
        [(VMEM((cells, width), BF), IN_VMEM), (plain(1, width), IN_VMEM)]
        + [(plain(*near.shape), IN_VMEM), (plain(FRONT, width, dtype=BF), IN_VMEM), (plain(BACK, width, dtype=BF), IN_VMEM)],
        [pltpu.VMEM((rows, width), F32)],
    )


def blocks_kernel(which, left_ref, low_ref, *out_refs):
    width = low_ref.shape[1]
    tile = width // 3
    for n, out_ref in zip(which, out_refs):

        def step(at, _, n=n, out_ref=out_ref):
            columns = pl.ds(pl.multiple_of(at * tile, LANES), tile)
            out_ref[:, columns] = jnp.dot(
                left_ref[n], low_ref[:, columns], preferred_element_type=F32
            ).astype(out_ref.dtype)
            return 0

        lax.fori_loop(0, 3, step, 0)


def blocks_of(left, low, which, dtype):
    cells, width = low.shape
    rows = left.shape[1]
    return call(
        functools.partial(blocks_kernel, which),
        "blocks",
        [(left, IN_VMEM), (low, IN_VMEM)],
        [(plain(rows, width, dtype=dtype), IN_VMEM)] * len(which),
        limit=6,
    )


def early_kernel(numbers_ref, target_ref, density_ref, side_ref, spot_ref, own_ref, sums_ref, held, sems):
    genes = target_ref.shape[0]
    count = genes // GROUP

    def copy(n):
        rows = pl.ds(n * GROUP, GROUP)
        return pltpu.make_async_copy(target_ref.at[rows], held.at[n % 2], sems.at[n % 2])

    mine = pltpu.make_async_copy(target_ref.at[columns_of(numbers_ref[0])], own_ref, sems.at[2])
    mine.start()
    copy(0).start()
    spot_ref[...] = jnp.zeros_like(spot_ref)
    for n in range(count):
        if n + 1 < count:
            copy(n + 1).start()
        copy(n).wait()
        target = held[n % 2].astype(F32)
        spot_ref[...] += jnp.sum(target * target, axis=0, keepdims=True)
    mine.wait()
    side = side_ref[...]
    other = 1.0 - side
    density = density_ref[...]
    target = own_ref[...].astype(F32)
    square = target * target
    lane = lax.broadcasted_iota(jnp.int32, (GROUP, LANES), 1)
    columns = jnp.where(
        lane == 0,
        jnp.sum(square * other, axis=1, keepdims=True),
        jnp.where(lane == 1, jnp.sum(square * side, axis=1, keepdims=True), 0.0),
    )
    sums_ref[0:2, :] = columns.T[:2]
    logged = density * jnp.log(density)
    known = packed_row([row_sum(value * part) for value in (1.0, density, logged) for part in (other, side)])
    sums_ref[2:3, :] = jnp.concatenate([known, jnp.zeros_like(known)], axis=1)


def early_of(numbers, target, density, side):
    width = target.shape[1]
    return call(
        early_kernel,
        "early",
        [(numbers, IN_SMEM), (pinned(target, HBM), IN_PLACE), (density, IN_VMEM), (side, IN_VMEM)],
        [(plain(1, width), IN_VMEM), (VMEM((GROUP, width), BF), IN_VMEM), (plain(3, GROUP), IN_VMEM)],
        [pltpu.VMEM((2, GROUP, width), BF), pltpu.SemaphoreType.DMA((3,))],
        limit=16,
    )


def half_kernel(kept_ref, front_ref, half_ref, front_out, back_out):
    half_ref[...] = kept_ref[...]
    half_ref[:FRONT] += front_ref[...].astype(F32)
    front_out[...] = half_ref[:FRONT].astype(BF)
    back_out[...] = half_ref[FRONT:].astype(BF)


def half_of(kept, front):
    width = kept.shape[1]
    return call(
        half_kernel,
        "half",
        [(kept, IN_VMEM), (front, IN_VMEM)],
        [(plain(*kept.shape), IN_VMEM)] + [(plain(rows, width, dtype=BF), IN_VMEM) for rows in (FRONT, BACK)],
        limit=10,
    )


def join_kernel(lines, numbers_ref, part_ref, back_ref, out_ref):
    out_ref[:FRONT] = part_ref[:FRONT].astype(BF)
    line = line_at(numbers_ref)
    here = jnp.logical_or(line == lines[0], line == lines[1])

    @pl.when(here)
    def _():
        out_ref[FRONT:] = (part_ref[FRONT:] + back_ref[...].astype(F32)).astype(BF)

    @pl.when(jnp.logical_not(here))
    def _():
        out_ref[FRONT:] = part_ref[FRONT:].astype(BF)


def join_of(numbers, part, back, lines):
    return call(
        functools.partial(join_kernel, lines),
        "join",
        [(numbers, IN_SMEM), (part, IN_VMEM), (back, IN_VMEM)],
        [(plain(*part.shape, dtype=BF), IN_VMEM)],
        limit=8,
    )[0]


def step_kernel(kept_ref, cross_ref, front_ref, back_ref, out_ref, front_out, back_out):
    for start, more_ref in ((0, front_ref), (FRONT, back_ref)):
        rows = pl.ds(start, more_ref.shape[0])
        out_ref[rows, :] = (
            kept_ref[rows, :] + cross_ref[rows, :].astype(F32) + more_ref[...].astype(F32)
        ).astype(BF)
    front_out[...] = out_ref[:FRONT]
    back_out[...] = out_ref[FRONT:]


def step_of(kept, cross, front, back):
    width = kept.shape[1]
    return call(
        step_kernel,
        "step",
        [(a, IN_VMEM) for a in (kept, cross, front, back)],
        [(plain(rows, width, dtype=BF), IN_VMEM) for rows in (ROWS, FRONT, BACK)],
        limit=12,
    )


def in_middle(numbers_ref):
    line = line_at(numbers_ref)
    return jnp.logical_or(line == 1, line == 2)


def turn_kernel(numbers_ref, kept_ref, cross_ref, early_ref, inner_ref, front_ref, back_ref, near_out, middle_out):
    middle = in_middle(numbers_ref)

    @pl.when(middle)
    def _():
        near_out[:FRONT] = (early_ref[:FRONT] + front_ref[...].astype(F32)).astype(BF)
        near_out[FRONT:] = (early_ref[FRONT:] + back_ref[...].astype(F32)).astype(BF)
        middle_out[...] = (kept_ref[...] + cross_ref[...].astype(F32) + inner_ref[...].astype(F32)).astype(BF)

    @pl.when(jnp.logical_not(middle))
    def _():
        near_out[...] = (kept_ref[...] + cross_ref[...].astype(F32)).astype(BF)
        middle_out[...] = near_out[...]


def turn_of(numbers, kept, cross, early, inner, front, back):
    return call(
        turn_kernel,
        "turn",
        [(numbers, IN_SMEM)] + [(a, IN_VMEM) for a in (kept, cross, early, inner, front, back)],
        [(plain(*inner.shape, dtype=BF), IN_VMEM)] * 2,
        limit=15,
    )


def sums_kernel(
    kept_ref, cross_ref, up_ref, down_ref, target_ref, side_ref, dens_ref,
    total_ref, low_ref, kinds_ref, gene_ref, spot_ref,
):
    total = (
        kept_ref[...] + cross_ref[...].astype(F32) + up_ref[...].astype(F32) + down_ref[...].astype(F32)
    )
    pred = total[:GROUP]
    total_ref[...] = pred
    kinds_ref[...] = total[GROUP:].astype(BF)
    low_ref[...] = pred.astype(BF)
    dot = pred * target_ref[...].astype(F32)
    square = pred * pred
    side = side_ref[...]
    spot_ref[0:1, :] = jnp.sum(dot, axis=0, keepdims=True)
    spot_ref[1:2, :] = jnp.sum(square, axis=0, keepdims=True)
    spot_ref[2:3, :] = dens_ref[...]
    sums = [
        jnp.sum(dot * (1.0 - side), axis=1, keepdims=True),
        jnp.sum(dot * side, axis=1, keepdims=True),
        jnp.sum(square * (1.0 - side), axis=1, keepdims=True),
        jnp.sum(square * side, axis=1, keepdims=True),
    ]
    lane = lax.broadcasted_iota(jnp.int32, (GROUP, LANES), 1)
    packed = jnp.zeros((GROUP, LANES), F32)
    for place, column in enumerate(sums):
        packed = jnp.where(lane == place, column, packed)
    gene_ref[...] = packed.T[:4]


def sums_of(kept, *inputs):
    rows, width = kept.shape
    return call(
        sums_kernel,
        "sums",
        [(a, IN_VMEM) for a in (kept, *inputs)],
        [(VMEM((GROUP, width), F32), IN_VMEM), (plain(GROUP, width, dtype=BF), IN_VMEM)]
        + [(plain(KINDS, width, dtype=BF), IN_VMEM)]
        + [(plain(4, GROUP), IN_VMEM), (plain(3, width), IN_VMEM)],
        limit=16,
    )


def put_sum(ref, start, value):
    high = value.astype(BF).astype(F32)
    middle = (value - high).astype(BF).astype(F32)
    low = (value - high) - middle
    row = lax.broadcasted_iota(jnp.int32, (KINDS, LANES), 0)
    tile = jnp.where(row == 0, high, jnp.where(row == 1, middle, jnp.where(row == 2, low, 0.0)))
    ref[start:, :] = jnp.zeros((KINDS, ref.shape[1]), BF)
    ref[start:, :LANES] = tile.astype(BF)


def get_sum(ref, start):
    tile = ref[start:, :LANES].astype(F32)
    return tile[0:1] + tile[1:2] + tile[2:3]


def grads_kernel(
    scale, slots, total_ref, target_ref, side_ref, density_ref, gene_ref, gene_more_ref, early_ref, spot_ref, spot_target_ref,
    more0_ref, more1_ref, more2_ref, kinds_ref, out_ref, dens_ref, cross_ref, kinds_out
):
    side = side_ref[...]
    other = 1.0 - side
    spot = spot_ref[...] + more0_ref[...] + more1_ref[...] + more2_ref[...]
    inv_spot_pred = lax.rsqrt(spot[1:2])
    inv_spot_target = lax.rsqrt(spot_target_ref[...])
    cosine = spot[0:1] * inv_spot_pred * inv_spot_target
    known = early_ref[2:3, :]
    weight = scale / (other * known[:, 0:1] + side * known[:, 1:2])
    spot_along_target = inv_spot_pred * inv_spot_target * weight
    spot_along_pred = cosine * inv_spot_pred * inv_spot_pred * weight
    gene = gene_ref[...] + gene_more_ref[...]
    inv_gene_pred = lax.rsqrt(gene[2:4])
    inv_gene_target = lax.rsqrt(early_ref[0:2, :])
    gene_cosine = gene[0:2] * inv_gene_pred * inv_gene_target
    along = jnp.concatenate(
        [
            (scale / GENES) * inv_gene_pred * inv_gene_target,
            (scale / GENES) * gene_cosine * inv_gene_pred * inv_gene_pred,
            jnp.zeros((LANES - 4, GROUP), F32),
        ],
        axis=0,
    ).T
    along_target = along[:, 0:1] * other + along[:, 1:2] * side + spot_along_target
    along_pred = along[:, 2:3] * other + along[:, 3:4] * side + spot_along_pred
    out_ref[...] = (total_ref[...] * along_pred - target_ref[...].astype(F32) * along_target).astype(BF)
    dens_pred = spot[2:3] / slots
    dens_ref[...] = dens_pred
    cross = density_ref[...] * jnp.log(dens_pred)
    cross_ref[...] = packed_row([row_sum(value * part) for value in (cross, dens_pred, cosine) for part in (other, side)])
    kinds_out[:KINDS] = kinds_ref[...]
    put_sum(kinds_out, KINDS, packed_row([row_sum(gene_cosine[0:1]), row_sum(gene_cosine[1:2])]))


def grads_of(scale, slots, total, *inputs):
    rows, width = total.shape
    return call(
        functools.partial(grads_kernel, scale, slots),
        "grads",
        [(a, IN_VMEM) for a in (total, *inputs)],
        [(plain(rows, width, dtype=BF), IN_VMEM), (plain(1, width), IN_VMEM)]
        + [(plain(1, LANES), IN_VMEM), (plain(2 * KINDS, width, dtype=BF), IN_VMEM)],
        limit=14,
    )


def density_kernel(scale, slots, early_ref, cross_ref, cross_more_ref, side_ref, density_ref, dens_ref, out_ref, cross_out):
    side = side_ref[...]
    other = 1.0 - side
    known = early_ref[2:3, :]
    cross = cross_ref[...] + cross_more_ref[...]
    cross_out[...] = cross
    inverse = other / cross[:, 2:3] + side / cross[:, 3:4]
    dens_mass = other * known[:, 2:3] + side * known[:, 3:4]
    out_ref[...] = (scale / slots) * (inverse - density_ref[...] / (dens_mass * dens_ref[...]))


def density_of(scale, slots, early, cross, cross_more, side, density, dens):
    return call(
        functools.partial(density_kernel, scale, slots),
        "density",
        [(a, IN_VMEM) for a in (early, cross, cross_more, side, density, dens)],
        [(plain(*side.shape), IN_VMEM), (plain(1, LANES), IN_VMEM)],
    )


def choose_kernel(plan, numbers_ref, *refs):
    count = max(max(choices) for choices, _, _, _, _ in plan) + 1
    sources, out_refs, sems = refs[:count], refs[count:-1], refs[-1]
    line = line_at(numbers_ref)
    for place in range(4):

        @pl.when(line == place)
        def _(place=place):
            copies = [
                pltpu.make_async_copy(
                    sources[choices[place]].at[pl.ds(start, rows)], out_refs[out].at[pl.ds(to, rows)], sems.at[n]
                )
                for n, (choices, start, rows, out, to) in enumerate(plan)
            ]
            for copy in copies:
                copy.start()
            for copy in copies:
                copy.wait()


def choose_of(numbers, arrays, outputs, plan):
    width = arrays[0].shape[1]
    return call(
        functools.partial(choose_kernel, plan),
        "choose",
        [(numbers, IN_SMEM)] + [(a, IN_PLACE) for a in arrays],
        [(plain(rows, width, dtype=BF), IN_PLACE) for rows in outputs],
        [pltpu.SemaphoreType.DMA((len(plan),))],
    )


def mine_at(numbers_ref, turn):
    return order_of(line_at(numbers_ref), turn) % 2 == numbers_ref[1] % 2


def keep(numbers_ref, turn, grads, mine_ref, *theirs_refs):
    mine = mine_at(numbers_ref, turn)

    @pl.when(mine)
    def _():
        mine_ref[...] = grads[...]

    @pl.when(jnp.logical_not(mine))
    def _():
        depth = theirs_refs[0].shape[0]
        for n, theirs_ref in enumerate(theirs_refs):
            theirs_ref[...] = grads[pl.ds(n * depth, depth), :].astype(BF)


def update_kernel(start, place, numbers_ref, expr_ref, low_ref, acc_ref, mass_ref, block_ref, *refs):
    acc_out, mass_out, mine_ref, theirs_ref, held, turned, grads, sem = refs[-8:]
    cells = low_ref.shape[0]
    copy = pltpu.make_async_copy(expr_ref.at[:, columns_of(block_at(numbers_ref, place))], held, sem)
    copy.start()
    turned[...] = block_ref[...].T
    copy.wait()
    for at in range(cells // CHUNK):
        part = pl.ds(at * CHUNK, CHUNK)
        expr = held[part, :]
        low = low_ref[part, :]
        more = jnp.dot(expr, block_ref[...], preferred_element_type=F32)
        grad = jnp.dot(low, turned[...], preferred_element_type=F32)
        grads[part, :] = grad
        mass = jnp.sum(expr.astype(F32) * grad, axis=1, keepdims=True)
        if start:
            dens = acc_ref[...]
            acc_out[part, :] = more + dens
            mass = mass + jnp.sum(low.astype(F32) * dens, axis=1, keepdims=True)
        else:
            acc_out[part, :] += more
        for half in range(CHUNK // LANES):
            line = pl.ds(at * (CHUNK // LANES) + half, 1)
            row = to_row(mass[half * LANES : (half + 1) * LANES])
            mass_out[line, :] = row if start else row + mass_ref[line, :]
    keep(numbers_ref, place[0], grads, mine_ref, theirs_ref)


def update_of(numbers, place, block, expression, low, acc, mass, start=False, kept=()):
    cells, width = low.shape
    inputs = [(numbers, IN_SMEM), (pinned(expression, HBM), IN_PLACE)]
    inputs += [(a, IN_VMEM) for a in (low, acc, mass, block, *kept)]
    aliases = {} if start else {3: 0}
    if kept:
        aliases |= {6: 2, 7: 3}
    acc, mass, *kept = call(
        functools.partial(update_kernel, start, place),
        "update",
        inputs,
        [(VMEM((cells, width), F32), IN_VMEM), (plain(*mass.shape), IN_VMEM)]
        + [(VMEM((cells, GROUP), F32), IN_VMEM), (VMEM((cells, GROUP), BF), IN_VMEM)],
        [
            pltpu.VMEM((cells, GROUP), BF),
            pltpu.VMEM((width, GROUP), BF),
            pltpu.VMEM((cells, GROUP), F32),
            pltpu.SemaphoreType.DMA,
        ],
        aliases=aliases,
        limit=6,
    )
    return acc, mass, kept


def both_kernel(places, numbers_ref, expr_ref, low_ref, mass_ref, first_ref, second_ref, *refs):
    mass_out, mine_ref, front_ref, back_ref, held, turned, grads, sems = refs
    cells = low_ref.shape[0]
    copies = [
        pltpu.make_async_copy(
            expr_ref.at[:, columns_of(block_at(numbers_ref, place))], held.at[n], sems.at[n]
        )
        for n, place in enumerate(places)
    ]
    for copy in copies:
        copy.start()
    for n, block_ref in enumerate((first_ref, second_ref)):
        turned[:, n * GROUP : (n + 1) * GROUP] = block_ref[...].T
    for copy in copies:
        copy.wait()
    for at in range(cells // CHUNK):
        part = pl.ds(at * CHUNK, CHUNK)
        grad = jnp.dot(low_ref[part, :], turned[...], preferred_element_type=F32)
        mass = 0.0
        for n in range(2):
            one = grad[:, n * GROUP : (n + 1) * GROUP]
            grads[n, part, :] = one
            mass = mass + jnp.sum(held[n, part, :].astype(F32) * one, axis=1, keepdims=True)
        for half in range(CHUNK // LANES):
            line = pl.ds(at * (CHUNK // LANES) + half, 1)
            mass_out[line, :] = mass_ref[line, :] + to_row(mass[half * LANES : (half + 1) * LANES])
    for n, (turn, _) in enumerate(places):
        keep(numbers_ref, turn, grads.at[n], mine_ref, front_ref, back_ref)


def both_of(numbers, places, blocks, expression, low, mass):
    cells, width = low.shape
    mass, mine, front, back, columns = call(
        functools.partial(both_kernel, places),
        "both",
        [(numbers, IN_SMEM), (pinned(expression, HBM), IN_PLACE)] + [(a, IN_VMEM) for a in (low, mass, *blocks)],
        [(plain(*mass.shape), IN_VMEM), (VMEM((cells, GROUP), F32), IN_VMEM)]
        + [(plain(cells // 2, GROUP, dtype=BF), IN_VMEM)] * 2
        + [(VMEM((2, cells, GROUP), BF), IN_VMEM)],
        [
            pltpu.VMEM((width, 2 * GROUP), BF),
            pltpu.VMEM((2, cells, GROUP), F32),
            pltpu.SemaphoreType.DMA((2,)),
        ],
        limit=10,
    )
    return mass, mine, (front, back), columns


def gather_kernel(columns_ref, acc_ref, first_ref, second_ref, logits_ref, *refs):
    acc_out, *fetched, sems = refs
    cells = acc_ref.shape[0]
    depth = fetched[0].shape[0]
    copies = [
        pltpu.make_async_copy(logits_ref.at[pl.ds(n * depth, depth)], piece, sems.at[n])
        for n, piece in enumerate(fetched)
    ]
    for copy in copies:
        copy.start()
    blocks = (first_ref, second_ref)
    for at in range(cells // CHUNK):
        part = pl.ds(at * CHUNK, CHUNK)
        total = acc_out[part, :]
        for n, block_ref in enumerate(blocks):
            total = total + jnp.dot(columns_ref[n, part, :], block_ref[...], preferred_element_type=F32)
        acc_out[part, :] = total
    for copy in copies:
        copy.wait()


def gather_of(columns, acc, blocks, logits):
    cells, width = acc.shape
    acc, *pieces = call(
        gather_kernel,
        "gather",
        [(a, IN_VMEM) for a in (columns, acc, *blocks)] + [(pinned(logits, HBM), IN_PLACE)],
        [(VMEM((cells, width), F32), IN_VMEM)]
        + [(VMEM((cells // PIECES, width), F32), IN_VMEM)] * PIECES,
        [pltpu.SemaphoreType.DMA((PIECES,))],
        aliases={1: 0},
        limit=5,
    )
    return acc, pieces


def part_kernel(
    place, numbers_ref, expr_ref, low_ref, mass_ref, front_ref, back_ref, *refs
):
    mass_out, mine_ref, theirs_ref, held, block, turned, grads, sem = refs
    cells = low_ref.shape[0]
    copy = pltpu.make_async_copy(expr_ref.at[:, columns_of(block_at(numbers_ref, place))], held, sem)
    copy.start()
    block[:UPPER] = front_ref[...]
    block[UPPER:] = back_ref[:LOWER]
    turned[...] = block[...].T
    copy.wait()
    for at in range(cells // CHUNK):
        part = pl.ds(at * CHUNK, CHUNK)
        grad = jnp.dot(low_ref[part, :], turned[...], preferred_element_type=F32)
        grads[part, :] = grad
        mass = jnp.sum(held[part, :].astype(F32) * grad, axis=1, keepdims=True)
        for half in range(CHUNK // LANES):
            line = pl.ds(at * (CHUNK // LANES) + half, 1)
            mass_out[line, :] = mass_ref[line, :] + to_row(mass[half * LANES : (half + 1) * LANES])
    keep(numbers_ref, place[0], grads, mine_ref, theirs_ref)


def part_of(numbers, place, front, back, expression, low, mass):
    cells, width = low.shape
    return call(
        functools.partial(part_kernel, place),
        "part",
        [(numbers, IN_SMEM), (pinned(expression, HBM), IN_PLACE)]
        + [(a, IN_VMEM) for a in (low, mass, front, back)],
        [(plain(*mass.shape), IN_VMEM)]
        + [(VMEM((cells, GROUP), F32), IN_VMEM), (VMEM((cells, GROUP), BF), IN_VMEM)]
        + [(VMEM((cells, GROUP), BF), IN_VMEM), (VMEM((GROUP, width), BF), IN_VMEM)],
        [
            pltpu.VMEM((width, GROUP), BF),
            pltpu.VMEM((cells, GROUP), F32),
            pltpu.SemaphoreType.DMA,
        ],
        limit=7,
    )


def pair_kernel(count, mine_ref, *refs):
    near_refs, out_refs = refs[:-count], refs[-count:]
    rows = mine_ref.shape[0]
    pieces = max(len(near_refs), count)
    depth = rows // pieces
    for n in range(pieces):
        near_ref = near_refs[n * len(near_refs) // pieces]
        out_ref = out_refs[n * count // pieces]
        near_at = n * depth % near_ref.shape[0]
        out_at = n * depth % (rows // count)
        out_ref[pl.ds(out_at, depth), :] = (
            mine_ref[pl.ds(n * depth, depth), :] + near_ref[pl.ds(near_at, depth), :].astype(F32)
        ).astype(BF)
    if count == 1:
        out_refs[0][rows:] = jnp.zeros((PAD, mine_ref.shape[1]), BF)


def pair_of(mine, nears, count=1):
    rows, columns = mine.shape
    return call(
        functools.partial(pair_kernel, count),
        "pair",
        [(mine, IN_VMEM)] + [(near, IN_VMEM) for near in nears],
        [(plain(rows // count + (PAD if count == 1 else 0), columns, dtype=BF), IN_VMEM)] * count,
        limit=5,
    )


def collect_kernel(plan, counts, numbers_ref, *refs):
    out_ref, total, near, far, sems = refs[-5:]
    triples, at = [], 0
    for near_count, far_count in counts:
        end = at + 1 + near_count
        triples.append((refs[at], refs[at + 1 : end], refs[end : end + far_count]))
        at = end + far_count
    rows = total.shape[1]
    rung = numbers_ref[0] % 2

    def loads(slot, pair):
        mine_ref, near_refs, far_refs = triples[pair]
        copies = [pltpu.make_async_copy(mine_ref, total.at[slot], sems.at[slot, 0])]
        for sources, buffer in ((near_refs, near), (far_refs, far)):
            depth = rows // len(sources)
            for n, source in enumerate(sources):
                copies.append(
                    pltpu.make_async_copy(
                        source.at[pl.ds(0, depth)],
                        buffer.at[slot, pl.ds(n * depth, depth)],
                        sems.at[slot, 1 + len(copies)],
                    )
                )
        return copies

    for turn in sorted({turn for (turn, _), _ in plan}):
        entries = [(other, pair) for (at, other), pair in plan if at == turn]

        @pl.when(order_of(line_at(numbers_ref), turn) == numbers_ref[1])
        def _(entries=entries):
            for slot, (_, pair) in enumerate(entries):
                for copy in loads(slot, pair):
                    copy.start()
            stores = []
            for slot, (other, pair) in enumerate(entries):
                for copy in loads(slot, pair):
                    copy.wait()
                total[slot] += near[slot].astype(F32) + far[slot].astype(F32)
                columns = columns_of(1 - rung if other else rung)
                stores.append(pltpu.make_async_copy(total.at[slot], out_ref.at[:, columns], sems.at[slot, 1]))
                stores[-1].start()
            for store in stores:
                store.wait()


def collect_of(numbers, plan, triples, result=None):
    cells = triples[0][0].shape[0]
    depth = max(sum(1 for (at, _), _ in plan if at == turn) for (turn, _), _ in plan)
    inputs = [(numbers, IN_SMEM)]
    inputs += [(a, IN_PLACE) for mine, nears, fars in triples for a in (mine, *nears, *fars)]
    aliases = {}
    if result is not None:
        aliases = {len(inputs): 0}
        inputs.append((result, IN_PLACE))
    return call(
        functools.partial(collect_kernel, plan, [(len(nears), len(fars)) for _, nears, fars in triples]),
        "collect",
        inputs,
        [(HBM((cells, 2 * GROUP), F32), IN_PLACE)],
        [
            pltpu.VMEM((depth, cells, GROUP), F32),
            pltpu.VMEM((depth, cells, GROUP), BF),
            pltpu.VMEM((depth, cells, GROUP), BF),
            pltpu.SemaphoreType.DMA((depth, 6)),
        ],
        aliases=aliases,
        limit=1 + 3 * depth,
    )[0]


def plus_kernel(first_ref, second_ref, out_ref):
    out_ref[...] = first_ref[...] + second_ref[...]


def plus(first, second):
    return call(
        plus_kernel,
        "plus",
        [(first, IN_VMEM), (second, IN_VMEM)],
        [(plain(*first.shape), IN_VMEM)],
        limit=1,
    )[0]


def finish_kernel(columns_ref, block_ref, factor_ref, acc_ref, mass_ref, more_ref, *refs):
    *pieces, out_ref, held, sems = refs
    lines = mass_ref.shape[0]
    share = lines // len(pieces)
    depth = held.shape[0]
    copies = []
    for at in range(lines):
        if at >= depth:
            copies[at - depth].wait()
        one = pl.ds(at, 1)
        rows = line_of(at)
        grad = acc_ref[rows, :] + jnp.dot(columns_ref[rows, :], block_ref[...], preferred_element_type=F32)
        logits = pieces[at // share][line_of(at % share), :]
        probs = jnp.exp(logits) * to_column(factor_ref[one, :])
        held[at % depth] = probs * (grad - to_column(mass_ref[one, :] + more_ref[one, :]))
        copies.append(pltpu.make_async_copy(held.at[at % depth], out_ref.at[rows], sems.at[at % depth]))
        copies[-1].start()
    for copy in copies[-depth:]:
        copy.wait()


def finish_of(columns, block, pieces, factor, acc, mass, more):
    rows, width = acc.shape
    depth = 4
    inputs = (columns, block, factor, acc, mass, more, *pieces)
    return call(
        finish_kernel,
        "finish",
        [(a, IN_VMEM) for a in inputs],
        [(HBM((rows, width), F32), IN_PLACE)],
        [pltpu.VMEM((depth, LANES, width), F32), pltpu.SemaphoreType.DMA((depth,))],
        limit=6,
        flops=1024,
    )[0]


def merge_kernel(bit, numbers_ref, mine_ref, theirs_ref, out_ref):
    rows = mine_ref.shape[0] - KINDS
    skip = theirs_ref.shape[0] - mine_ref.shape[0]
    own = (numbers_ref[0] // 2**bit) % 2
    for value in range(2):

        @pl.when(own == value)
        def _(value=value):
            out_ref[value * rows : (value + 1) * rows, :] = mine_ref[:rows]
            out_ref[(1 - value) * rows : (2 - value) * rows, :] = theirs_ref[skip : skip + rows]

    put_sum(out_ref, 2 * rows, get_sum(mine_ref, rows) + get_sum(theirs_ref, skip + rows))


def merge_of(numbers, bit, mine, theirs):
    rows, width = mine.shape
    return call(
        functools.partial(merge_kernel, bit),
        "merge",
        [(numbers, IN_SMEM), (mine, IN_VMEM), (theirs, IN_VMEM)],
        [(plain(2 * rows - KINDS, width, dtype=BF), IN_VMEM)],
        limit=2,
    )[0]


def kinds_kernel(numbers_ref, mine_ref, theirs_ref, early_ref, cross_ref, out_ref, table_ref, held, sem):
    own = numbers_ref[0] % 2
    for low_bit in range(2):
        for middle in range(2):
            for high in range(2):
                source = (2 * high + middle) * KINDS
                block = (4 * high + 2 * middle + low_bit) * KINDS

                @pl.when(own == low_bit)
                def _(source=source, block=block):
                    held[block : block + KINDS, :] = mine_ref[source : source + KINDS, :].astype(F32) * NTYPE

                @pl.when(own != low_bit)
                def _(source=source, block=block):
                    held[block : block + KINDS, :] = theirs_ref[source : source + KINDS, :].astype(F32) * NTYPE

    copy = pltpu.make_async_copy(held, out_ref, sem)
    copy.start()
    loss = get_sum(mine_ref, 4 * KINDS) + get_sum(theirs_ref, 4 * KINDS)
    known = early_ref[2:3, :LANES]
    cross = cross_ref[...]
    for k in range(2):
        one = lambda row, at: row[:, 2 * at + k : 2 * at + k + 1]
        count, dens_mass, dens_log = one(known, 0), one(known, 1), one(known, 2)
        cross_log, pred_mass, cosine_sum = one(cross, 0), one(cross, 1), one(cross, 2)
        divergence = (dens_log - cross_log) / dens_mass - jnp.log(dens_mass) + jnp.log(pred_mass)
        row = packed_row([loss[:, k : k + 1] / GENES, cosine_sum / count, divergence])
        table_ref[k : k + 1, :] = row[:, :3]
    copy.wait()


def kinds_of(numbers, mine, theirs, early, cross):
    width = mine.shape[1]
    return call(
        kinds_kernel,
        "kinds",
        [(numbers, IN_SMEM)] + [(a, IN_VMEM) for a in (mine, theirs, early, cross)],
        [(HBM((NTYPE, width), F32), IN_PLACE), (plain(2, 3), IN_VMEM)],
        [pltpu.VMEM((NTYPE, width), F32), pltpu.SemaphoreType.DMA],
        limit=3,
    )


tied = lax.optimization_barrier


def across(array):
    return lax.ppermute(array, "cells", [(at, at ^ 1) for at in range(8)])


def inward(array):
    return lax.ppermute(array, "cells", [(at, at ^ 2) for at in (0, 1, 6, 7)])


def between(array):
    return lax.ppermute(array, "cells", [(at, at ^ 6) for at in range(2, 6)])


def outward(array):
    return lax.ppermute(array, "cells", [(at ^ 2, at) for at in (0, 1, 6, 7)])


def on_line(array, step):
    return lax.ppermute(array, "cells", [(at, at ^ (2 * step)) for at in range(8)])


def swapped(array, step):
    return lax.ppermute(array, "spots", [(at, at ^ step) for at in range(4)])


def near_of(theirs, turns):
    pairs = [
        (at * 4 + place, at * 4 + (place ^ 1))
        for at in range(8)
        for place in range(4)
        if any(order_of(at // 2, turn) % 2 != place % 2 for turn in turns)
    ]
    return [lax.ppermute(piece, ("cells", "spots"), pairs) for piece in theirs]


def far_of(pair, turns):
    pairs = []
    for at in range(8):
        for owner in (order_of(at // 2, turn) for turn in turns):
            pairs.append((at * 4 + (owner ^ 2), at * 4 + owner))
    return [lax.ppermute(piece, ("cells", "spots"), pairs) for piece in pair]


def ladder(logits, expression, target, density, assignment, labels, counts):
    cells, width = logits.shape
    slots = float(cells * lax.axis_size("cells"))
    scale = float(cells * lax.axis_size("cells") * width * lax.axis_size("spots"))
    numbers = jnp.stack([lax.axis_index("cells"), lax.axis_index("spots")]).astype(jnp.int32)
    logits, numbers = tied((logits, numbers))
    side = (assignment == 1).astype(F32)[None, :]
    density = density[None, :]
    labels = labels[None, :]

    raised, mass = mass_of(logits)
    left_a = left_of(numbers, ((3, 1), (3, 0)), expression, labels)
    mass_near = mass + swapped(mass, 1)
    mass_near, left_a = tied((mass_near, left_a))
    mass_far = swapped(mass_near, 2)
    left_b = left_of(numbers, ((2, 1), (2, 0)), expression, labels)
    mass_far, left_b = tied((mass_far, left_b))
    low, dens_part, factor, front, back = first_of(counts, raised, mass_near, mass_far, left_a)

    front = across(front)
    back = on_line(back, 1)
    (kept3,) = blocks_of(left_a, low, (1,), F32)
    (send2,) = blocks_of(left_b, low, (0,), F32)
    left_c = left_of(numbers, ((1, 1), (1, 0), (0, 1), (0, 0)), expression, labels)
    front, back, kept3, send2, left_c = tied((front, back, kept3, send2, left_c))
    send2 = join_of(numbers, send2, back, (1, 2))
    cross2 = across(send2)
    front, send2 = tied((front, send2))
    half3, half3_f, half3_b = half_of(kept3, front)
    more_f = inward(half3_f)
    more_b = inward(half3_b)
    (kept2,) = blocks_of(left_b, low, (1,), F32)
    (send1,) = blocks_of(left_c, low, (0,), BF)
    cross1 = across(send1)
    (kept1,) = blocks_of(left_c, low, (1,), F32)
    (send0,) = blocks_of(left_c, low, (2,), F32)
    send0 = join_of(numbers, send0, back, (0, 3))
    more_f, more_b, cross2, kept2, kept1, send0 = tied((more_f, more_b, cross2, kept2, kept1, send0))
    more, more_f, more_b = step_of(kept2, cross2, more_f, more_b)
    inner = inward(more)
    mid_f = between(more_f)
    mid_b = between(more_b)
    cross0 = across(send0)
    (kept0,) = blocks_of(left_c, low, (3,), F32)
    spot_target, own_target, early = early_of(numbers, target, density, side)
    early = early + swapped(early, 1)
    early = early + swapped(early, 2)
    inner, mid_f, mid_b, cross1, early, kept0 = tied((inner, mid_f, mid_b, cross1, early, kept0))
    close, mid = turn_of(numbers, kept1, cross1, half3, inner, mid_f, mid_b)
    close = on_line(close, 1)
    mid = between(mid)
    close, mid, cross0 = tied((close, mid, cross0))

    total, predicted, kinds, gene, spots = sums_of(kept0, cross0, close, mid, own_target, side, dens_part)
    spots_more = across(spots)
    gene_more = swapped(gene, 1)
    spots_more, gene_more = tied((spots_more, gene_more))
    gene = gene + gene_more
    gene_more = swapped(gene, 2)
    spots = spots + spots_more
    mores = [on_line(spots, step) for step in (1,2,3)]
    own, dens, cross, kinds = grads_of(
        scale, slots, total, own_target, side, density, gene, gene_more, early, spots, spot_target, *mores, kinds
    )

    def update(place, block, acc, mass, **options):
        return update_of(numbers, place, block, expression, low, acc, mass, **options)

    cross0 = across(own)
    close0 = on_line(own, 1)
    mid0 = between(own)
    cross = cross + swapped(cross, 1)
    dens_row, cross = density_of(scale, slots, early, cross, swapped(cross, 2), side, density, dens)
    acc, mass, (mine0, theirs0) = update((0, 0), own, dens_row, mass, start=True)
    near0 = near_of([theirs0], (0,))
    close0, mid0, cross0, mass, near0 = tied((close0, mid0, cross0, mass, near0))

    whole = [((0, 1, 1, 0), 0, GROUP, 0, 0)]
    (block1,) = choose_of(numbers, (close0, mid0), (GROUP,), whole)
    cross1 = across(block1)
    mid1 = between(close0)
    outer1 = outward(mid0)
    far0 = far_of(pair_of(mine0, near0), (0,))
    acc, mass, kept = update((0, 1), cross0, acc, mass)
    acc, mass, (mine1, theirs1) = update((1, 0), block1, acc, mass, kept=kept)
    near1 = near_of([theirs1], (0, 1))
    outer1, mid1, cross1, mass, near1, far0 = tied((outer1, mid1, cross1, mass, near1, far0))

    (block2,) = choose_of(numbers, (outer1, mid1), (GROUP,), whole)
    last = outward(mid1)
    cross2 = across(block2)
    far1 = far_of(pair_of(mine1, near1), (0, 1))
    acc, mass, kept = update((2, 0), block2, acc, mass)
    acc, mass, (mine2, theirs2) = update((1, 1), cross1, acc, mass, kept=kept)
    near2 = near_of([theirs2], (1, 2))
    last, cross2, mass, near2, far1 = tied((last, cross2, mass, near2, far1))

    front, back = choose_of(
        numbers,
        (close0, last, cross0, cross2, kinds),
        (UPPER, LOWER + 2 * KINDS),
        [
            ((1, 0, 0, 1), 0, UPPER, 0, 0),
            ((2, 3, 3, 2), UPPER, LOWER, 1, 0),
            ((4, 4, 4, 4), 0, 2 * KINDS, 1, LOWER),
        ],
    )
    (block3,) = choose_of(numbers, (close0, last), (GROUP,), [((1, 0, 0, 1), 0, GROUP, 0, 0)])
    front = across(front)
    back = on_line(back, 1)
    far2 = far_of(pair_of(mine2, near2, 1), (1, 2))
    mass, mine3, theirs3, columns3 = both_of(numbers, ((2, 1), (3, 0)), (cross2, block3), expression, low, mass)
    near3 = near_of(theirs3, (2, 3))
    pair3 = pair_of(mine3, near3)
    front, back, mass, pair3, far2 = tied((front, back, mass, pair3, far2))

    mass, mine4, theirs4, columns, block = part_of(numbers, (3, 1), front, back, expression, low, mass)
    mass_far = swapped(mass, 2)
    far3 = far_of(pair3, (2, 3))
    near4 = near_of([theirs4], (3,))
    pair4 = pair_of(mine4, near4)
    kinds = merge_of(numbers, 1, kinds, back)
    kinds_more = on_line(kinds, 2)
    acc, fetched = gather_of(columns3, acc, (cross2, block3), logits)
    mass_far, far3, pair4, kinds_more, acc = tied((mass_far, far3, pair4, kinds_more, acc))
    mass = plus(mass, mass_far)
    mass_near = swapped(mass, 1)
    far4 = far_of(pair4, (3,))
    kinds = merge_of(numbers, 2, kinds, kinds_more)
    kinds_more = across(kinds)
    triples = [(mine0, near0, far0), (mine1, near1, far1), (mine2, near2, far2), (mine3, near3, far3)]
    plan = [((turn, 0), turn) for turn in range(4)] + [((turn, 1), turn + 1) for turn in range(3)]
    result = collect_of(numbers, plan, triples)
    mass_near, result = tied((mass_near, result))
    grad_logits = finish_of(columns, block, fetched, factor, acc, mass, mass_near)
    grad_logits, kinds = tied((grad_logits, kinds))
    types, table = kinds_of(numbers, kinds, kinds_more, early, cross)
    result = collect_of(numbers, [((3, 1), 0)], [(mine4, near4, far4)], result)
    return (predicted, grad_logits, result, table, types)


def solution(mesh):
    in_specs = (
        P("cells", "spots"),
        P("cells", None),
        P(None, "spots"),
        P("spots"),
        P("spots"),
        P("cells"),
        P("cells"),
    )
    out_specs = (
        P("cells", "spots"),
        P("cells", "spots"),
        P("cells", "spots"),
        P(),
        P(None, "spots"),
    )
    fits = mesh.shape["cells"] == 8 and mesh.shape["spots"] == 4
    return jax.shard_map(
        ladder if fits else general, mesh=mesh, in_specs=in_specs, out_specs=out_specs, check_vma=False
    )
```
